32 devices in a mesh: dp: 8 (over z, y), seq: 4 (over x, core).
Axes of the slice: x: 2, y: 2, z: 4, core: 2. Of those that a mesh axis runs over, the one named last changes fastest.
Arguments:
- inputs: bfloat16 [8192, 1024], P(('dp', 'seq')), may hold values from -6 to 6
- doc_starts: int32 [8, 4], P('dp'), may hold values from 0 to 1023, as said below
- cotangent: bfloat16 [8192, 1024], P(('dp', 'seq')), may hold values from -6 to 6
- attn_gain: bfloat16 [1024], P(('dp', 'seq')), may hold values from 0.5 to 1.5
- w_query: bfloat16 [1024, 1024], P(('dp', 'seq')), may hold values from -0.1875 to 0.1875
- key_projection_weight: bfloat16 [1024, 512], P(('dp', 'seq')), may hold values from -0.1875 to 0.1875
- value_projection_weight: bfloat16 [1024, 512], P(('dp', 'seq')), may hold values from -0.1875 to 0.1875
- q_gain: bfloat16 [64], replicated, may hold values from 0.099609375 to 1.8984375
- k_gain: bfloat16 [64], replicated, may hold values from 0.099609375 to 1.8984375
- w_out: bfloat16 [1024, 1024], P(('dp', 'seq')), may hold values from -1 to 1
- ffn_gain: bfloat16 [1024], P(('dp', 'seq')), may hold values from 0.5 to 1.5
- w_gate: bfloat16 [1024, 4608], P(('dp', 'seq')), may hold values from -0.1875 to 0.1875
- w_up: bfloat16 [1024, 4608], P(('dp', 'seq')), may hold values from -0.1875 to 0.1875
- w_down: bfloat16 [4608, 1024], P(('dp', 'seq')), may hold values from -0.09375 to 0.09375
Outputs:
- output: bfloat16 [8192, 1024], P(('dp', 'seq'))
- input_grad: float32 [8192, 1024], P(('dp', 'seq'))
- attn_gain_grad: float32 [1024], P(('dp', 'seq'))
- query_grad: float32 [1024, 1024], P(('dp', 'seq'))
- key_grad: float32 [1024, 512], P(('dp', 'seq'))
- value_grad: float32 [1024, 512], P(('dp', 'seq'))
- q_gain_grad: float32 [64], replicated
- k_gain_grad: float32 [64], replicated
- out_grad: float32 [1024, 1024], P(('dp', 'seq'))
- ffn_gain_grad: float32 [1024], P(('dp', 'seq'))
- gate_grad: float32 [1024, 4608], P(('dp', 'seq'))
- up_grad: float32 [1024, 4608], P(('dp', 'seq'))
- down_grad: float32 [4608, 1024], P(('dp', 'seq'))
The draws below stay inside these ranges and needn't reach their ends.
Inputs may be any that keep to these rules, and one draw needn't show every extreme that they name: `doc_starts`: each row holds 4 document starts, strictly increasing, the first 0; the second document starts within the first 256 positions of the row and ends within its last 256 positions.
All inputs are finite; a program needn't handle non-finite values.
Results may differ from the reference program's by a relative error of at most 0.015.
Values may be sent and summed in bfloat16 or wider, within the bound.
A program may use at most 320 MiB of HBM per device.

```python
import jax
import jax.numpy as jnp
from jax import lax

MODEL_WIDTH = 1024
QUERY_HEADS = 16
KEY_VALUE_HEADS = 8
HEAD_SIZE = 64
FF = 4608
TOK_SEQ = 256
LENGTH = 1024
ROWS = 8
TOKENS = 8192


def draw_doc_starts(key, part):
    key = jax.random.fold_in(key, 11)
    first, second, third, fourth = jax.random.split(key, 4)
    long_start = jax.random.randint(first, (ROWS,), 1, TOK_SEQ)
    long_end = jax.random.randint(second, (ROWS,), LENGTH - TOK_SEQ + 1, LENGTH - 1)
    last_start = jax.random.randint(third, (ROWS,), long_end + 1, LENGTH)
    chosen = jax.random.randint(fourth, (), 0, ROWS)
    last_start = jnp.where(jnp.arange(ROWS) == chosen, LENGTH - 1, last_start)
    zero_col = jnp.zeros((ROWS,), jnp.int32)
    return jnp.stack([zero_col, long_start, long_end, last_start], axis=1).astype(jnp.int32)


def shard_levels(own_key, shape, shards, smallest, top_value):
    gain = 1.0
    for dim, blocks in shards:
        heights = jax.random.uniform(jax.random.fold_in(jax.random.fold_in(own_key, 6), dim), (blocks,), jnp.float32, smallest / len(shards), top_value / len(shards))
        gain = gain * jnp.repeat(jnp.exp(heights), shape[dim] // blocks).reshape((-1,) + (1,) * (len(shape) - 1 - dim))
    return gain


def gaussian(stream_key, shape, width, bound, shards=(), held_as=jnp.bfloat16):
    values = jax.random.normal(stream_key, shape, jnp.float32) * width
    if len(shards) > 0:
        values = shard_levels(stream_key, shape, shards, -0.22, 0.18) * values
    return jnp.clip(values, min=-bound, max=bound).astype(held_as)


def setup_inputs(seed: int = 0) -> dict:
    seeds = jax.random.split(jax.random.key(seed), 15)
    return {
        "inputs": gaussian(seeds[0], (TOKENS, MODEL_WIDTH), 1.0, 6.0, ((0, 32),)),
        "doc_starts": draw_doc_starts(jax.random.fold_in(seeds[14], 71), 0),
        "cotangent": gaussian(seeds[2], (TOKENS, MODEL_WIDTH), 1.0, 6.0, ((0, 32),)),
        "attn_gain": jnp.clip(1.0 + 0.1 * jax.random.normal(seeds[3], (MODEL_WIDTH,), jnp.float32), 0.5, 1.5).astype(jnp.bfloat16),
        "w_query": gaussian(seeds[4], (MODEL_WIDTH, QUERY_HEADS * HEAD_SIZE), MODEL_WIDTH ** -0.5, 0.1875, ((0, 32),)),
        "key_projection_weight": gaussian(seeds[5], (MODEL_WIDTH, KEY_VALUE_HEADS * HEAD_SIZE), MODEL_WIDTH ** -0.5, 0.1875, ((0, 32),)),
        "value_projection_weight": gaussian(seeds[6], (MODEL_WIDTH, KEY_VALUE_HEADS * HEAD_SIZE), MODEL_WIDTH ** -0.5, 0.1875, ((0, 32),)),
        "q_gain": jnp.clip(1.0 + 0.18 * jax.random.normal(seeds[7], (HEAD_SIZE,), jnp.float32), 0.099609375, 1.8984375).astype(jnp.bfloat16),
        "k_gain": jnp.clip(1.0 + 0.18 * jax.random.normal(seeds[8], (HEAD_SIZE,), jnp.float32), 0.099609375, 1.8984375).astype(jnp.bfloat16),
        "w_out": gaussian(seeds[9], (QUERY_HEADS * HEAD_SIZE, MODEL_WIDTH), (QUERY_HEADS * HEAD_SIZE // 32) ** -0.5, 1.0, ((0, 32),)),
        "ffn_gain": jnp.clip(1.0 + 0.1 * jax.random.normal(seeds[10], (MODEL_WIDTH,), jnp.float32), 0.5, 1.5).astype(jnp.bfloat16),
        "w_gate": gaussian(seeds[11], (MODEL_WIDTH, FF), MODEL_WIDTH ** -0.5, 0.1875, ((0, 32),)),
        "w_up": gaussian(seeds[12], (MODEL_WIDTH, FF), MODEL_WIDTH ** -0.5, 0.1875, ((0, 32),)),
        "w_down": gaussian(seeds[13], (FF, MODEL_WIDTH), FF ** -0.5, 0.09375, ((0, 32),)),
    }


EPS = 1e-05
THETA = 1000000.0
MASKED = -1e+30
HIGHEST = lax.Precision.HIGHEST

@jax.custom_vjp
def low(v):
    return lax.optimization_barrier(v.astype(jnp.bfloat16)).astype(jnp.float32)

@jax.custom_vjp
def low_back(v):
    return v

def low_keep(v):
    return (low(v), None)

def low_pass(kept, grad):
    return (grad,)

def back_keep(v):
    return (v, None)

def back_low(kept, grad):
    return (low(grad),)
low.defvjp(low_keep, low_pass)
low_back.defvjp(back_keep, back_low)

def matrix_product(left, right):
    return jnp.dot(left, right, precision=HIGHEST, preferred_element_type=jnp.float32)

def rms_norm(values, gain_vec):
    return values * lax.rsqrt(lax.optimization_barrier(jnp.mean(values * values, axis=-1, keepdims=True)) + EPS) * gain_vec

def rotate_half(values):
    half_len = values.shape[-1] // 2
    return jnp.concatenate([-values[..., half_len:], values[..., :half_len]], axis=-1)

def row_layout(row_starts, places):
    inside = places[:, None] >= row_starts[None, :]
    doc_ids = lax.optimization_barrier(jnp.sum(inside.astype(jnp.int32), axis=1)) - 1
    begins = lax.optimization_barrier(jnp.max(jnp.where(inside, row_starts[None, :], 0), axis=1))
    offsets = (places - begins).astype(jnp.float32)
    freq_steps = jnp.arange(HEAD_SIZE // 2, dtype=jnp.float32) * (2.0 / HEAD_SIZE)
    frequency = THETA ** (-freq_steps)
    angles = offsets[:, None] * frequency[None, :]
    angles = jnp.concatenate([angles, angles], axis=-1)
    return (doc_ids, jnp.cos(angles), jnp.sin(angles))

def forward(params, row_in, row_starts):
    attn_scale, w_query, key_projection_weight, value_projection_weight, q_gain, k_gain, w_out, ffn_scale, w_gate, w_up, w_down = params
    total_length = row_in.shape[0]
    places = jnp.arange(total_length, dtype=jnp.int32)
    doc_ids, cosine_table, sine_table = row_layout(row_starts, places)
    cosine_table = cosine_table[:, None, :]
    sine_table = sine_table[:, None, :]
    normalized_input = low(rms_norm(row_in, attn_scale))
    query_rows = low_back(matrix_product(normalized_input, w_query)).reshape(total_length, QUERY_HEADS, HEAD_SIZE)
    key_row_slice = low_back(matrix_product(normalized_input, key_projection_weight)).reshape(total_length, KEY_VALUE_HEADS, HEAD_SIZE)
    query_rows = rms_norm(query_rows, q_gain)
    query_rows = low_back(low(query_rows * cosine_table + rotate_half(query_rows) * sine_table))
    key_row_slice = rms_norm(key_row_slice, k_gain)
    key_row_slice = low_back(low(key_row_slice * cosine_table + rotate_half(key_row_slice) * sine_table))
    value_row_slice = low_back(low(matrix_product(normalized_input, value_projection_weight))).reshape(total_length, KEY_VALUE_HEADS, HEAD_SIZE)
    block_length = min(512, total_length)
    number_of_blocks = total_length // block_length
    grouped_queries = query_rows.reshape(number_of_blocks, block_length, KEY_VALUE_HEADS, QUERY_HEADS // KEY_VALUE_HEADS, HEAD_SIZE)
    score_scale = HEAD_SIZE ** (-0.5)

    def attend(pieces):
        q_block, block_places, block_docs = pieces
        scores = jnp.einsum('qkgd,skd->kgqs', q_block, key_row_slice, precision=HIGHEST) * score_scale
        scores = low_back(scores)
        allowed = (places[None, :] <= block_places[:, None]) & (doc_ids[None, :] == block_docs[:, None])
        scores = jnp.where(allowed[None, None], scores, MASKED)
        row_max = lax.optimization_barrier(jnp.max(scores, axis=-1, keepdims=True))
        weights = jnp.exp(scores - row_max)
        soft_max = low(weights / lax.optimization_barrier(jnp.sum(weights, axis=-1, keepdims=True)))
        mixture = jnp.einsum('kgqs,skd->qkgd', soft_max, value_row_slice, precision=HIGHEST)
        return low_back(low(mixture))
    mixture = lax.map(jax.checkpoint(attend), (grouped_queries, places.reshape(number_of_blocks, block_length), doc_ids.reshape(number_of_blocks, block_length)))
    attended = mixture.reshape(total_length, QUERY_HEADS * HEAD_SIZE)
    middle = row_in + low_back(matrix_product(attended, w_out))
    normed_mid = low(rms_norm(middle, ffn_scale))
    gate_lin = low_back(matrix_product(normed_mid, w_gate))
    upward = low_back(matrix_product(normed_mid, w_up))
    active = low(jax.nn.silu(gate_lin) * upward)
    return middle + matrix_product(active, w_down)

def reference(inputs, doc_starts, cotangent, attn_gain, w_query, key_projection_weight, value_projection_weight, q_gain, k_gain, w_out, ffn_gain, w_gate, w_up, w_down):
    params = tuple((weight.astype(jnp.float32) for weight in (attn_gain, w_query, key_projection_weight, value_projection_weight, q_gain, k_gain, w_out, ffn_gain, w_gate, w_up, w_down)))
    rows_in = inputs.astype(jnp.float32).reshape(ROWS, LENGTH, MODEL_WIDTH)
    rows_cot = cotangent.astype(jnp.float32).reshape(ROWS, LENGTH, MODEL_WIDTH)

    def one_row(totals, pieces):
        row_in, row_starts, row_cot = pieces
        result, pullback = jax.vjp(lambda weights, values: forward(weights, values, row_starts), params, row_in)
        weight_grads, input_part = pullback(row_cot)
        totals = jax.tree.map(jnp.add, totals, weight_grads)
        return (totals, (result, input_part))
    zero_grads = jax.tree.map(jnp.zeros_like, params)
    totals, (results, input_parts) = lax.scan(one_row, zero_grads, (rows_in, doc_starts, rows_cot))
    g_attn, g_query, g_key, g_value, g_qgain, g_kgain, g_out, g_ffn, g_gate, g_up, g_down = totals
    return (results.reshape(TOKENS, MODEL_WIDTH).astype(jnp.bfloat16), input_parts.reshape(TOKENS, MODEL_WIDTH), g_attn, g_query, g_key, g_value, g_qgain, g_kgain, g_out, g_ffn, g_gate, g_up, g_down)
```

```python
import jax
import jax.numpy as jnp
import numpy as np
from jax import lax
from jax.experimental import pallas as pl
from jax.experimental.pallas import tpu as pltpu
from jax.sharding import PartitionSpec as P

QUERY_HEADS = 16
KEY_VALUE_HEADS = 8
HEAD_SIZE = 64
FF = 4608


EPS = 1e-05
THETA = 1000000.0
MASKED = -1e30
CONTRACT_ROWS = (((0,), (0,)), ((), ()))
CONTRACT_COLS = (((1,), (1,)), ((), ()))


def rms_norm(values, gain_vec):
    return values * lax.rsqrt(jnp.mean(values * values, axis=-1, keepdims=True) + EPS) * gain_vec


def rotate_half(values):
    half_len = values.shape[-1] // 2
    return jnp.concatenate([-values[..., half_len:], values[..., :half_len]], axis=-1)


def unrotate_half(values):
    half_len = values.shape[-1] // 2
    return jnp.concatenate([values[..., half_len:], -values[..., :half_len]], axis=-1)


def row_layout(row_starts, places):
    inside = places[:, None] >= row_starts[None, :]
    doc_ids = jnp.sum(inside.astype(jnp.int32), axis=1) - 1
    begins = jnp.max(jnp.where(inside, row_starts[None, :], 0), axis=1)
    offsets = (places - begins).astype(jnp.float32)
    freq_steps = jnp.arange(HEAD_SIZE // 2, dtype=jnp.float32) * (2.0 / HEAD_SIZE)
    frequency = THETA ** (-freq_steps)
    angles = offsets[:, None] * frequency[None, :]
    angles = jnp.concatenate([angles, angles], axis=-1)
    return (doc_ids, jnp.cos(angles), jnp.sin(angles))


def norm_back(upstream, values, gain_vec):
    inverse = lax.rsqrt(jnp.mean(values * values, axis=-1, keepdims=True) + EPS)
    unit_vec = values * inverse
    gain_part = jnp.sum(upstream * unit_vec, axis=tuple(range(values.ndim - 1)))
    scaled = upstream * gain_vec
    return (
        inverse * (scaled - unit_vec * jnp.mean(scaled * unit_vec, axis=-1, keepdims=True)),
        gain_part,
    )


def head_forward_pass(linear, gain_vec, cosine_table, sine_table, heads):
    local_rows = linear.shape[0]
    shaped = rms_norm(linear.reshape(local_rows, heads, HEAD_SIZE), gain_vec)
    turned = shaped * cosine_table + rotate_half(shaped) * sine_table
    return turned.astype(jnp.bfloat16).reshape(local_rows, heads * HEAD_SIZE)


def head_backward_pass(grad_in, linear, gain_vec, cosine_table, sine_table, heads):
    local_rows = linear.shape[0]
    shaped = linear.reshape(local_rows, heads, HEAD_SIZE)
    upstream = grad_in.astype(jnp.float32).reshape(local_rows, heads, HEAD_SIZE)
    d_normed = upstream * cosine_table + unrotate_half(upstream * sine_table)
    d_linear, gain_part = norm_back(d_normed, shaped, gain_vec)
    return (d_linear.reshape(local_rows, heads * HEAD_SIZE).astype(jnp.bfloat16), gain_part)


def block_scores(q_block, keys_all, block_places, block_docs, places, doc_ids):
    score_scale = HEAD_SIZE ** (-0.5)
    scores = (
        jnp.einsum("qkgd,skd->kgqs", q_block, keys_all, preferred_element_type=jnp.float32)
        * score_scale
    )
    allowed = (places[None, :] <= block_places[:, None]) & (doc_ids[None, :] == block_docs[:, None])
    return jnp.where(allowed[None, None], scores, MASKED)


def attend_forward(query_rows, keys_in, values_in, places, doc_ids):
    total_length = query_rows.shape[0]
    kv_heads = keys_in.shape[1] // HEAD_SIZE
    query_group = QUERY_HEADS // KEY_VALUE_HEADS
    block_length = min(512, total_length)
    number_of_blocks = total_length // block_length
    keys_all = keys_in.reshape(total_length, kv_heads, HEAD_SIZE)
    values_all = values_in.reshape(total_length, kv_heads, HEAD_SIZE)
    grouped_queries = query_rows.reshape(
        number_of_blocks, block_length, kv_heads, query_group, HEAD_SIZE
    )

    def one_block(pieces):
        q_block, block_places, block_docs = pieces
        scores = block_scores(q_block, keys_all, block_places, block_docs, places, doc_ids)
        row_max = jnp.max(scores, axis=-1, keepdims=True)
        weights = jnp.exp(scores - row_max)
        sum_total = jnp.sum(weights, axis=-1, keepdims=True)
        soft_max = (weights / sum_total).astype(jnp.bfloat16)
        mixture = jnp.einsum(
            "kgqs,skd->qkgd", soft_max, values_all, preferred_element_type=jnp.float32
        )
        return (mixture.astype(jnp.bfloat16), row_max[..., 0] + jnp.log(sum_total[..., 0]))

    mixture, log_total = lax.map(
        one_block,
        (
            grouped_queries,
            places.reshape(number_of_blocks, block_length),
            doc_ids.reshape(number_of_blocks, block_length),
        ),
    )
    return (mixture.reshape(total_length, kv_heads * query_group * HEAD_SIZE), log_total)


def attend_back(query_rows, keys_in, values_in, grad_out, log_total, places, doc_ids):
    total_length = query_rows.shape[0]
    kv_heads = keys_in.shape[1] // HEAD_SIZE
    query_group = QUERY_HEADS // KEY_VALUE_HEADS
    block_length = min(512, total_length)
    number_of_blocks = total_length // block_length
    score_scale = HEAD_SIZE ** (-0.5)
    keys_all = keys_in.reshape(total_length, kv_heads, HEAD_SIZE)
    values_all = values_in.reshape(total_length, kv_heads, HEAD_SIZE)
    grouped_queries = query_rows.reshape(
        number_of_blocks, block_length, kv_heads, query_group, HEAD_SIZE
    )
    grads_all = grad_out.reshape(number_of_blocks, block_length, kv_heads, query_group, HEAD_SIZE)

    def one_block(carried, pieces):
        key_total, value_total = carried
        q_block, g_block, block_log, block_places, block_docs = pieces
        scores = block_scores(q_block, keys_all, block_places, block_docs, places, doc_ids)
        chances = jnp.exp(scores - block_log[..., None])
        d_chances = jnp.einsum(
            "qkgd,skd->kgqs", g_block, values_all, preferred_element_type=jnp.float32
        )
        row_dots = jnp.sum(d_chances * chances, axis=-1, keepdims=True)
        d_scores = (chances * (d_chances - row_dots)).astype(jnp.bfloat16)
        d_query = (
            jnp.einsum("kgqs,skd->qkgd", d_scores, keys_all, preferred_element_type=jnp.float32)
            * score_scale
        )
        key_total = (
            key_total
            + jnp.einsum("kgqs,qkgd->skd", d_scores, q_block, preferred_element_type=jnp.float32)
            * score_scale
        )
        value_total = value_total + jnp.einsum(
            "kgqs,qkgd->skd",
            chances.astype(jnp.bfloat16),
            g_block,
            preferred_element_type=jnp.float32,
        )
        return ((key_total, value_total), d_query)

    zero_kv = jnp.zeros((total_length, kv_heads, HEAD_SIZE), jnp.float32)
    inputs_scan = (
        grouped_queries,
        grads_all,
        log_total,
        places.reshape(number_of_blocks, block_length),
        doc_ids.reshape(number_of_blocks, block_length),
    )
    (key_total, value_total), d_query = lax.scan(one_block, (zero_kv, zero_kv), inputs_scan)
    return (
        d_query.reshape(total_length, kv_heads * query_group * HEAD_SIZE).astype(jnp.bfloat16),
        key_total.reshape(total_length, kv_heads * HEAD_SIZE).astype(jnp.bfloat16),
        value_total.reshape(total_length, kv_heads * HEAD_SIZE).astype(jnp.bfloat16),
    )


def on_device(
    inputs,
    doc_starts,
    cotangent,
    attn_gain,
    w_query,
    key_projection_weight,
    value_projection_weight,
    q_gain,
    k_gain,
    w_out,
    ffn_gain,
    w_gate,
    w_up,
    w_down,
):
    local_rows = inputs.shape[0]
    seq_parts = lax.axis_size("seq")
    total_length = local_rows * seq_parts
    row_starts = doc_starts[0]
    local_places = lax.axis_index("seq") * local_rows + jnp.arange(local_rows, dtype=jnp.int32)
    unused_docs, cosine_table, sine_table = row_layout(row_starts, local_places)
    cosine_table = cosine_table[:, None, :]
    sine_table = sine_table[:, None, :]
    all_places = jnp.arange(total_length, dtype=jnp.int32)
    all_docs = jnp.sum((all_places[:, None] >= row_starts[None, :]).astype(jnp.int32), axis=1) - 1
    q_scale = q_gain.astype(jnp.float32)
    key_norm_scale = k_gain.astype(jnp.float32)
    attn_scale, query_full, key_full, value_full, out_full = (
        lax.all_gather(attn_gain, ("dp", "seq"), axis=0, tiled=True),
        lax.all_gather(w_query, ("dp", "seq"), axis=0, tiled=True),
        lax.all_gather(key_projection_weight, ("dp", "seq"), axis=0, tiled=True),
        lax.all_gather(value_projection_weight, ("dp", "seq"), axis=0, tiled=True),
        lax.all_gather(w_out, ("dp", "seq"), axis=0, tiled=True),
    )
    source = inputs.astype(jnp.float32)
    normalized_input = rms_norm(source, attn_scale.astype(jnp.float32)).astype(jnp.bfloat16)
    q_linear = jnp.dot(normalized_input, query_full, preferred_element_type=jnp.float32)
    key_linear_output = jnp.dot(normalized_input, key_full, preferred_element_type=jnp.float32)
    q_sent = head_forward_pass(q_linear, q_scale, cosine_table, sine_table, QUERY_HEADS)
    key_sent_rows = head_forward_pass(
        key_linear_output, key_norm_scale, cosine_table, sine_table, KEY_VALUE_HEADS
    )
    v_sent = jnp.dot(normalized_input, value_full, preferred_element_type=jnp.float32).astype(
        jnp.bfloat16
    )
    q_heads, k_heads, v_heads = (
        lax.all_to_all(q_sent, "seq", split_axis=1, concat_axis=0, tiled=True),
        lax.all_to_all(key_sent_rows, "seq", split_axis=1, concat_axis=0, tiled=True),
        lax.all_to_all(v_sent, "seq", split_axis=1, concat_axis=0, tiled=True),
    )
    mixture, log_total = attend_forward(q_heads, k_heads, v_heads, all_places, all_docs)
    attended = lax.all_to_all(mixture, "seq", split_axis=0, concat_axis=1, tiled=True)
    middle = source + jnp.dot(attended, out_full, preferred_element_type=jnp.float32)
    ffn_scale, gate_full, up_full, down_full = (
        lax.all_gather(ffn_gain, ("dp", "seq"), axis=0, tiled=True),
        lax.all_gather(w_gate, ("dp", "seq"), axis=0, tiled=True),
        lax.all_gather(w_up, ("dp", "seq"), axis=0, tiled=True),
        lax.all_gather(w_down, ("dp", "seq"), axis=0, tiled=True),
    )
    normed_mid = rms_norm(middle, ffn_scale.astype(jnp.float32)).astype(jnp.bfloat16)
    gate_lin = jnp.dot(normed_mid, gate_full, preferred_element_type=jnp.float32)
    upward = jnp.dot(normed_mid, up_full, preferred_element_type=jnp.float32)
    sigmoid_gate = jax.nn.sigmoid(gate_lin)
    swish = gate_lin * sigmoid_gate
    active = (swish * upward).astype(jnp.bfloat16)
    output = (middle + jnp.dot(active, down_full, preferred_element_type=jnp.float32)).astype(
        jnp.bfloat16
    )
    ffn_scale, gate_full, up_full, down_full = (
        lax.all_gather(ffn_gain, ("dp", "seq"), axis=0, tiled=True),
        lax.all_gather(w_gate, ("dp", "seq"), axis=0, tiled=True),
        lax.all_gather(w_up, ("dp", "seq"), axis=0, tiled=True),
        lax.all_gather(w_down, ("dp", "seq"), axis=0, tiled=True),
    )
    d_active = lax.dot_general(
        cotangent, down_full, CONTRACT_COLS, preferred_element_type=jnp.float32
    )
    d_gate = (d_active * upward * (sigmoid_gate * (1.0 + gate_lin * (1.0 - sigmoid_gate)))).astype(
        jnp.bfloat16
    )
    d_up = (d_active * swish).astype(jnp.bfloat16)
    d_normed_mid = lax.dot_general(
        d_gate, gate_full, CONTRACT_COLS, preferred_element_type=jnp.float32
    )
    d_normed_mid = d_normed_mid + lax.dot_general(
        d_up, up_full, CONTRACT_COLS, preferred_element_type=jnp.float32
    )
    d_middle_norm, ffn_gain_part = norm_back(d_normed_mid, middle, ffn_scale.astype(jnp.float32))
    d_middle = cotangent.astype(jnp.float32) + d_middle_norm
    d_branch = d_middle.astype(jnp.bfloat16)
    attn_scale, query_full, key_full, value_full, out_full = (
        lax.all_gather(attn_gain, ("dp", "seq"), axis=0, tiled=True),
        lax.all_gather(w_query, ("dp", "seq"), axis=0, tiled=True),
        lax.all_gather(key_projection_weight, ("dp", "seq"), axis=0, tiled=True),
        lax.all_gather(value_projection_weight, ("dp", "seq"), axis=0, tiled=True),
        lax.all_gather(w_out, ("dp", "seq"), axis=0, tiled=True),
    )
    d_attended = lax.dot_general(
        d_branch, out_full, CONTRACT_COLS, preferred_element_type=jnp.float32
    ).astype(jnp.bfloat16)
    d_mixture = lax.all_to_all(d_attended, "seq", split_axis=1, concat_axis=0, tiled=True)
    d_q_heads, d_k_heads, d_v_heads = attend_back(
        q_heads, k_heads, v_heads, d_mixture, log_total, all_places, all_docs
    )
    d_q_sent, key_sent_gradient, d_v_sent = (
        lax.all_to_all(d_q_heads, "seq", split_axis=0, concat_axis=1, tiled=True),
        lax.all_to_all(d_k_heads, "seq", split_axis=0, concat_axis=1, tiled=True),
        lax.all_to_all(d_v_heads, "seq", split_axis=0, concat_axis=1, tiled=True),
    )
    d_q_linear, q_gain_part = head_backward_pass(
        d_q_sent, q_linear, q_scale, cosine_table, sine_table, QUERY_HEADS
    )
    key_linear_gradient, key_gain_piece = head_backward_pass(
        key_sent_gradient,
        key_linear_output,
        key_norm_scale,
        cosine_table,
        sine_table,
        KEY_VALUE_HEADS,
    )
    d_normed = lax.dot_general(
        d_q_linear, query_full, CONTRACT_COLS, preferred_element_type=jnp.float32
    )
    d_normed = d_normed + lax.dot_general(
        key_linear_gradient, key_full, CONTRACT_COLS, preferred_element_type=jnp.float32
    )
    d_normed = d_normed + lax.dot_general(
        d_v_sent, value_full, CONTRACT_COLS, preferred_element_type=jnp.float32
    )
    d_source_norm, attn_gain_part = norm_back(d_normed, source, attn_scale.astype(jnp.float32))
    input_grad = d_middle + d_source_norm
    attn_columns = jnp.concatenate([d_q_linear, key_linear_gradient, d_v_sent], axis=1)
    ffn_columns = jnp.concatenate([d_gate, d_up], axis=1)
    left = normalized_input
    first_part = lax.dot_general(
        left, attn_columns, CONTRACT_ROWS, preferred_element_type=jnp.float32
    )
    second_part = lax.dot_general(
        normed_mid, ffn_columns, CONTRACT_ROWS, preferred_element_type=jnp.float32
    )
    width_sums = lax.psum_scatter(
        jnp.concatenate([first_part, second_part], axis=1),
        ("dp", "seq"),
        scatter_dimension=0,
        tiled=True,
    )
    left = attended
    out_grad = lax.psum_scatter(
        lax.dot_general(left, d_branch, CONTRACT_ROWS, preferred_element_type=jnp.float32),
        ("dp", "seq"),
        scatter_dimension=0,
        tiled=True,
    )
    left = active
    down_grad = lax.psum_scatter(
        lax.dot_general(left, cotangent, CONTRACT_ROWS, preferred_element_type=jnp.float32),
        ("dp", "seq"),
        scatter_dimension=0,
        tiled=True,
    )
    attn_gain_grad, ffn_gain_grad = (
        lax.psum_scatter(attn_gain_part, ("dp", "seq"), scatter_dimension=0, tiled=True),
        lax.psum_scatter(ffn_gain_part, ("dp", "seq"), scatter_dimension=0, tiled=True),
    )
    q_gain_grad, k_gain_grad = lax.psum((q_gain_part, key_gain_piece), ("dp", "seq"))
    q_cols = QUERY_HEADS * HEAD_SIZE
    kv_cols = KEY_VALUE_HEADS * HEAD_SIZE
    query_grad = width_sums[:, :q_cols]
    key_grad = width_sums[:, q_cols : q_cols + kv_cols]
    value_grad = width_sums[:, q_cols + kv_cols : q_cols + 2 * kv_cols]
    gate_grad = width_sums[:, q_cols + 2 * kv_cols : q_cols + 2 * kv_cols + FF]
    up_grad = width_sums[:, q_cols + 2 * kv_cols + FF :]
    return (
        output,
        input_grad,
        attn_gain_grad,
        query_grad,
        key_grad,
        value_grad,
        q_gain_grad,
        k_gain_grad,
        out_grad,
        ffn_gain_grad,
        gate_grad,
        up_grad,
        down_grad,
    )


BF = jnp.bfloat16
F32 = jnp.float32
MESH = pl.DeviceIdType.MESH
SEQ = 4
PLANES = 4
TOK = 256
WIDTH = 1024
ROW = 1024
OWN_Q = 256
OWN_K = 128
QKV = 512
FF_OWN = 1152
FF_SHARD = 144
HIDDEN_TWO = 2304
DOWN_A = 64
DOWN_B = 80


def flip(value, bit):
    return value + bit - 2 * bit * lax.rem(lax.div(value, bit), 2)


def dot(left, right):
    return lax.dot_general(left, right, (((1,), (0,)), ((), ())), preferred_element_type=F32)


def dot_nt(left, right):
    return lax.dot_general(left, right, (((1,), (1,)), ((), ())), preferred_element_type=F32)


def dot_tn(left, right):
    return lax.dot_general(left, right, (((0,), (0,)), ((), ())), preferred_element_type=F32)


class Links:
    def __init__(self, send_sems, recv_sems):
        self.send_sems, self.recv_sems = send_sems, recv_sems
        self.used = 0
        self.open = []
        self.dp = lax.axis_index("dp")
        self.s = lax.axis_index("seq")
        self.s1 = flip(self.s, 1)
        self.s2 = flip(self.s, 2)
        self.s3 = flip(self.s1, 2)
        self.others = (self.s1, self.s2, self.s3)
        self.y = lax.rem(self.dp, 2)
        self.z = lax.div(self.dp, 2)
        self.y_peer = flip(self.dp, 1)
        z1 = flip(self.z, 1)
        self.planes = (z1, flip(self.z, 2), flip(z1, 2))
        self.z_peers = tuple(2 * z + self.y for z in self.planes)

    def greet(self, semaphore, partners):
        for place in partners:
            pl.semaphore_signal(semaphore, inc=1, device_id=place, device_id_type=MESH)

    def column(self):
        return [(p, self.s) for p in (self.y_peer,) + self.z_peers]

    def everyone(self):
        return [(self.dp, s) for s in self.others] + self.column()

    def plan(self, src, dst, dp=None, s=None):
        n = self.used
        self.used += 1
        copy = pltpu.make_async_remote_copy(
            src_ref=src,
            dst_ref=dst,
            send_sem=self.send_sems.at[n],
            recv_sem=self.recv_sems.at[n],
            device_id=(self.dp if dp is None else dp, self.s if s is None else s),
            device_id_type=MESH,
        )
        return copy

    def push(self, src, dst, dp=None, s=None, when=None):
        copy = self.plan(src, dst, dp, s)
        if when is None:
            copy.start()
        else:
            pl.when(when)(copy.start)
        self.open.append((copy, when))
        return copy

    def settle(self, copies):
        for copy in copies:
            copy.wait_send()
        self.open = [item for item in self.open if all(item[0] is not copy for copy in copies)]

    def drain(self):
        for copy, when in self.open:
            if when is None:
                copy.wait_send()
            else:
                pl.when(when)(copy.wait_send)
        self.open = []


class Line:
    def __init__(self, links, view):
        self.links, self.view = links, view
        self.hops = []

    def pass_on(self, step):
        l = self.links
        below, above = l.z - step, l.z + step
        low = self.view(jnp.maximum(below, 0))
        high = self.view(jnp.minimum(above, PLANES - 1))
        up = l.push(
            low, low, dp=jnp.minimum(l.dp + 2, 2 * PLANES - 1), when=(below >= 0) & (l.z < PLANES - 1)
        )
        down = l.push(high, high, dp=jnp.maximum(l.dp - 2, 0), when=(above <= PLANES - 1) & (l.z > 0))
        self.hops.append((up, down))

    def start(self):
        self.pass_on(0)

    def step(self, k):
        l = self.links
        below, above = l.z - 1 - k, l.z + 1 + k
        from_below, from_above = below >= 0, above <= PLANES - 1
        pl.when(from_below)(self.hops[k][0].wait_recv)
        pl.when(from_above)(self.hops[k][1].wait_recv)
        if k < PLANES - 2:
            self.pass_on(k + 1)
        return [
            (from_below, self.view(jnp.maximum(below, 0))),
            (from_above, self.view(jnp.minimum(above, PLANES - 1))),
        ]


class Gather:
    def __init__(self, links, view):
        self.links = links
        self.line = Line(links, lambda z: view(2 * z + links.y))
        self.own = view(links.dp)
        self.over_y = []

    def start_y(self):
        self.over_y.append((None, self.links.push(self.own, self.own, dp=self.links.y_peer)))

    def start_z(self):
        self.line.start()

    def step(self, k):
        for when, block in self.line.step(k):
            copy = self.links.push(block, block, dp=self.links.y_peer, when=when)
            self.over_y.append((when, copy))

    def finish(self):
        for when, copy in self.over_y:
            if when is None:
                copy.wait_recv()
            else:
                pl.when(when)(copy.wait_recv)


class PairGather:
    def __init__(self, links, view):
        self.links = links
        self.near = Line(links, lambda z: view(2 * z + links.y))
        self.far = Line(links, lambda z: view(2 * z + 1 - links.y))
        self.own = view(links.dp)

    def start_y(self):
        self.over_y = self.links.push(self.own, self.own, dp=self.links.y_peer)

    def start_z(self):
        self.near.start()

    def join(self):
        self.over_y.wait_recv()
        self.far.start()

    def step(self, k):
        self.near.step(k)
        self.far.step(k)


class Chain:
    def __init__(self, links, view, slots):
        self.links, self.view, self.slots = links, view, slots
        self.up, self.down = {}, {}

    def start(self):
        l = self.links
        last = PLANES - 1
        for d in range(PLANES):
            if d > 0:
                self.up[d] = l.plan(self.view(d), self.slots(d), dp=jnp.minimum(l.dp + 2, 2 * last + 1))
            if d < last:
                place = jnp.where(l.z == d + 1, PLANES, d)
                self.down[d] = l.plan(self.view(d), self.slots(place), dp=jnp.maximum(l.dp - 2, 0))

    def add(self, d, copy):
        copy.wait_recv()
        block = self.view(d)
        block[...] = (block[...].astype(F32) + self.slots(d)[...].astype(F32)).astype(BF)

    def step(self, j):
        last = PLANES - 1

        @pl.when(self.links.z == j)
        def _():
            for d in range(last, j, -1):
                if j > 0:
                    self.add(d, self.up[d])
                self.up[d].start()

        @pl.when(self.links.z == last - j)
        def _():
            for d in range(last - j):
                if j > 0:
                    self.add(d, self.down[d])
                self.down[d].start()

        for d in range(PLANES):
            if d > j:
                self.links.open.append((self.up[d], self.links.z == j))
            if d < last - j:
                self.links.open.append((self.down[d], self.links.z == last - j))

    def total(self):
        l = self.links
        for d in range(PLANES):
            if d > 0:
                pl.when(l.z == d)(self.up[d].wait_recv)
            if d < PLANES - 1:
                pl.when(l.z == d)(self.down[d].wait_recv)
        own = self.view(l.z)[...].astype(F32)
        below = jnp.where(l.z > 0, self.slots(l.z)[...].astype(F32), 0.0)
        above = jnp.where(l.z < PLANES - 1, self.slots(PLANES)[...].astype(F32), 0.0)
        return own + (below + above)


class Scatter:
    def __init__(self, links, view, y_slots, z_slots):
        self.links, self.view, self.y_slots = links, view, y_slots
        self.chain = Chain(links, lambda z: view(2 * z + links.y), z_slots)

    def start(self):
        l = self.links
        self.order = [jnp.where(l.z < PLANES // 2, PLANES - 1 - k, k) for k in range(PLANES)]
        self.over_y = [
            l.push(self.view(2 * d + 1 - l.y), self.y_slots(k), dp=l.y_peer) for k, d in enumerate(self.order)
        ]
        self.chain.start()

    def join(self):
        for k, copy in enumerate(self.over_y):
            copy.wait_recv()
            block = self.view(2 * self.order[k] + self.links.y)
            block[...] = (block[...].astype(F32) + self.y_slots(k)[...].astype(F32)).astype(BF)

    def step(self, j):
        self.chain.step(j)

    def total(self):
        return self.chain.total()


class PairScatter:
    def __init__(self, links, view, y_slot, near_slots, far_slots):
        self.links, self.view, self.y_slot = links, view, y_slot
        self.near = Chain(links, lambda z: view(2 * z + links.y), near_slots)
        self.far = Chain(links, lambda z: view(2 * z + 1 - links.y), far_slots)

    def start(self):
        self.far.start()
        self.near.start()

    def step(self, j):
        self.far.step(j)
        self.near.step(j)

    def cross(self):
        l = self.links
        block = self.view(2 * l.z + 1 - l.y)
        block[...] = self.far.total().astype(BF)
        self.over_y = l.push(block, self.y_slot, dp=l.y_peer)

    def total(self):
        own = self.near.total()
        self.over_y.wait_recv()
        return own + self.y_slot[...].astype(F32)


class RowSum:
    def __init__(self, links, slots):
        self.links, self.slots = links, slots

    def hand_over(self, src):
        self.first = self.links.push(src, self.slots.at[0], s=self.links.s1)

    def cross(self, src):
        self.first.wait_recv()
        src[...] = (src[...].astype(F32) + self.slots[0].astype(F32).reshape(src.shape)).astype(BF)
        self.second = self.links.push(src, self.slots.at[1], s=self.links.s2)

    def near(self, src):
        self.third = self.links.push(src, self.slots.at[2], s=self.links.s1)

    def total(self, own):
        self.third.wait_recv()
        self.second.wait_recv()
        return own + self.slots[1].astype(F32).reshape(own.shape) + self.slots[2].astype(F32).reshape(own.shape)


def lane_masks(rows):
    lane = lax.broadcasted_iota(jnp.int32, (rows, 128), 1)
    return lane < 64, lax.rem(lane, 64) < 32


def turned(values, low):
    return jnp.where(low, -pltpu.roll(values, 96, 1), pltpu.roll(values, 32, 1))


def unturned(values, low):
    return jnp.where(low, pltpu.roll(values, 96, 1), -pltpu.roll(values, 32, 1))


def per_head_mean(values, first):
    left = jnp.sum(jnp.where(first, values, 0.0), axis=-1, keepdims=True)
    right = jnp.sum(jnp.where(first, 0.0, values), axis=-1, keepdims=True)
    return jnp.where(first, left, right) * (1.0 / HEAD_SIZE)


def norm_rope(values, gain, cosine, sine, first, low):
    normed = values * lax.rsqrt(per_head_mean(values * values, first) + EPS) * gain
    return normed * cosine + turned(normed, low) * sine


def norm_rope_back(upstream, values, gain, cosine, sine, first, low):
    d_normed = upstream * cosine + unturned(upstream * sine, low)
    inverse = lax.rsqrt(per_head_mean(values * values, first) + EPS)
    unit = values * inverse
    scaled = d_normed * gain
    d_values = inverse * (scaled - unit * per_head_mean(scaled * unit, first))
    return d_values, jnp.sum(d_normed * unit, axis=0, keepdims=True)


def allowed_block(r, block, keys):
    query = lax.broadcasted_iota(jnp.int32, (TOK, keys), 0) + block * TOK
    key = lax.broadcasted_iota(jnp.int32, (TOK, keys), 1)
    place = lax.broadcasted_iota(jnp.int32, (TOK, 1), 0) + block * TOK
    begin = jnp.zeros((TOK, 1), jnp.int32)
    for k in range(4):
        start = r.doc_starts[0, k]
        begin = jnp.maximum(begin, jnp.where(place >= start, start, 0))
    return (key <= query) & (key >= begin)


SCORE_SCALE = HEAD_SIZE ** (-0.5)


def attention_block(r, pair, block):
    keys = (block + 1) * TOK
    rows = pl.ds(block * TOK, TOK)
    queries = r.q_heads[pair, :, rows, :].reshape(2 * TOK, HEAD_SIZE)
    scores = dot_nt(queries, r.k_heads[pair, :keys, :]).reshape(2, TOK, keys) * SCORE_SCALE
    scores = jnp.where(allowed_block(r, block, keys)[None], scores, MASKED)
    top = jnp.max(scores, axis=-1, keepdims=True)
    weights = jnp.exp(scores - top)
    total = jnp.sum(weights, axis=-1, keepdims=True)
    mixed = dot(weights.astype(BF).reshape(2 * TOK, keys), r.v_heads[pair, :keys, :])
    mixed = mixed.reshape(2, TOK, HEAD_SIZE) / total
    log_total = top + jnp.log(total)
    r.log_total[rows, 2 * pair : 2 * pair + 1] = log_total[0]
    r.log_total[rows, 2 * pair + 1 : 2 * pair + 2] = log_total[1]
    r.att_own[block, :, pair * 128 : (pair + 1) * 128] = jnp.concatenate(
        [mixed[0], mixed[1]], axis=-1
    ).astype(BF)


def attention_block_back(r, pair, block):
    keys = (block + 1) * TOK
    rows = pl.ds(block * TOK, TOK)
    queries = r.q_heads[pair, :, rows, :].reshape(2 * TOK, HEAD_SIZE)
    grads = r.d_att_rows[block, :, pair * 128 : (pair + 1) * 128]
    grads = jnp.concatenate([grads[:, :HEAD_SIZE], grads[:, HEAD_SIZE:]], axis=0)
    keys_in, values_in = r.k_heads[pair, :keys, :], r.v_heads[pair, :keys, :]
    scores = dot_nt(queries, keys_in).reshape(2, TOK, keys) * SCORE_SCALE
    log_total = jnp.stack([r.log_total[rows, 2 * pair + g : 2 * pair + g + 1] for g in range(2)])
    chances = jnp.exp(scores - log_total)
    chances = jnp.where(allowed_block(r, block, keys)[None], chances, 0.0)
    d_chances = dot_nt(grads, values_in).reshape(2, TOK, keys)
    row_dots = jnp.sum(d_chances * chances, axis=-1, keepdims=True)
    d_scores = (chances * (d_chances - row_dots)).astype(BF).reshape(2 * TOK, keys)
    d_query = (dot(d_scores, keys_in) * SCORE_SCALE).astype(BF)
    r.d_query[rows, pair * 128 : (pair + 1) * 128] = jnp.concatenate(
        [d_query[:TOK], d_query[TOK:]], axis=-1
    )
    d_key = dot_tn(d_scores, queries) * SCORE_SCALE
    d_value = dot_tn(chances.astype(BF).reshape(2 * TOK, keys), grads)
    if block == ROW // TOK - 1:
        r.d_kv[pair, :, :HEAD_SIZE] = d_key
        r.d_kv[pair, :, HEAD_SIZE:] = d_value
    else:
        r.d_kv[pair, :keys, :HEAD_SIZE] += d_key
        r.d_kv[pair, :keys, HEAD_SIZE:] += d_value


def norm_back_unit(upstream, values):
    inverse = lax.rsqrt(jnp.mean(values * values, axis=-1, keepdims=True) + EPS)
    unit = values * inverse
    d_values = inverse * (
        upstream - unit * jnp.mean(upstream * unit, axis=-1, keepdims=True)
    )
    return d_values, jnp.sum(upstream * unit, axis=0, keepdims=True)


def unit_norm(values):
    return values * lax.rsqrt(jnp.mean(values * values, axis=-1, keepdims=True) + EPS)


def own_parts(r):
    scale = r.attn_gain[...]
    for o in range(SEQ):
        for ref, first, size in ((r.w_query, 0, OWN_Q), (r.w_key, OWN_Q, OWN_K), (r.w_value, OWN_Q + OWN_K, OWN_K)):
            part = ref[:, o * size : (o + 1) * size].astype(F32) * scale
            r.w_qkv[o, :, first : first + size] = part.astype(BF)


def own_units(r):
    scale = r.ffn_gain[...]
    for ref, first in ((r.w_gate, 0), (r.w_up, FF_OWN)):
        scaled = ref[...].astype(F32) * scale
        for o in range(SEQ):
            parts = [scaled[:, (4 * j + o) * FF_SHARD : (4 * j + o + 1) * FF_SHARD] for j in range(8)]
            r.w_gu[o, :, first : first + FF_OWN] = jnp.concatenate(parts, axis=1).astype(BF)


def rotation_tables(r, half):
    size = ROW // 2
    rows = pl.ds(half * size, size)
    place = lax.broadcasted_iota(jnp.int32, (size, 1), 0) + half * size
    begin = jnp.zeros((size, 1), jnp.int32)
    for k in range(4):
        start = r.doc_starts[0, k]
        begin = jnp.maximum(begin, jnp.where(place >= start, start, 0))
    angles = (place - begin).astype(F32) * r.frequency[...]
    r.cosine[rows, :] = jnp.cos(angles)
    r.sine[rows, :] = jnp.sin(angles)


def head_forward(r):
    first, low = lane_masks(TOK)

    @pl.loop(0, SEQ)
    def _(t):
        rows = pl.ds(pl.multiple_of(t * TOK, TOK), TOK)
        linear = dot(r.u_rows[t], r.qkv_all[...].reshape(WIDTH, QKV))
        r.q_linear[rows, :] = linear[:, :OWN_Q]
        r.k_linear[rows, :] = linear[:, OWN_Q : OWN_Q + OWN_K]
        cosine, sine = r.cosine[rows, :], r.sine[rows, :]
        for pair in range(2):
            part = linear[:, pair * 128 : (pair + 1) * 128]
            part = norm_rope(part, r.q_gain[...], cosine, sine, first, low).astype(BF)
            r.q_heads[pair, 0, rows, :] = part[:, :HEAD_SIZE]
            r.q_heads[pair, 1, rows, :] = part[:, HEAD_SIZE:]
        part = linear[:, OWN_Q : OWN_Q + OWN_K]
        part = norm_rope(part, r.k_gain[...], cosine, sine, first, low).astype(BF)
        r.k_heads[0, rows, :] = part[:, :HEAD_SIZE]
        r.k_heads[1, rows, :] = part[:, HEAD_SIZE:]
        part = linear[:, OWN_Q + OWN_K :].astype(BF)
        r.v_heads[0, rows, :] = part[:, :HEAD_SIZE]
        r.v_heads[1, rows, :] = part[:, HEAD_SIZE:]


def head_backward(r):
    first, low = lane_masks(TOK)
    r.head_gain_part[...] = jnp.zeros((2, 128), F32)

    @pl.loop(0, SEQ)
    def _(t):
        rows = pl.ds(pl.multiple_of(t * TOK, TOK), TOK)
        cosine, sine = r.cosine[rows, :], r.sine[rows, :]
        for pair in range(2):
            cols = slice(pair * 128, (pair + 1) * 128)
            up = r.d_query[rows, cols].astype(F32)
            back, gain_part = norm_rope_back(up, r.q_linear[rows, cols], r.q_gain[...], cosine, sine, first, low)
            r.d_qkv[rows, cols] = back.astype(BF)
            r.head_gain_part[0:1] += gain_part
        up = jnp.concatenate([r.d_kv[0, rows, :HEAD_SIZE], r.d_kv[1, rows, :HEAD_SIZE]], axis=-1)
        up = up.astype(BF).astype(F32)
        back, gain_part = norm_rope_back(up, r.k_linear[rows, :], r.k_gain[...], cosine, sine, first, low)
        r.d_qkv[rows, OWN_Q : OWN_Q + OWN_K] = back.astype(BF)
        r.head_gain_part[1:2] += gain_part
        up = jnp.concatenate([r.d_kv[0, rows, HEAD_SIZE:], r.d_kv[1, rows, HEAD_SIZE:]], axis=-1)
        r.d_qkv[rows, OWN_Q + OWN_K :] = up.astype(BF)


def units_up(r, t):
    gate_up = dot(r.mid_rows[t], r.gu_all[...].reshape(WIDTH, HIDDEN_TWO))
    gate, up = gate_up[:, :FF_OWN], gate_up[:, FF_OWN:]
    sigmoid = 1.0 / (1.0 + jnp.exp(-gate))
    swish = gate * sigmoid
    r.active[t] = (swish * up).astype(BF)
    blocks = pl.ds(8 * t, 8)
    by_gate = up * (sigmoid * (1.0 + gate * (1.0 - sigmoid)))
    r.d_gu[blocks, :, :FF_OWN] = by_gate.astype(BF).reshape(8, 32, FF_OWN)
    r.d_gu[blocks, :, FF_OWN:] = swish.astype(BF).reshape(8, 32, FF_OWN)


def units_down(r, t):
    d_active = dot_nt(r.cot_rows[t], r.down_all[...].reshape(FF_OWN, WIDTH)).reshape(8, 32, FF_OWN)
    blocks = pl.ds(8 * t, 8)
    r.d_gu[blocks, :, :FF_OWN] = (d_active * r.d_gu[blocks, :, :FF_OWN].astype(F32)).astype(BF)
    r.d_gu[blocks, :, FF_OWN:] = (d_active * r.d_gu[blocks, :, FF_OWN:].astype(F32)).astype(BF)
    d_gu = r.d_gu[blocks].reshape(TOK, HIDDEN_TWO)
    return dot_nt(d_gu, r.gu_all[...].reshape(WIDTH, HIDDEN_TWO))


def whole_block(r):
    l = r.links = Links(r.send_sems, r.recv_sems)
    l.greet(pltpu.get_barrier_semaphore(), l.everyone())
    x = r.inputs[...].astype(F32)
    r.u_rows[l.s] = unit_norm(x).astype(BF)
    own_parts(r)
    own_units(r)
    r.out_all[l.dp, l.s] = r.w_out[...]
    r.qkv_all[l.dp, l.s] = r.w_qkv[l.s]
    r.gu_all[l.dp, l.s] = r.w_gu[l.s]
    r.down_all[l.dp] = r.w_down[...]
    r.cot_rows[l.s] = r.cotangent[...]
    pl.semaphore_wait(pltpu.get_barrier_semaphore(), len(l.everyone()))
    qkv_cols = [l.push(r.w_qkv.at[o], r.qkv_all.at[l.dp, l.s], s=o) for o in l.others]
    out = Gather(l, lambda b: r.out_all.at[b, l.s])
    qkv = Gather(l, lambda b: r.qkv_all.at[b])
    gate_up = [Gather(l, lambda b, g=g: r.gu_all.at[b, g]) for g in (l.s,) + l.others]
    down_a = Gather(l, lambda b: r.down_all.at[b, pl.ds(0, DOWN_A)])
    down_b = PairGather(l, lambda b: r.down_all.at[b, pl.ds(DOWN_A, DOWN_B)])
    out.start_z()
    out.start_y()
    gu_cols = [l.push(r.w_gu.at[o], r.gu_all.at[l.dp, l.s], s=o) for o in l.others]
    u_far = l.push(r.u_rows.at[l.s], r.u_rows.at[l.s], s=l.s2)
    u_near = l.push(r.u_rows.at[l.s], r.u_rows.at[l.s], s=l.s1)
    for copy in qkv_cols:
        copy.wait_recv()
    qkv.start_z()
    qkv.start_y()
    down_a.start_y()
    down_b.start_y()
    gate_up[0].start_y()
    out.step(0)
    qkv.step(0)
    rotation_tables(r, 0)
    out.step(1)
    qkv.step(1)
    rotation_tables(r, 1)
    out.step(2)
    qkv.step(2)
    gate_up[0].start_z()
    for k in range(3):
        gu_cols[k].wait_recv()
        gate_up[1 + k].start_z()
        gate_up[1 + k].start_y()
    u_far.wait_recv()
    u_more = l.push(r.u_rows.at[l.s2], r.u_rows.at[l.s2], s=l.s1)
    out.finish()
    out_far = l.push(r.out_all.at[:, l.s], r.out_all.at[:, l.s], s=l.s2)
    out_near = l.push(r.out_all.at[:, l.s], r.out_all.at[:, l.s], s=l.s1)
    qkv.finish()
    u_near.wait_recv()
    u_more.wait_recv()
    for piece in gate_up[:2]:
        piece.step(0)
    head_forward(r)
    for piece in gate_up[2:]:
        piece.step(0)
    attention_block(r, 0, 3)
    attention_block(r, 1, 3)
    gate_up[0].step(1)
    attention_block(r, 0, 2)
    attention_block(r, 1, 2)
    gate_up[1].step(1)
    out_far.wait_recv()
    out_more = l.push(r.out_all.at[:, l.s2], r.out_all.at[:, l.s2], s=l.s1)
    attention_block(r, 0, 1)
    attention_block(r, 1, 1)
    gate_up[2].step(1)
    attention_block(r, 0, 0)
    attention_block(r, 1, 0)
    att = [l.push(r.att_own.at[o], r.att_local.at[l.s], s=o) for o in l.others]
    cot_far = l.push(r.cot_rows.at[l.s], r.cot_rows.at[l.s], s=l.s2)
    cot_near = l.push(r.cot_rows.at[l.s], r.cot_rows.at[l.s], s=l.s1)
    r.att_local[l.s] = r.att_own[l.s]
    gate_up[3].step(1)
    down_a.start_z()
    gate_up[0].step(2)
    out_near.wait_recv()
    out_more.wait_recv()
    for copy in att:
        copy.wait_recv()
    middle = x
    for part in range(SEQ):
        rows = r.out_all[part * 2 : (part + 1) * 2].reshape(OWN_Q, WIDTH)
        middle = middle + dot(r.att_local[part], rows)
    r.middle[...] = middle
    r.mid_rows[l.s] = unit_norm(middle).astype(BF)
    mid_far = l.push(r.mid_rows.at[l.s], r.mid_rows.at[l.s], s=l.s2)
    mid_near = l.push(r.mid_rows.at[l.s], r.mid_rows.at[l.s], s=l.s1)
    for piece in gate_up[1:]:
        piece.step(2)
    down_a.step(0)
    down_b.start_z()
    cot_far.wait_recv()
    cot_more = l.push(r.cot_rows.at[l.s2], r.cot_rows.at[l.s2], s=l.s1)
    down_b.join()
    mid_far.wait_recv()
    mid_more = l.push(r.mid_rows.at[l.s2], r.mid_rows.at[l.s2], s=l.s1)
    down_a.step(1)
    down_b.step(0)
    down_a.step(2)
    mid_near.wait_recv()
    mid_more.wait_recv()
    for piece in gate_up:
        piece.finish()
    units_up(r, l.s3)
    units_up(r, l.s2)
    down_b.step(1)
    units_up(r, l.s1)
    units_up(r, l.s)
    down_b.step(2)
    cot_near.wait_recv()
    cot_more.wait_recv()
    for t in range(SEQ):
        r.flipped[:, t * TOK : (t + 1) * TOK] = r.active[t].T
    cot = r.cot_rows[...].reshape(ROW, WIDTH)

    @pl.loop(0, 4)
    def _(k):
        rows = pl.ds(pl.multiple_of(k * 288, 32), 288)
        grad = dot(r.flipped[rows, :], cot).astype(BF)
        r.down_part[pl.ds(2 * k, 2)] = grad.reshape(2, FF_SHARD, WIDTH)

    down_a_sum = Scatter(
        l, lambda b: r.down_part.at[b, pl.ds(0, DOWN_A)], lambda k: r.down_a_slots.at[k], lambda k: r.down_a_slots.at[4 + k]
    )
    down_b_sum = PairScatter(
        l,
        lambda b: r.down_part.at[b, pl.ds(DOWN_A, DOWN_B)],
        r.down_b_slots.at[10],
        lambda k: r.down_b_slots.at[k],
        lambda k: r.down_b_slots.at[5 + k],
    )
    down_a_sum.start()
    down_b_sum.start()
    down_b_sum.step(0)
    down_a.finish()
    d_mid = RowSum(l, r.slots_a)
    r.parts[0] = units_down(r, l.s3).astype(BF).reshape(8, 32, WIDTH)
    d_mid.hand_over(r.parts.at[0])
    r.parts[1] = units_down(r, l.s2).astype(BF).reshape(8, 32, WIDTH)
    d_mid.cross(r.parts.at[1])
    down_b_sum.step(1)
    r.parts[2] = units_down(r, l.s1).astype(BF).reshape(8, 32, WIDTH)
    d_mid.near(r.parts.at[2])
    own = units_down(r, l.s)
    down_b_sum.step(2)
    d_values, ffn_gain_part = norm_back_unit(d_mid.total(own), r.middle[...])
    d_middle = r.cotangent[...].astype(F32) + d_values
    r.input_grad[...] = d_middle
    d_branch = d_middle.astype(BF)
    r.gains[0, 1:2, :] = ffn_gain_part
    l.drain()
    for part in range(SEQ):
        rows = r.out_all[part * 2 : (part + 1) * 2].reshape(OWN_Q, WIDTH)
        r.att_own[part] = dot_nt(d_branch, rows).astype(BF)
    d_att = [l.push(r.att_own.at[o], r.d_att_rows.at[l.s], s=o) for o in l.others]
    r.d_att_rows[l.s] = r.att_own[l.s]
    for part in range(SEQ):
        grad = dot_tn(r.att_local[part], d_branch).astype(BF)
        r.out_all[2 * part : 2 * part + 2] = grad.reshape(2, 4, 32, WIDTH)
    for t in range(SEQ):
        r.flipped[:WIDTH, t * TOK : (t + 1) * TOK] = r.mid_rows[t].T
    d_gu = r.d_gu[0:32].reshape(ROW, HIDDEN_TWO)

    @pl.loop(0, 4)
    def _(k):
        rows = pl.ds(pl.multiple_of(k * 256, 256), 256)
        grad = dot(r.flipped[rows, :], d_gu).astype(BF)
        r.gu_all[pl.ds(2 * k, 2)] = grad.reshape(2, 4, 32, HIDDEN_TWO)

    l.greet(r.free, l.column())
    pl.semaphore_wait(r.free, len(l.column()))
    gu_sums = [
        Scatter(
            l,
            lambda b, g=g: r.gu_all.at[b, g],
            lambda k, n=n: r.d_gu.at[4 * n + k],
            lambda k, n=n: r.d_gu.at[16 + 5 * n + k],
        )
        for n, g in enumerate(l.others + (l.s,))
    ]
    for piece in gu_sums:
        piece.start()
    down_a_sum.join()
    down_a_sum.step(0)
    down_b_sum.cross()
    for copy in d_att:
        copy.wait_recv()
    out_row = RowSum(l, r.slots_b)
    out_row.hand_over(r.out_all.at[:, l.s3])
    attention_block_back(r, 0, 3)
    out_row.cross(r.out_all.at[:, l.s2])
    out_row.near(r.out_all.at[:, l.s1])
    down_a_sum.step(1)
    attention_block_back(r, 1, 3)
    attention_block_back(r, 0, 2)
    down_a_sum.step(2)
    attention_block_back(r, 1, 2)
    gu_sums[0].join()
    gu_sums[0].step(0)
    attention_block_back(r, 0, 1)
    attention_block_back(r, 1, 1)
    gu_sums[0].step(1)
    attention_block_back(r, 0, 0)
    attention_block_back(r, 1, 0)
    gu_sums[0].step(2)
    out_total = out_row.total(r.out_all[:, l.s].astype(F32))
    r.out_all[:, l.s] = out_total.astype(BF)
    head_backward(r)
    d_u = RowSum(l, r.slots_a)
    weights = r.qkv_all[...].reshape(WIDTH, QKV)

    def d_u_part(t):
        return dot_nt(r.d_qkv[pl.ds(pl.multiple_of(t * TOK, TOK), TOK), :], weights)

    r.parts[0] = d_u_part(l.s3).astype(BF).reshape(8, 32, WIDTH)
    d_u.hand_over(r.parts.at[0])
    r.parts[1] = d_u_part(l.s2).astype(BF).reshape(8, 32, WIDTH)
    d_u.cross(r.parts.at[1])
    r.parts[2] = d_u_part(l.s1).astype(BF).reshape(8, 32, WIDTH)
    d_u.near(r.parts.at[2])
    own = d_u_part(l.s)
    gu_sums[1].join()
    gu_sums[1].step(0)
    for t in range(SEQ):
        r.flipped[:WIDTH, t * TOK : (t + 1) * TOK] = r.u_rows[t].T
    grad = dot(r.flipped[:WIDTH, :], r.d_qkv[...]).astype(BF)
    r.qkv_all[...] = grad.reshape(8, 4, 32, QKV)
    qkv_sum = Scatter(l, lambda b: r.qkv_all.at[b], lambda k: r.qkv_slots.at[k], lambda k: r.qkv_slots.at[4 + k])
    qkv_sum.start()
    out_sum = Scatter(
        l, lambda b: r.out_all.at[b, l.s], lambda k: r.out_slots.at[k], lambda k: r.out_slots.at[4 + k]
    )
    out_sum.start()
    gu_sums[1].step(1)
    x = r.inputs[...].astype(F32)
    d_values, attn_gain_part = norm_back_unit(d_u.total(own), x)
    r.input_grad[...] += d_values
    r.gains[0, 0:1, :] = attn_gain_part
    r.gains[0, 2:3, 0:128] = r.head_gain_part[0:1]
    r.gains[0, 2:3, 128:256] = r.head_gain_part[1:2]
    r.gains[0, 2:3, 256:] = jnp.zeros((1, WIDTH - 256), F32)
    r.gains[0, 3:8, :] = jnp.zeros((5, WIDTH), F32)
    gains = [l.push(r.gains.at[0], r.gain_slots.at[k], s=o) for k, o in enumerate(l.others)]
    d_u.links.settle((d_u.first, d_u.second, d_u.third))
    gu_sums[1].step(2)
    down_all = r.down_all[...].reshape(FF_OWN, WIDTH)
    last = RowSum(l, r.slots_b)
    r.parts[0] = dot(r.active[l.s3], down_all).astype(BF).reshape(8, 32, WIDTH)
    last.hand_over(r.parts.at[0])
    r.parts[1] = dot(r.active[l.s2], down_all).astype(BF).reshape(8, 32, WIDTH)
    last.cross(r.parts.at[1])
    r.parts[2] = dot(r.active[l.s1], down_all).astype(BF).reshape(8, 32, WIDTH)
    last.near(r.parts.at[2])
    own = r.middle[...] + dot(r.active[l.s], down_all)
    for copy in gains:
        copy.wait_recv()
    r.gains[1] = r.gains[0] + r.gain_slots[0] + r.gain_slots[1] + r.gain_slots[2]
    gains_y = l.push(r.gains.at[1], r.gain_slots.at[3], dp=l.y_peer)
    gu_sums[2].join()
    gu_sums[2].step(0)
    home = []
    r.gu_sum[0] = gu_sums[0].total().astype(BF)
    home.append(l.push(r.gu_sum.at[0], r.gu_grad.at[l.s], s=l.s1))
    gu_sums[2].step(1)
    r.down_grad[0:DOWN_A] = down_a_sum.total()
    r.down_grad[DOWN_A:] = down_b_sum.total()
    r.gu_sum[1] = gu_sums[1].total().astype(BF)
    home.append(l.push(r.gu_sum.at[1], r.gu_grad.at[l.s], s=l.s2))
    gu_sums[2].step(2)
    r.output[...] = last.total(own).astype(BF)
    gu_sums[3].join()
    gu_sums[3].step(0)
    gains_y.wait_recv()
    r.gains[2] = r.gains[1] + r.gain_slots[3]
    gains_z = [l.push(r.gains.at[2], r.gain_slots.at[4 + k], dp=p) for k, p in enumerate(l.z_peers)]
    gu_sums[3].step(1)
    r.gu_sum[2] = gu_sums[2].total().astype(BF)
    home.append(l.push(r.gu_sum.at[2], r.gu_grad.at[l.s], s=l.s3))
    gu_sums[3].step(2)
    qkv_sum.join()
    qkv_sum.step(0)
    out_sum.join()
    out_sum.step(0)
    qkv_sum.step(1)
    out_sum.step(1)
    qkv_sum.step(2)
    out_sum.step(2)
    r.gu_grad[l.s] = gu_sums[3].total().astype(BF)
    r.qkv_sum[...] = qkv_sum.total().astype(BF)
    home += [l.push(r.qkv_sum.at[o], r.qkv_grad.at[l.s], s=o) for o in l.others]
    r.qkv_grad[l.s] = r.qkv_sum[l.s]
    r.out_grad[...] = out_sum.total()
    for copy in gains_z + home:
        copy.wait_recv()
    r.gain_grads[...] = r.gains[2] + r.gain_slots[4] + r.gain_slots[5] + r.gain_slots[6]
    l.drain()


class Names:
    pass


def frequencies():
    steps = np.arange(HEAD_SIZE // 2, dtype=np.float64) * (2.0 / HEAD_SIZE)
    return jnp.asarray(np.tile(THETA ** (-steps), 4)[None], F32)


MAX_COPIES = 260
VMEM_BYTES = 63 * 2**20


def on_device_in_kernels(
    inputs,
    doc_starts,
    cotangent,
    attn_gain,
    w_query,
    key_projection_weight,
    value_projection_weight,
    q_gain,
    k_gain,
    w_out,
    ffn_gain,
    w_gate,
    w_up,
    w_down,
):
    given = dict(
        inputs=inputs,
        cotangent=cotangent,
        attn_gain=attn_gain.astype(F32)[:, None],
        ffn_gain=ffn_gain.astype(F32)[:, None],
        q_gain=jnp.tile(q_gain.astype(F32), 2)[None],
        k_gain=jnp.tile(k_gain.astype(F32), 2)[None],
        w_query=w_query,
        w_key=key_projection_weight,
        w_value=value_projection_weight,
        w_out=w_out,
        w_gate=w_gate,
        w_up=w_up,
        w_down=w_down,
        frequency=frequencies(),
        doc_starts=doc_starts,
    )
    results = dict(
        output=((TOK, WIDTH), BF),
        input_grad=((TOK, WIDTH), F32),
        down_grad=((FF_SHARD, WIDTH), F32),
        out_grad=((32, WIDTH), F32),
        gu_grad=((SEQ, 32, HIDDEN_TWO), BF),
        qkv_grad=((SEQ, 32, QKV), BF),
        gain_grads=((8, WIDTH), F32),
    )
    kept = dict(
        w_qkv=((SEQ, 32, QKV), BF),
        w_gu=((SEQ, 32, HIDDEN_TWO), BF),
        cosine=((ROW, 128), F32),
        sine=((ROW, 128), F32),
        u_rows=((SEQ, TOK, WIDTH), BF),
        cot_rows=((SEQ, TOK, WIDTH), BF),
        mid_rows=((SEQ, TOK, WIDTH), BF),
        qkv_all=((8, 4, 32, QKV), BF),
        gu_all=((8, 4, 32, HIDDEN_TWO), BF),
        down_all=((8, FF_SHARD, WIDTH), BF),
        out_all=((8, 4, 32, WIDTH), BF),
        q_linear=((ROW, OWN_Q), F32),
        k_linear=((ROW, OWN_K), F32),
        q_heads=((2, 2, ROW, HEAD_SIZE), BF),
        k_heads=((2, ROW, HEAD_SIZE), BF),
        v_heads=((2, ROW, HEAD_SIZE), BF),
        log_total=((ROW, 128), F32),
        att_own=((SEQ, TOK, OWN_Q), BF),
        att_local=((SEQ, TOK, OWN_Q), BF),
        middle=((TOK, WIDTH), F32),
        active=((SEQ, TOK, FF_OWN), BF),
        d_gu=((36, 32, HIDDEN_TWO), BF),
        parts=((3, 8, 32, WIDTH), BF),
        slots_a=((3, 8, 32, WIDTH), BF),
        slots_b=((3, 8, 32, WIDTH), BF),
        d_att_rows=((SEQ, TOK, OWN_Q), BF),
        flipped=((FF_OWN, ROW), BF),
        down_part=((8, FF_SHARD, WIDTH), BF),
        down_a_slots=((9, DOWN_A, WIDTH), BF),
        down_b_slots=((11, DOWN_B, WIDTH), BF),
        out_slots=((9, 32, WIDTH), BF),
        qkv_slots=((9, 4, 32, QKV), BF),
        d_query=((ROW, OWN_Q), BF),
        d_kv=((2, ROW, 128), F32),
        d_qkv=((ROW, QKV), BF),
        head_gain_part=((2, 128), F32),
        gains=((3, 8, WIDTH), F32),
        gain_slots=((7, 8, WIDTH), F32),
        gu_sum=((3, 32, HIDDEN_TWO), BF),
        qkv_sum=((4, 32, QKV), BF),
    )

    def body(*refs):
        r = Names()
        names = [*given, *results, *kept]
        for name, ref in zip(names, refs):
            setattr(r, name, ref)
        r.send_sems, r.recv_sems, r.free = refs[len(names) :]
        whole_block(r)

    done = pl.pallas_call(
        body,
        out_shape=[jax.ShapeDtypeStruct(*result) for result in results.values()],
        in_specs=[
            pl.BlockSpec(memory_space=pltpu.SMEM if a is doc_starts else pltpu.VMEM) for a in given.values()
        ],
        out_specs=[pl.BlockSpec(memory_space=pltpu.VMEM)] * len(results),
        scratch_shapes=[pltpu.VMEM(*shape) for shape in kept.values()]
        + [
            pltpu.SemaphoreType.DMA((MAX_COPIES,)),
            pltpu.SemaphoreType.DMA((MAX_COPIES,)),
            pltpu.SemaphoreType.REGULAR,
        ],
        compiler_params=pltpu.CompilerParams(
            collective_id=0, has_side_effects=True, vmem_limit_bytes=VMEM_BYTES
        ),
        cost_estimate=pl.CostEstimate(flops=30_000_000_000, bytes_accessed=10_000_000, transcendentals=0),
    )(*given.values())
    output, input_grad, down_grad, out_grad, gu_grad, qkv_grad, gains = done
    rows = w_query.shape[0]
    attn_scale = attn_gain.astype(F32)[:, None]
    ffn_scale = ffn_gain.astype(F32)[:, None]

    def whole_heads(part):
        return part.astype(F32).transpose(1, 0, 2).reshape(rows, -1) * attn_scale

    def whole_units(part):
        part = part.astype(F32).reshape(SEQ, rows, 8, FF_SHARD).transpose(1, 2, 0, 3)
        return part.reshape(rows, -1) * ffn_scale

    place = (lax.axis_index("dp") * SEQ + lax.axis_index("seq")) * rows
    attn_part = lax.dynamic_slice(gains[0], (place,), (rows,)) / attn_gain.astype(F32)
    ffn_part = lax.dynamic_slice(gains[1], (place,), (rows,)) / ffn_gain.astype(F32)
    return (
        output,
        input_grad,
        attn_part,
        whole_heads(qkv_grad[..., :OWN_Q]),
        whole_heads(qkv_grad[..., OWN_Q : OWN_Q + OWN_K]),
        whole_heads(qkv_grad[..., OWN_Q + OWN_K :]),
        gains[2, 0:64] + gains[2, 64:128],
        gains[2, 128:192] + gains[2, 192:256],
        out_grad,
        ffn_part,
        whole_units(gu_grad[..., :FF_OWN]),
        whole_units(gu_grad[..., FF_OWN:]),
        down_grad,
    )


def solution(mesh):
    in_kernels = (mesh.shape["dp"], mesh.shape["seq"]) == (8, 4)
    placed = (
        P(("dp", "seq"), None),
        P("dp", None),
        P(("dp", "seq"), None),
        P(("dp", "seq")),
        P(("dp", "seq"), None),
        P(("dp", "seq"), None),
        P(("dp", "seq"), None),
        P(),
        P(),
        P(("dp", "seq"), None),
        P(("dp", "seq")),
        P(("dp", "seq"), None),
        P(("dp", "seq"), None),
        P(("dp", "seq"), None),
    )
    return jax.shard_map(
        on_device_in_kernels if in_kernels else on_device,
        mesh=mesh,
        in_specs=placed,
        out_specs=(
            P(("dp", "seq"), None),
            P(("dp", "seq"), None),
            P(("dp", "seq")),
            P(("dp", "seq"), None),
            P(("dp", "seq"), None),
            P(("dp", "seq"), None),
            P(),
            P(),
            P(("dp", "seq"), None),
            P(("dp", "seq")),
            P(("dp", "seq"), None),
            P(("dp", "seq"), None),
            P(("dp", "seq"), None),
        ),
        check_vma=False,
    )
```

```python
import jax
import jax.numpy as jnp
import numpy as np
from jax import lax
from jax.experimental import pallas as pl
from jax.experimental.pallas import tpu as pltpu
from jax.sharding import PartitionSpec as P

QUERY_HEADS = 16
KEY_VALUE_HEADS = 8
HEAD_SIZE = 64
FF = 4608


EPS = 1e-05
THETA = 1000000.0
MASKED = -1e30
CONTRACT_ROWS = (((0,), (0,)), ((), ()))
CONTRACT_COLS = (((1,), (1,)), ((), ()))


def rms_norm(values, gain_vec):
    return values * lax.rsqrt(jnp.mean(values * values, axis=-1, keepdims=True) + EPS) * gain_vec


def rotate_half(values):
    half_len = values.shape[-1] // 2
    return jnp.concatenate([-values[..., half_len:], values[..., :half_len]], axis=-1)


def unrotate_half(values):
    half_len = values.shape[-1] // 2
    return jnp.concatenate([values[..., half_len:], -values[..., :half_len]], axis=-1)


def row_layout(row_starts, places):
    inside = places[:, None] >= row_starts[None, :]
    doc_ids = jnp.sum(inside.astype(jnp.int32), axis=1) - 1
    begins = jnp.max(jnp.where(inside, row_starts[None, :], 0), axis=1)
    offsets = (places - begins).astype(jnp.float32)
    freq_steps = jnp.arange(HEAD_SIZE // 2, dtype=jnp.float32) * (2.0 / HEAD_SIZE)
    frequency = THETA ** (-freq_steps)
    angles = offsets[:, None] * frequency[None, :]
    angles = jnp.concatenate([angles, angles], axis=-1)
    return (doc_ids, jnp.cos(angles), jnp.sin(angles))


def norm_back(upstream, values, gain_vec):
    inverse = lax.rsqrt(jnp.mean(values * values, axis=-1, keepdims=True) + EPS)
    unit_vec = values * inverse
    gain_part = jnp.sum(upstream * unit_vec, axis=tuple(range(values.ndim - 1)))
    scaled = upstream * gain_vec
    return (
        inverse * (scaled - unit_vec * jnp.mean(scaled * unit_vec, axis=-1, keepdims=True)),
        gain_part,
    )


def head_forward_pass(linear, gain_vec, cosine_table, sine_table, heads):
    local_rows = linear.shape[0]
    shaped = rms_norm(linear.reshape(local_rows, heads, HEAD_SIZE), gain_vec)
    turned = shaped * cosine_table + rotate_half(shaped) * sine_table
    return turned.astype(jnp.bfloat16).reshape(local_rows, heads * HEAD_SIZE)


def head_backward_pass(grad_in, linear, gain_vec, cosine_table, sine_table, heads):
    local_rows = linear.shape[0]
    shaped = linear.reshape(local_rows, heads, HEAD_SIZE)
    upstream = grad_in.astype(jnp.float32).reshape(local_rows, heads, HEAD_SIZE)
    d_normed = upstream * cosine_table + unrotate_half(upstream * sine_table)
    d_linear, gain_part = norm_back(d_normed, shaped, gain_vec)
    return (d_linear.reshape(local_rows, heads * HEAD_SIZE).astype(jnp.bfloat16), gain_part)


def block_scores(q_block, keys_all, block_places, block_docs, places, doc_ids):
    score_scale = HEAD_SIZE ** (-0.5)
    scores = (
        jnp.einsum("qkgd,skd->kgqs", q_block, keys_all, preferred_element_type=jnp.float32)
        * score_scale
    )
    allowed = (places[None, :] <= block_places[:, None]) & (doc_ids[None, :] == block_docs[:, None])
    return jnp.where(allowed[None, None], scores, MASKED)


def attend_forward(query_rows, keys_in, values_in, places, doc_ids):
    total_length = query_rows.shape[0]
    kv_heads = keys_in.shape[1] // HEAD_SIZE
    query_group = QUERY_HEADS // KEY_VALUE_HEADS
    block_length = min(512, total_length)
    number_of_blocks = total_length // block_length
    keys_all = keys_in.reshape(total_length, kv_heads, HEAD_SIZE)
    values_all = values_in.reshape(total_length, kv_heads, HEAD_SIZE)
    grouped_queries = query_rows.reshape(
        number_of_blocks, block_length, kv_heads, query_group, HEAD_SIZE
    )

    def one_block(pieces):
        q_block, block_places, block_docs = pieces
        scores = block_scores(q_block, keys_all, block_places, block_docs, places, doc_ids)
        row_max = jnp.max(scores, axis=-1, keepdims=True)
        weights = jnp.exp(scores - row_max)
        sum_total = jnp.sum(weights, axis=-1, keepdims=True)
        soft_max = (weights / sum_total).astype(jnp.bfloat16)
        mixture = jnp.einsum(
            "kgqs,skd->qkgd", soft_max, values_all, preferred_element_type=jnp.float32
        )
        return (mixture.astype(jnp.bfloat16), row_max[..., 0] + jnp.log(sum_total[..., 0]))

    mixture, log_total = lax.map(
        one_block,
        (
            grouped_queries,
            places.reshape(number_of_blocks, block_length),
            doc_ids.reshape(number_of_blocks, block_length),
        ),
    )
    return (mixture.reshape(total_length, kv_heads * query_group * HEAD_SIZE), log_total)


def attend_back(query_rows, keys_in, values_in, grad_out, log_total, places, doc_ids):
    total_length = query_rows.shape[0]
    kv_heads = keys_in.shape[1] // HEAD_SIZE
    query_group = QUERY_HEADS // KEY_VALUE_HEADS
    block_length = min(512, total_length)
    number_of_blocks = total_length // block_length
    score_scale = HEAD_SIZE ** (-0.5)
    keys_all = keys_in.reshape(total_length, kv_heads, HEAD_SIZE)
    values_all = values_in.reshape(total_length, kv_heads, HEAD_SIZE)
    grouped_queries = query_rows.reshape(
        number_of_blocks, block_length, kv_heads, query_group, HEAD_SIZE
    )
    grads_all = grad_out.reshape(number_of_blocks, block_length, kv_heads, query_group, HEAD_SIZE)

    def one_block(carried, pieces):
        key_total, value_total = carried
        q_block, g_block, block_log, block_places, block_docs = pieces
        scores = block_scores(q_block, keys_all, block_places, block_docs, places, doc_ids)
        chances = jnp.exp(scores - block_log[..., None])
        d_chances = jnp.einsum(
            "qkgd,skd->kgqs", g_block, values_all, preferred_element_type=jnp.float32
        )
        row_dots = jnp.sum(d_chances * chances, axis=-1, keepdims=True)
        d_scores = (chances * (d_chances - row_dots)).astype(jnp.bfloat16)
        d_query = (
            jnp.einsum("kgqs,skd->qkgd", d_scores, keys_all, preferred_element_type=jnp.float32)
            * score_scale
        )
        key_total = (
            key_total
            + jnp.einsum("kgqs,qkgd->skd", d_scores, q_block, preferred_element_type=jnp.float32)
            * score_scale
        )
        value_total = value_total + jnp.einsum(
            "kgqs,qkgd->skd",
            chances.astype(jnp.bfloat16),
            g_block,
            preferred_element_type=jnp.float32,
        )
        return ((key_total, value_total), d_query)

    zero_kv = jnp.zeros((total_length, kv_heads, HEAD_SIZE), jnp.float32)
    inputs_scan = (
        grouped_queries,
        grads_all,
        log_total,
        places.reshape(number_of_blocks, block_length),
        doc_ids.reshape(number_of_blocks, block_length),
    )
    (key_total, value_total), d_query = lax.scan(one_block, (zero_kv, zero_kv), inputs_scan)
    return (
        d_query.reshape(total_length, kv_heads * query_group * HEAD_SIZE).astype(jnp.bfloat16),
        key_total.reshape(total_length, kv_heads * HEAD_SIZE).astype(jnp.bfloat16),
        value_total.reshape(total_length, kv_heads * HEAD_SIZE).astype(jnp.bfloat16),
    )


def on_device(
    inputs,
    doc_starts,
    cotangent,
    attn_gain,
    w_query,
    key_projection_weight,
    value_projection_weight,
    q_gain,
    k_gain,
    w_out,
    ffn_gain,
    w_gate,
    w_up,
    w_down,
):
    local_rows = inputs.shape[0]
    seq_parts = lax.axis_size("seq")
    total_length = local_rows * seq_parts
    row_starts = doc_starts[0]
    local_places = lax.axis_index("seq") * local_rows + jnp.arange(local_rows, dtype=jnp.int32)
    unused_docs, cosine_table, sine_table = row_layout(row_starts, local_places)
    cosine_table = cosine_table[:, None, :]
    sine_table = sine_table[:, None, :]
    all_places = jnp.arange(total_length, dtype=jnp.int32)
    all_docs = jnp.sum((all_places[:, None] >= row_starts[None, :]).astype(jnp.int32), axis=1) - 1
    q_scale = q_gain.astype(jnp.float32)
    key_norm_scale = k_gain.astype(jnp.float32)
    attn_scale, query_full, key_full, value_full, out_full = (
        lax.all_gather(attn_gain, ("dp", "seq"), axis=0, tiled=True),
        lax.all_gather(w_query, ("dp", "seq"), axis=0, tiled=True),
        lax.all_gather(key_projection_weight, ("dp", "seq"), axis=0, tiled=True),
        lax.all_gather(value_projection_weight, ("dp", "seq"), axis=0, tiled=True),
        lax.all_gather(w_out, ("dp", "seq"), axis=0, tiled=True),
    )
    source = inputs.astype(jnp.float32)
    normalized_input = rms_norm(source, attn_scale.astype(jnp.float32)).astype(jnp.bfloat16)
    q_linear = jnp.dot(normalized_input, query_full, preferred_element_type=jnp.float32)
    key_linear_output = jnp.dot(normalized_input, key_full, preferred_element_type=jnp.float32)
    q_sent = head_forward_pass(q_linear, q_scale, cosine_table, sine_table, QUERY_HEADS)
    key_sent_rows = head_forward_pass(
        key_linear_output, key_norm_scale, cosine_table, sine_table, KEY_VALUE_HEADS
    )
    v_sent = jnp.dot(normalized_input, value_full, preferred_element_type=jnp.float32).astype(
        jnp.bfloat16
    )
    q_heads, k_heads, v_heads = (
        lax.all_to_all(q_sent, "seq", split_axis=1, concat_axis=0, tiled=True),
        lax.all_to_all(key_sent_rows, "seq", split_axis=1, concat_axis=0, tiled=True),
        lax.all_to_all(v_sent, "seq", split_axis=1, concat_axis=0, tiled=True),
    )
    mixture, log_total = attend_forward(q_heads, k_heads, v_heads, all_places, all_docs)
    attended = lax.all_to_all(mixture, "seq", split_axis=0, concat_axis=1, tiled=True)
    middle = source + jnp.dot(attended, out_full, preferred_element_type=jnp.float32)
    ffn_scale, gate_full, up_full, down_full = (
        lax.all_gather(ffn_gain, ("dp", "seq"), axis=0, tiled=True),
        lax.all_gather(w_gate, ("dp", "seq"), axis=0, tiled=True),
        lax.all_gather(w_up, ("dp", "seq"), axis=0, tiled=True),
        lax.all_gather(w_down, ("dp", "seq"), axis=0, tiled=True),
    )
    normed_mid = rms_norm(middle, ffn_scale.astype(jnp.float32)).astype(jnp.bfloat16)
    gate_lin = jnp.dot(normed_mid, gate_full, preferred_element_type=jnp.float32)
    upward = jnp.dot(normed_mid, up_full, preferred_element_type=jnp.float32)
    sigmoid_gate = jax.nn.sigmoid(gate_lin)
    swish = gate_lin * sigmoid_gate
    active = (swish * upward).astype(jnp.bfloat16)
    output = (middle + jnp.dot(active, down_full, preferred_element_type=jnp.float32)).astype(
        jnp.bfloat16
    )
    ffn_scale, gate_full, up_full, down_full = (
        lax.all_gather(ffn_gain, ("dp", "seq"), axis=0, tiled=True),
        lax.all_gather(w_gate, ("dp", "seq"), axis=0, tiled=True),
        lax.all_gather(w_up, ("dp", "seq"), axis=0, tiled=True),
        lax.all_gather(w_down, ("dp", "seq"), axis=0, tiled=True),
    )
    d_active = lax.dot_general(
        cotangent, down_full, CONTRACT_COLS, preferred_element_type=jnp.float32
    )
    d_gate = (d_active * upward * (sigmoid_gate * (1.0 + gate_lin * (1.0 - sigmoid_gate)))).astype(
        jnp.bfloat16
    )
    d_up = (d_active * swish).astype(jnp.bfloat16)
    d_normed_mid = lax.dot_general(
        d_gate, gate_full, CONTRACT_COLS, preferred_element_type=jnp.float32
    )
    d_normed_mid = d_normed_mid + lax.dot_general(
        d_up, up_full, CONTRACT_COLS, preferred_element_type=jnp.float32
    )
    d_middle_norm, ffn_gain_part = norm_back(d_normed_mid, middle, ffn_scale.astype(jnp.float32))
    d_middle = cotangent.astype(jnp.float32) + d_middle_norm
    d_branch = d_middle.astype(jnp.bfloat16)
    attn_scale, query_full, key_full, value_full, out_full = (
        lax.all_gather(attn_gain, ("dp", "seq"), axis=0, tiled=True),
        lax.all_gather(w_query, ("dp", "seq"), axis=0, tiled=True),
        lax.all_gather(key_projection_weight, ("dp", "seq"), axis=0, tiled=True),
        lax.all_gather(value_projection_weight, ("dp", "seq"), axis=0, tiled=True),
        lax.all_gather(w_out, ("dp", "seq"), axis=0, tiled=True),
    )
    d_attended = lax.dot_general(
        d_branch, out_full, CONTRACT_COLS, preferred_element_type=jnp.float32
    ).astype(jnp.bfloat16)
    d_mixture = lax.all_to_all(d_attended, "seq", split_axis=1, concat_axis=0, tiled=True)
    d_q_heads, d_k_heads, d_v_heads = attend_back(
        q_heads, k_heads, v_heads, d_mixture, log_total, all_places, all_docs
    )
    d_q_sent, key_sent_gradient, d_v_sent = (
        lax.all_to_all(d_q_heads, "seq", split_axis=0, concat_axis=1, tiled=True),
        lax.all_to_all(d_k_heads, "seq", split_axis=0, concat_axis=1, tiled=True),
        lax.all_to_all(d_v_heads, "seq", split_axis=0, concat_axis=1, tiled=True),
    )
    d_q_linear, q_gain_part = head_backward_pass(
        d_q_sent, q_linear, q_scale, cosine_table, sine_table, QUERY_HEADS
    )
    key_linear_gradient, key_gain_piece = head_backward_pass(
        key_sent_gradient,
        key_linear_output,
        key_norm_scale,
        cosine_table,
        sine_table,
        KEY_VALUE_HEADS,
    )
    d_normed = lax.dot_general(
        d_q_linear, query_full, CONTRACT_COLS, preferred_element_type=jnp.float32
    )
    d_normed = d_normed + lax.dot_general(
        key_linear_gradient, key_full, CONTRACT_COLS, preferred_element_type=jnp.float32
    )
    d_normed = d_normed + lax.dot_general(
        d_v_sent, value_full, CONTRACT_COLS, preferred_element_type=jnp.float32
    )
    d_source_norm, attn_gain_part = norm_back(d_normed, source, attn_scale.astype(jnp.float32))
    input_grad = d_middle + d_source_norm
    attn_columns = jnp.concatenate([d_q_linear, key_linear_gradient, d_v_sent], axis=1)
    ffn_columns = jnp.concatenate([d_gate, d_up], axis=1)
    left = normalized_input
    first_part = lax.dot_general(
        left, attn_columns, CONTRACT_ROWS, preferred_element_type=jnp.float32
    )
    second_part = lax.dot_general(
        normed_mid, ffn_columns, CONTRACT_ROWS, preferred_element_type=jnp.float32
    )
    width_sums = lax.psum_scatter(
        jnp.concatenate([first_part, second_part], axis=1),
        ("dp", "seq"),
        scatter_dimension=0,
        tiled=True,
    )
    left = attended
    out_grad = lax.psum_scatter(
        lax.dot_general(left, d_branch, CONTRACT_ROWS, preferred_element_type=jnp.float32),
        ("dp", "seq"),
        scatter_dimension=0,
        tiled=True,
    )
    left = active
    down_grad = lax.psum_scatter(
        lax.dot_general(left, cotangent, CONTRACT_ROWS, preferred_element_type=jnp.float32),
        ("dp", "seq"),
        scatter_dimension=0,
        tiled=True,
    )
    attn_gain_grad, ffn_gain_grad = (
        lax.psum_scatter(attn_gain_part, ("dp", "seq"), scatter_dimension=0, tiled=True),
        lax.psum_scatter(ffn_gain_part, ("dp", "seq"), scatter_dimension=0, tiled=True),
    )
    q_gain_grad, k_gain_grad = lax.psum((q_gain_part, key_gain_piece), ("dp", "seq"))
    q_cols = QUERY_HEADS * HEAD_SIZE
    kv_cols = KEY_VALUE_HEADS * HEAD_SIZE
    query_grad = width_sums[:, :q_cols]
    key_grad = width_sums[:, q_cols : q_cols + kv_cols]
    value_grad = width_sums[:, q_cols + kv_cols : q_cols + 2 * kv_cols]
    gate_grad = width_sums[:, q_cols + 2 * kv_cols : q_cols + 2 * kv_cols + FF]
    up_grad = width_sums[:, q_cols + 2 * kv_cols + FF :]
    return (
        output,
        input_grad,
        attn_gain_grad,
        query_grad,
        key_grad,
        value_grad,
        q_gain_grad,
        k_gain_grad,
        out_grad,
        ffn_gain_grad,
        gate_grad,
        up_grad,
        down_grad,
    )


BF = jnp.bfloat16
F32 = jnp.float32
MESH = pl.DeviceIdType.MESH
SEQ = 4
PLANES = 4
TOK = 256
WIDTH = 1024
ROW = 1024
OWN_Q = 256
OWN_K = 128
QKV = 512
FF_OWN = 1152
FF_SHARD = 144
HIDDEN_TWO = 2304
DOWN_A = 64
DOWN_B = 80
SUM_A = 96
SUM_B = 48


def flip(value, bit):
    return value + bit - 2 * bit * lax.rem(lax.div(value, bit), 2)


def dot(left, right):
    return lax.dot_general(left, right, (((1,), (0,)), ((), ())), preferred_element_type=F32)


def dot_nt(left, right):
    return lax.dot_general(left, right, (((1,), (1,)), ((), ())), preferred_element_type=F32)


def dot_tn(left, right):
    return lax.dot_general(left, right, (((0,), (0,)), ((), ())), preferred_element_type=F32)


class Links:
    def __init__(self, send_sems, recv_sems):
        self.send_sems, self.recv_sems = send_sems, recv_sems
        self.used = 0
        self.open = []
        self.dp = lax.axis_index("dp")
        self.s = lax.axis_index("seq")
        self.s1 = flip(self.s, 1)
        self.s2 = flip(self.s, 2)
        self.s3 = flip(self.s1, 2)
        self.others = (self.s1, self.s2, self.s3)
        self.y = lax.rem(self.dp, 2)
        self.z = lax.div(self.dp, 2)
        self.y_peer = flip(self.dp, 1)
        z1 = flip(self.z, 1)
        self.planes = (z1, flip(self.z, 2), flip(z1, 2))
        self.z_peers = tuple(2 * z + self.y for z in self.planes)

    def greet(self, semaphore, partners):
        for place in partners:
            pl.semaphore_signal(semaphore, inc=1, device_id=place, device_id_type=MESH)

    def column(self):
        return [(p, self.s) for p in (self.y_peer,) + self.z_peers]

    def everyone(self):
        return [(self.dp, s) for s in self.others] + self.column()

    def plan(self, src, dst, dp=None, s=None):
        n = self.used
        self.used += 1
        copy = pltpu.make_async_remote_copy(
            src_ref=src,
            dst_ref=dst,
            send_sem=self.send_sems.at[n],
            recv_sem=self.recv_sems.at[n],
            device_id=(self.dp if dp is None else dp, self.s if s is None else s),
            device_id_type=MESH,
        )
        return copy

    def push(self, src, dst, dp=None, s=None, when=None):
        copy = self.plan(src, dst, dp, s)
        if when is None:
            copy.start()
        else:
            pl.when(when)(copy.start)
        self.open.append((copy, when))
        return copy

    def settle(self, copies):
        for copy in copies:
            copy.wait_send()
        self.open = [item for item in self.open if all(item[0] is not copy for copy in copies)]

    def drain(self):
        for copy, when in self.open:
            if when is None:
                copy.wait_send()
            else:
                pl.when(when)(copy.wait_send)
        self.open = []


class Line:
    def __init__(self, links, view):
        self.links, self.view = links, view
        self.hops = []

    def pass_on(self, step):
        l = self.links
        below, above = l.z - step, l.z + step
        low = self.view(jnp.maximum(below, 0))
        high = self.view(jnp.minimum(above, PLANES - 1))
        up = l.push(
            low, low, dp=jnp.minimum(l.dp + 2, 2 * PLANES - 1), when=(below >= 0) & (l.z < PLANES - 1)
        )
        down = l.push(high, high, dp=jnp.maximum(l.dp - 2, 0), when=(above <= PLANES - 1) & (l.z > 0))
        self.hops.append((up, down))

    def start(self):
        self.pass_on(0)

    def step(self, k):
        l = self.links
        below, above = l.z - 1 - k, l.z + 1 + k
        from_below, from_above = below >= 0, above <= PLANES - 1
        pl.when(from_below)(self.hops[k][0].wait_recv)
        pl.when(from_above)(self.hops[k][1].wait_recv)
        if k < PLANES - 2:
            self.pass_on(k + 1)
        return [
            (from_below, self.view(jnp.maximum(below, 0))),
            (from_above, self.view(jnp.minimum(above, PLANES - 1))),
        ]


class Gather:
    def __init__(self, links, view):
        self.links = links
        self.line = Line(links, lambda z: view(2 * z + links.y))
        self.own = view(links.dp)
        self.over_y = []

    def start_y(self):
        self.over_y.append((None, self.links.push(self.own, self.own, dp=self.links.y_peer)))

    def start_z(self):
        self.line.start()

    def step(self, k):
        for when, block in self.line.step(k):
            copy = self.links.push(block, block, dp=self.links.y_peer, when=when)
            self.over_y.append((when, copy))

    def finish(self):
        for when, copy in self.over_y:
            if when is None:
                copy.wait_recv()
            else:
                pl.when(when)(copy.wait_recv)


class PairGather:
    def __init__(self, links, view):
        self.links = links
        self.near = Line(links, lambda z: view(2 * z + links.y))
        self.far = Line(links, lambda z: view(2 * z + 1 - links.y))
        self.own = view(links.dp)

    def start_y(self):
        self.over_y = self.links.push(self.own, self.own, dp=self.links.y_peer)

    def start_z(self):
        self.near.start()

    def join(self):
        self.over_y.wait_recv()
        self.far.start()

    def step(self, k):
        self.near.step(k)
        self.far.step(k)


class Chain:
    def __init__(self, links, view, slots):
        self.links, self.view, self.slots = links, view, slots
        self.up, self.down = {}, {}

    def start(self):
        l = self.links
        last = PLANES - 1
        for d in range(PLANES):
            if d > 0:
                self.up[d] = l.plan(self.view(d), self.slots(d), dp=jnp.minimum(l.dp + 2, 2 * last + 1))
            if d < last:
                place = jnp.where(l.z == d + 1, PLANES, d)
                self.down[d] = l.plan(self.view(d), self.slots(place), dp=jnp.maximum(l.dp - 2, 0))

    def add(self, d, copy):
        copy.wait_recv()
        block = self.view(d)
        block[...] = (block[...].astype(F32) + self.slots(d)[...].astype(F32)).astype(BF)

    def step(self, j):
        last = PLANES - 1

        @pl.when(self.links.z == j)
        def _():
            for d in range(last, j, -1):
                if j > 0:
                    self.add(d, self.up[d])
                self.up[d].start()

        @pl.when(self.links.z == last - j)
        def _():
            for d in range(last - j):
                if j > 0:
                    self.add(d, self.down[d])
                self.down[d].start()

        for d in range(PLANES):
            if d > j:
                self.links.open.append((self.up[d], self.links.z == j))
            if d < last - j:
                self.links.open.append((self.down[d], self.links.z == last - j))

    def total(self):
        l = self.links
        for d in range(PLANES):
            if d > 0:
                pl.when(l.z == d)(self.up[d].wait_recv)
            if d < PLANES - 1:
                pl.when(l.z == d)(self.down[d].wait_recv)
        own = self.view(l.z)[...].astype(F32)
        below = jnp.where(l.z > 0, self.slots(l.z)[...].astype(F32), 0.0)
        above = jnp.where(l.z < PLANES - 1, self.slots(PLANES)[...].astype(F32), 0.0)
        return own + (below + above)


class Scatter:
    def __init__(self, links, view, y_slots, z_slots):
        self.links, self.view, self.y_slots = links, view, y_slots
        self.chain = Chain(links, lambda z: view(2 * z + links.y), z_slots)

    def start(self):
        l = self.links
        self.order = [jnp.where(l.z < PLANES // 2, PLANES - 1 - k, k) for k in range(PLANES)]
        self.over_y = [
            l.push(self.view(2 * d + 1 - l.y), self.y_slots(k), dp=l.y_peer) for k, d in enumerate(self.order)
        ]
        self.chain.start()

    def join(self):
        for k, copy in enumerate(self.over_y):
            copy.wait_recv()
            block = self.view(2 * self.order[k] + self.links.y)
            block[...] = (block[...].astype(F32) + self.y_slots(k)[...].astype(F32)).astype(BF)

    def step(self, j):
        self.chain.step(j)

    def total(self):
        return self.chain.total()


class PairScatter:
    def __init__(self, links, view, y_slot, near_slots, far_slots):
        self.links, self.view, self.y_slot = links, view, y_slot
        self.near = Chain(links, lambda z: view(2 * z + links.y), near_slots)
        self.far = Chain(links, lambda z: view(2 * z + 1 - links.y), far_slots)

    def start(self):
        self.far.start()
        self.near.start()

    def step(self, j):
        self.far.step(j)
        self.near.step(j)

    def cross(self):
        l = self.links
        block = self.view(2 * l.z + 1 - l.y)
        block[...] = self.far.total().astype(BF)
        self.over_y = l.push(block, self.y_slot, dp=l.y_peer)

    def total(self):
        own = self.near.total()
        self.over_y.wait_recv()
        return own + self.y_slot[...].astype(F32)


class RowSum:
    def __init__(self, links, slots):
        self.links, self.slots = links, slots

    def hand_over(self, src):
        self.first = self.links.push(src, self.slots.at[0], s=self.links.s1)

    def cross(self, src):
        self.first.wait_recv()
        src[...] = (src[...].astype(F32) + self.slots[0].astype(F32).reshape(src.shape)).astype(BF)
        self.second = self.links.push(src, self.slots.at[1], s=self.links.s2)

    def near(self, src):
        self.third = self.links.push(src, self.slots.at[2], s=self.links.s1)

    def total(self, own):
        self.third.wait_recv()
        self.second.wait_recv()
        return own + self.slots[1].astype(F32).reshape(own.shape) + self.slots[2].astype(F32).reshape(own.shape)


def lane_masks(rows):
    lane = lax.broadcasted_iota(jnp.int32, (rows, 128), 1)
    return lane < 64, lax.rem(lane, 64) < 32


def turned(values, low):
    return jnp.where(low, -pltpu.roll(values, 96, 1), pltpu.roll(values, 32, 1))


def unturned(values, low):
    return jnp.where(low, pltpu.roll(values, 96, 1), -pltpu.roll(values, 32, 1))


def per_head_mean(values, first):
    left = jnp.sum(jnp.where(first, values, 0.0), axis=-1, keepdims=True)
    right = jnp.sum(jnp.where(first, 0.0, values), axis=-1, keepdims=True)
    return jnp.where(first, left, right) * (1.0 / HEAD_SIZE)


def norm_rope(values, gain, cosine, sine, first, low):
    normed = values * lax.rsqrt(per_head_mean(values * values, first) + EPS) * gain
    return normed * cosine + turned(normed, low) * sine


def norm_rope_back(upstream, values, gain, cosine, sine, first, low):
    d_normed = upstream * cosine + unturned(upstream * sine, low)
    inverse = lax.rsqrt(per_head_mean(values * values, first) + EPS)
    unit = values * inverse
    scaled = d_normed * gain
    d_values = inverse * (scaled - unit * per_head_mean(scaled * unit, first))
    return d_values, jnp.sum(d_normed * unit, axis=0, keepdims=True)


def allowed_block(r, block, keys):
    query = lax.broadcasted_iota(jnp.int32, (TOK, keys), 0) + block * TOK
    key = lax.broadcasted_iota(jnp.int32, (TOK, keys), 1)
    place = lax.broadcasted_iota(jnp.int32, (TOK, 1), 0) + block * TOK
    begin = jnp.zeros((TOK, 1), jnp.int32)
    for k in range(4):
        start = r.doc_starts[0, k]
        begin = jnp.maximum(begin, jnp.where(place >= start, start, 0))
    return (key <= query) & (key >= begin)


SCORE_SCALE = HEAD_SIZE ** (-0.5)


def attention_block(r, pair, block):
    keys = (block + 1) * TOK
    rows = pl.ds(block * TOK, TOK)
    queries = r.q_heads[pair, :, rows, :].reshape(2 * TOK, HEAD_SIZE)
    scores = dot_nt(queries, r.k_heads[pair, :keys, :]).reshape(2, TOK, keys) * SCORE_SCALE
    scores = jnp.where(allowed_block(r, block, keys)[None], scores, MASKED)
    top = jnp.max(scores, axis=-1, keepdims=True)
    weights = jnp.exp(scores - top)
    total = jnp.sum(weights, axis=-1, keepdims=True)
    mixed = dot(weights.astype(BF).reshape(2 * TOK, keys), r.v_heads[pair, :keys, :])
    mixed = mixed.reshape(2, TOK, HEAD_SIZE) / total
    log_total = top + jnp.log(total)
    r.log_total[rows, 2 * pair : 2 * pair + 1] = log_total[0]
    r.log_total[rows, 2 * pair + 1 : 2 * pair + 2] = log_total[1]
    r.att_own[block, :, pair * 128 : (pair + 1) * 128] = jnp.concatenate(
        [mixed[0], mixed[1]], axis=-1
    ).astype(BF)


def attention_block_back(r, pair, block):
    keys = (block + 1) * TOK
    rows = pl.ds(block * TOK, TOK)
    queries = r.q_heads[pair, :, rows, :].reshape(2 * TOK, HEAD_SIZE)
    grads = r.d_att_rows[block, :, pair * 128 : (pair + 1) * 128]
    grads = jnp.concatenate([grads[:, :HEAD_SIZE], grads[:, HEAD_SIZE:]], axis=0)
    keys_in, values_in = r.k_heads[pair, :keys, :], r.v_heads[pair, :keys, :]
    scores = dot_nt(queries, keys_in).reshape(2, TOK, keys) * SCORE_SCALE
    log_total = jnp.stack([r.log_total[rows, 2 * pair + g : 2 * pair + g + 1] for g in range(2)])
    chances = jnp.exp(scores - log_total)
    chances = jnp.where(allowed_block(r, block, keys)[None], chances, 0.0)
    d_chances = dot_nt(grads, values_in).reshape(2, TOK, keys)
    row_dots = jnp.sum(d_chances * chances, axis=-1, keepdims=True)
    d_scores = (chances * (d_chances - row_dots)).astype(BF).reshape(2 * TOK, keys)
    d_query = (dot(d_scores, keys_in) * SCORE_SCALE).astype(BF)
    r.d_query[rows, pair * 128 : (pair + 1) * 128] = jnp.concatenate(
        [d_query[:TOK], d_query[TOK:]], axis=-1
    )
    d_key = dot_tn(d_scores, queries) * SCORE_SCALE
    d_value = dot_tn(chances.astype(BF).reshape(2 * TOK, keys), grads)
    if block == ROW // TOK - 1:
        r.d_kv[pair, :, :HEAD_SIZE] = d_key
        r.d_kv[pair, :, HEAD_SIZE:] = d_value
    else:
        r.d_kv[pair, :keys, :HEAD_SIZE] += d_key
        r.d_kv[pair, :keys, HEAD_SIZE:] += d_value


def norm_back_unit(upstream, values):
    inverse = lax.rsqrt(jnp.mean(values * values, axis=-1, keepdims=True) + EPS)
    unit = values * inverse
    d_values = inverse * (
        upstream - unit * jnp.mean(upstream * unit, axis=-1, keepdims=True)
    )
    return d_values, jnp.sum(upstream * unit, axis=0, keepdims=True)


def unit_norm(values):
    return values * lax.rsqrt(jnp.mean(values * values, axis=-1, keepdims=True) + EPS)


def own_parts(r):
    scale = r.attn_gain[...]
    for o in range(SEQ):
        for ref, first, size in ((r.w_query, 0, OWN_Q), (r.w_key, OWN_Q, OWN_K), (r.w_value, OWN_Q + OWN_K, OWN_K)):
            part = ref[:, o * size : (o + 1) * size].astype(F32) * scale
            r.w_qkv[o, :, first : first + size] = part.astype(BF)


def own_units(r):
    scale = r.ffn_gain[...]
    for ref, first in ((r.w_gate, 0), (r.w_up, FF_OWN)):
        scaled = ref[...].astype(F32) * scale
        for o in range(SEQ):
            parts = [scaled[:, (4 * j + o) * FF_SHARD : (4 * j + o + 1) * FF_SHARD] for j in range(8)]
            r.d_gu[32 + o, :, first : first + FF_OWN] = jnp.concatenate(parts, axis=1).astype(BF)


def rotation_tables(r, half):
    size = ROW // 2
    rows = pl.ds(half * size, size)
    place = lax.broadcasted_iota(jnp.int32, (size, 1), 0) + half * size
    begin = jnp.zeros((size, 1), jnp.int32)
    for k in range(4):
        start = r.doc_starts[0, k]
        begin = jnp.maximum(begin, jnp.where(place >= start, start, 0))
    angles = (place - begin).astype(F32) * r.frequency[...]
    r.cosine[rows, :] = jnp.cos(angles)
    r.sine[rows, :] = jnp.sin(angles)


def head_forward(r):
    first, low = lane_masks(TOK)

    @pl.loop(0, SEQ)
    def _(t):
        rows = pl.ds(pl.multiple_of(t * TOK, TOK), TOK)
        linear = dot(r.u_rows[t], r.qkv_all[...].reshape(WIDTH, QKV))
        r.q_linear[rows, :] = linear[:, :OWN_Q]
        r.k_linear[rows, :] = linear[:, OWN_Q : OWN_Q + OWN_K]
        cosine, sine = r.cosine[rows, :], r.sine[rows, :]
        for pair in range(2):
            part = linear[:, pair * 128 : (pair + 1) * 128]
            part = norm_rope(part, r.q_gain[...], cosine, sine, first, low).astype(BF)
            r.q_heads[pair, 0, rows, :] = part[:, :HEAD_SIZE]
            r.q_heads[pair, 1, rows, :] = part[:, HEAD_SIZE:]
        part = linear[:, OWN_Q : OWN_Q + OWN_K]
        part = norm_rope(part, r.k_gain[...], cosine, sine, first, low).astype(BF)
        r.k_heads[0, rows, :] = part[:, :HEAD_SIZE]
        r.k_heads[1, rows, :] = part[:, HEAD_SIZE:]
        part = linear[:, OWN_Q + OWN_K :].astype(BF)
        r.v_heads[0, rows, :] = part[:, :HEAD_SIZE]
        r.v_heads[1, rows, :] = part[:, HEAD_SIZE:]


def head_backward(r):
    first, low = lane_masks(TOK)
    r.head_gain_part[...] = jnp.zeros((2, 128), F32)

    @pl.loop(0, SEQ)
    def _(t):
        rows = pl.ds(pl.multiple_of(t * TOK, TOK), TOK)
        cosine, sine = r.cosine[rows, :], r.sine[rows, :]
        for pair in range(2):
            cols = slice(pair * 128, (pair + 1) * 128)
            up = r.d_query[rows, cols].astype(F32)
            back, gain_part = norm_rope_back(up, r.q_linear[rows, cols], r.q_gain[...], cosine, sine, first, low)
            r.d_qkv[rows, cols] = back.astype(BF)
            r.head_gain_part[0:1] += gain_part
        up = jnp.concatenate([r.d_kv[0, rows, :HEAD_SIZE], r.d_kv[1, rows, :HEAD_SIZE]], axis=-1)
        up = up.astype(BF).astype(F32)
        back, gain_part = norm_rope_back(up, r.k_linear[rows, :], r.k_gain[...], cosine, sine, first, low)
        r.d_qkv[rows, OWN_Q : OWN_Q + OWN_K] = back.astype(BF)
        r.head_gain_part[1:2] += gain_part
        up = jnp.concatenate([r.d_kv[0, rows, HEAD_SIZE:], r.d_kv[1, rows, HEAD_SIZE:]], axis=-1)
        r.d_qkv[rows, OWN_Q + OWN_K :] = up.astype(BF)


def units_up(r, t):
    gate_up = dot(r.mid_rows[t], r.gu_all[...].reshape(WIDTH, HIDDEN_TWO))
    gate, up = gate_up[:, :FF_OWN], gate_up[:, FF_OWN:]
    sigmoid = 1.0 / (1.0 + jnp.exp(-gate))
    swish = gate * sigmoid
    r.active[t] = (swish * up).astype(BF)
    blocks = pl.ds(8 * t, 8)
    by_gate = up * (sigmoid * (1.0 + gate * (1.0 - sigmoid)))
    r.d_gu[blocks, :, :FF_OWN] = by_gate.astype(BF).reshape(8, 32, FF_OWN)
    r.d_gu[blocks, :, FF_OWN:] = swish.astype(BF).reshape(8, 32, FF_OWN)


def units_down(r, t):
    d_active = dot_nt(r.cot_rows[t], r.down_all[...].reshape(FF_OWN, WIDTH)).reshape(8, 32, FF_OWN)
    blocks = pl.ds(8 * t, 8)
    r.d_gu[blocks, :, :FF_OWN] = (d_active * r.d_gu[blocks, :, :FF_OWN].astype(F32)).astype(BF)
    r.d_gu[blocks, :, FF_OWN:] = (d_active * r.d_gu[blocks, :, FF_OWN:].astype(F32)).astype(BF)
    d_gu = r.d_gu[blocks].reshape(TOK, HIDDEN_TWO)
    return dot_nt(d_gu, r.gu_all[...].reshape(WIDTH, HIDDEN_TWO))


def whole_block(r):
    l = r.links = Links(r.send_sems, r.recv_sems)
    l.greet(pltpu.get_barrier_semaphore(), l.everyone())
    x = r.inputs[...].astype(F32)
    r.u_rows[l.s] = unit_norm(x).astype(BF)
    own_parts(r)
    own_units(r)
    r.out_all[l.dp, l.s] = r.w_out[...]
    r.qkv_all[l.dp, l.s] = r.w_qkv[l.s]
    r.gu_all[l.dp, l.s] = r.d_gu[32 + l.s]
    r.down_all[l.dp] = r.w_down[...]
    r.cot_rows[l.s] = r.cotangent[...]
    pl.semaphore_wait(pltpu.get_barrier_semaphore(), len(l.everyone()))
    qkv_cols = [l.push(r.w_qkv.at[o], r.qkv_all.at[l.dp, l.s], s=o) for o in l.others]
    out = Gather(l, lambda b: r.out_all.at[b, l.s])
    qkv = Gather(l, lambda b: r.qkv_all.at[b])
    gate_up = [Gather(l, lambda b, g=g: r.gu_all.at[b, g]) for g in (l.s,) + l.others]
    down_a = Gather(l, lambda b: r.down_all.at[b, pl.ds(0, DOWN_A)])
    down_b = PairGather(l, lambda b: r.down_all.at[b, pl.ds(DOWN_A, DOWN_B)])
    out.start_z()
    out.start_y()
    gu_cols = [l.push(r.d_gu.at[32 + o], r.gu_all.at[l.dp, l.s], s=o) for o in l.others]
    u_far = l.push(r.u_rows.at[l.s], r.u_rows.at[l.s], s=l.s2)
    u_near = l.push(r.u_rows.at[l.s], r.u_rows.at[l.s], s=l.s1)
    for copy in qkv_cols:
        copy.wait_recv()
    qkv.start_z()
    qkv.start_y()
    gate_up[0].start_z()
    down_a.start_y()
    down_b.start_y()
    out.step(0)
    qkv.step(0)
    gu_cols[0].wait_recv()
    gate_up[1].start_z()
    rotation_tables(r, 0)
    out.step(1)
    qkv.step(1)
    gu_cols[1].wait_recv()
    gate_up[2].start_z()
    rotation_tables(r, 1)
    out.step(2)
    qkv.step(2)
    gu_cols[2].wait_recv()
    gate_up[3].start_z()
    for piece in gate_up:
        piece.start_y()
    u_far.wait_recv()
    u_more = l.push(r.u_rows.at[l.s2], r.u_rows.at[l.s2], s=l.s1)
    out.finish()
    out_far = l.push(r.out_all.at[:, l.s], r.out_all.at[:, l.s], s=l.s2)
    out_near = l.push(r.out_all.at[:, l.s], r.out_all.at[:, l.s], s=l.s1)
    qkv.finish()
    u_near.wait_recv()
    u_more.wait_recv()
    for piece in gate_up[:2]:
        piece.step(0)
    head_forward(r)
    for piece in gate_up[2:]:
        piece.step(0)
    attention_block(r, 0, 3)
    attention_block(r, 1, 3)
    gate_up[0].step(1)
    attention_block(r, 0, 2)
    attention_block(r, 1, 2)
    gate_up[1].step(1)
    out_far.wait_recv()
    out_more = l.push(r.out_all.at[:, l.s2], r.out_all.at[:, l.s2], s=l.s1)
    attention_block(r, 0, 1)
    attention_block(r, 1, 1)
    gate_up[2].step(1)
    attention_block(r, 0, 0)
    attention_block(r, 1, 0)
    att = [l.push(r.att_own.at[o], r.att_local.at[l.s], s=o) for o in l.others]
    cot_far = l.push(r.cot_rows.at[l.s], r.cot_rows.at[l.s], s=l.s2)
    cot_near = l.push(r.cot_rows.at[l.s], r.cot_rows.at[l.s], s=l.s1)
    r.att_local[l.s] = r.att_own[l.s]
    gate_up[3].step(1)
    down_a.start_z()
    gate_up[0].step(2)
    out_near.wait_recv()
    out_more.wait_recv()
    for copy in att:
        copy.wait_recv()
    middle = x
    for part in range(SEQ):
        rows = r.out_all[part * 2 : (part + 1) * 2].reshape(OWN_Q, WIDTH)
        middle = middle + dot(r.att_local[part], rows)
    r.middle[...] = middle
    r.mid_rows[l.s] = unit_norm(middle).astype(BF)
    mid_far = l.push(r.mid_rows.at[l.s], r.mid_rows.at[l.s], s=l.s2)
    mid_near = l.push(r.mid_rows.at[l.s], r.mid_rows.at[l.s], s=l.s1)
    for piece in gate_up[1:]:
        piece.step(2)
    down_a.step(0)
    down_b.start_z()
    cot_far.wait_recv()
    cot_more = l.push(r.cot_rows.at[l.s2], r.cot_rows.at[l.s2], s=l.s1)
    down_b.join()
    mid_far.wait_recv()
    mid_more = l.push(r.mid_rows.at[l.s2], r.mid_rows.at[l.s2], s=l.s1)
    down_a.step(1)
    down_b.step(0)
    down_a.step(2)
    mid_near.wait_recv()
    mid_more.wait_recv()
    for piece in gate_up:
        piece.finish()
    units_up(r, l.s3)
    units_up(r, l.s2)
    down_b.step(1)
    units_up(r, l.s1)
    units_up(r, l.s)
    down_b.step(2)
    cot_near.wait_recv()
    cot_more.wait_recv()
    for t in range(SEQ):
        r.flipped[:, t * TOK : (t + 1) * TOK] = r.active[t].T
    cot = r.cot_rows[...].reshape(ROW, WIDTH)

    @pl.loop(0, 4)
    def _(k):
        rows = pl.ds(pl.multiple_of(k * 288, 32), 288)
        grad = dot(r.flipped[rows, :], cot).astype(BF)
        r.down_part[pl.ds(2 * k, 2)] = grad.reshape(2, FF_SHARD, WIDTH)

    down_a.finish()
    l.drain()
    down_a_sum = Scatter(
        l, lambda b: r.down_part.at[b, pl.ds(0, SUM_A)], lambda k: r.down_a_slots.at[k], lambda k: r.down_a_slots.at[4 + k]
    )
    down_b_sum = PairScatter(
        l,
        lambda b: r.down_part.at[b, pl.ds(SUM_A, SUM_B)],
        r.down_b_slots.at[10],
        lambda k: r.down_b_slots.at[k],
        lambda k: r.down_b_slots.at[5 + k],
    )
    d_mid = RowSum(l, r.slots_a)
    home = []
    down_a_sum.start()
    down_b_sum.start()
    down_b_sum.step(0)
    r.parts[0] = units_down(r, l.s3).astype(BF).reshape(8, 32, WIDTH)
    d_mid.hand_over(r.parts.at[0])
    r.parts[1] = units_down(r, l.s2).astype(BF).reshape(8, 32, WIDTH)
    d_mid.cross(r.parts.at[1])
    down_b_sum.step(1)
    r.parts[2] = units_down(r, l.s1).astype(BF).reshape(8, 32, WIDTH)
    d_mid.near(r.parts.at[2])
    r.input_grad[...] = units_down(r, l.s)
    for t in range(SEQ):
        r.flipped[:WIDTH, t * TOK : (t + 1) * TOK] = r.mid_rows[t].T
    d_gu = r.d_gu[0:32].reshape(ROW, HIDDEN_TWO)

    @pl.loop(0, 4)
    def _(k):
        rows = pl.ds(pl.multiple_of(k * 256, 256), 256)
        grad = dot(r.flipped[rows, :], d_gu).astype(BF)
        r.gu_all[pl.ds(2 * k, 2)] = grad.reshape(2, 4, 32, HIDDEN_TWO)

    l.greet(r.free, l.column())
    pl.semaphore_wait(r.free, len(l.column()))
    gu_sums = [
        Scatter(
            l,
            lambda b, g=g: r.gu_all.at[b, g],
            lambda k, n=n: r.d_gu.at[9 * n + k],
            lambda k, n=n: r.d_gu.at[9 * n + 4 + k],
        )
        for n, g in enumerate(l.others)
    ]
    own_gu_sum = PairScatter(
        l,
        lambda b: r.gu_all.at[b, l.s],
        r.d_gu.at[37],
        lambda k: r.d_gu.at[27 + k],
        lambda k: r.d_gu.at[32 + k],
    )
    own_gu_sum.start()
    own_gu_sum.step(0)
    gu_sums[1].start()
    d_values, ffn_gain_part = norm_back_unit(d_mid.total(r.input_grad[...]), r.middle[...])
    d_middle = r.cotangent[...].astype(F32) + d_values
    r.input_grad[...] = d_middle
    d_branch = d_middle.astype(BF)
    r.gains[0, 1:2, :] = ffn_gain_part
    for part in range(SEQ):
        rows = r.out_all[part * 2 : (part + 1) * 2].reshape(OWN_Q, WIDTH)
        r.att_own[part] = dot_nt(d_branch, rows).astype(BF)
    d_att = [l.push(r.att_own.at[o], r.d_att_rows.at[l.s], s=o) for o in l.others]
    r.d_att_rows[l.s] = r.att_own[l.s]
    gu_sums[2].start()
    down_a_sum.join()
    down_a_sum.step(0)
    own_gu_sum.step(1)
    for copy in d_att:
        copy.wait_recv()
    l.settle((d_mid.first, d_mid.second, d_mid.third))
    attention_block_back(r, 0, 3)
    for part in range(SEQ):
        grad = dot_tn(r.att_local[part], d_branch).astype(BF)
        r.out_all[2 * part : 2 * part + 2] = grad.reshape(2, 4, 32, WIDTH)
    out_row = RowSum(l, r.slots_b)
    out_row.hand_over(r.out_all.at[:, l.s3])
    out_row.cross(r.out_all.at[:, l.s2])
    out_row.near(r.out_all.at[:, l.s1])
    gu_sums[0].start()
    own_gu_sum.step(2)
    attention_block_back(r, 1, 3)
    attention_block_back(r, 0, 2)
    attention_block_back(r, 1, 2)
    attention_block_back(r, 0, 1)
    attention_block_back(r, 1, 1)
    attention_block_back(r, 0, 0)
    attention_block_back(r, 1, 0)
    gu_sums[1].join()
    gu_sums[1].step(0)
    down_b_sum.step(2)
    down_a_sum.step(1)
    head_backward(r)
    out_total = out_row.total(r.out_all[:, l.s].astype(F32))
    r.out_all[:, l.s] = out_total.astype(BF)
    out_sum = Scatter(
        l, lambda b: r.out_all.at[b, l.s], lambda k: r.out_slots.at[k], lambda k: r.out_slots.at[4 + k]
    )
    d_u = RowSum(l, r.slots_a)
    weights = r.qkv_all[...].reshape(WIDTH, QKV)

    def d_u_part(t):
        return dot_nt(r.d_qkv[pl.ds(pl.multiple_of(t * TOK, TOK), TOK), :], weights)

    r.parts[0] = d_u_part(l.s3).astype(BF).reshape(8, 32, WIDTH)
    d_u.hand_over(r.parts.at[0])
    r.parts[1] = d_u_part(l.s2).astype(BF).reshape(8, 32, WIDTH)
    d_u.cross(r.parts.at[1])
    r.parts[2] = d_u_part(l.s1).astype(BF).reshape(8, 32, WIDTH)
    d_u.near(r.parts.at[2])
    own = d_u_part(l.s)
    down_b_sum.cross()
    gu_sums[1].step(1)
    down_a_sum.step(2)
    for t in range(SEQ):
        r.flipped[:WIDTH, t * TOK : (t + 1) * TOK] = r.u_rows[t].T
    grad = dot(r.flipped[:WIDTH, :], r.d_qkv[...]).astype(BF)
    r.qkv_all[...] = grad.reshape(8, 4, 32, QKV)
    qkv_sum = Scatter(l, lambda b: r.qkv_all.at[b], lambda k: r.qkv_slots.at[k], lambda k: r.qkv_slots.at[4 + k])
    gu_sums[2].join()
    gu_sums[2].step(0)
    qkv_sum.start()
    out_sum.start()
    gu_sums[1].step(2)
    gu_sums[0].join()
    gu_sums[0].step(0)
    r.gu_all[l.dp, l.s2] = gu_sums[1].total().astype(BF)
    home.append(l.push(r.gu_all.at[l.dp, l.s2], r.gu_grad.at[l.s], s=l.s2))
    gu_sums[2].step(1)
    own_gu_sum.cross()
    x = r.inputs[...].astype(F32)
    d_values, attn_gain_part = norm_back_unit(d_u.total(own), x)
    r.input_grad[...] += d_values
    r.gains[0, 0:1, :] = attn_gain_part
    r.gains[0, 2:3, 0:128] = r.head_gain_part[0:1]
    r.gains[0, 2:3, 128:256] = r.head_gain_part[1:2]
    r.gains[0, 2:3, 256:] = jnp.zeros((1, WIDTH - 256), F32)
    r.gains[0, 3:8, :] = jnp.zeros((5, WIDTH), F32)
    gains = [l.push(r.gains.at[0], r.gain_slots.at[k], s=o) for k, o in enumerate(l.others)]
    l.settle((d_u.first, d_u.second, d_u.third))
    down_all = r.down_all[...].reshape(FF_OWN, WIDTH)
    last = RowSum(l, r.slots_b)
    r.parts[0] = dot(r.active[l.s3], down_all).astype(BF).reshape(8, 32, WIDTH)
    last.hand_over(r.parts.at[0])
    r.parts[1] = dot(r.active[l.s2], down_all).astype(BF).reshape(8, 32, WIDTH)
    last.cross(r.parts.at[1])
    gu_sums[2].step(2)
    gu_sums[0].step(1)
    r.parts[2] = dot(r.active[l.s1], down_all).astype(BF).reshape(8, 32, WIDTH)
    last.near(r.parts.at[2])
    own = r.middle[...] + dot(r.active[l.s], down_all)
    for copy in gains:
        copy.wait_recv()
    r.gains[1] = r.gains[0] + r.gain_slots[0] + r.gain_slots[1] + r.gain_slots[2]
    gains_y = l.push(r.gains.at[1], r.gain_slots.at[3], dp=l.y_peer)
    gu_sums[0].step(2)
    qkv_sum.join()
    qkv_sum.step(0)
    r.gu_all[l.dp, l.s3] = gu_sums[2].total().astype(BF)
    home.append(l.push(r.gu_all.at[l.dp, l.s3], r.gu_grad.at[l.s], s=l.s3))
    r.down_grad[SUM_A:] = down_b_sum.total()
    qkv_sum.step(1)
    r.gu_all[l.dp, l.s1] = gu_sums[0].total().astype(BF)
    home.append(l.push(r.gu_all.at[l.dp, l.s1], r.gu_grad.at[l.s], s=l.s1))
    out_sum.join()
    out_sum.step(0)
    qkv_sum.step(2)
    r.down_grad[0:SUM_A] = down_a_sum.total()
    r.output[...] = last.total(own).astype(BF)
    gains_y.wait_recv()
    r.gains[2] = r.gains[1] + r.gain_slots[3]
    gains_z = [l.push(r.gains.at[2], r.gain_slots.at[4 + k], dp=p) for k, p in enumerate(l.z_peers)]
    out_sum.step(1)
    r.gu_grad[l.s] = own_gu_sum.total().astype(BF)
    r.qkv_all[l.dp] = qkv_sum.total().astype(BF)
    home += [l.push(r.qkv_all.at[l.dp, o], r.qkv_grad.at[l.s], s=o) for o in l.others]
    r.qkv_grad[l.s] = r.qkv_all[l.dp, l.s]
    out_sum.step(2)
    r.out_grad[...] = out_sum.total()
    for copy in gains_z + home:
        copy.wait_recv()
    r.gain_grads[...] = r.gains[2] + r.gain_slots[4] + r.gain_slots[5] + r.gain_slots[6]
    l.drain()


def own_lanes(row, size):
    place = (lax.axis_index("dp") * SEQ + lax.axis_index("seq")) * size
    return pltpu.roll(row, lax.rem(WIDTH - place, WIDTH), 1)[:, :size]


def column(row):
    n = row.shape[1]
    same = lax.broadcasted_iota(jnp.int32, (n, n), 0) == lax.broadcasted_iota(jnp.int32, (n, n), 1)
    return jnp.sum(jnp.where(same, row, 0.0), axis=1, keepdims=True)


def lay_out(
    output, input_grad, down_grad, out_grad, gu_grad, qkv_grad, gains, attn_gain, ffn_gain,
    output_o, input_o, attn_o, query_o, key_o, value_o, q_gain_o, k_gain_o, out_o, ffn_o, gate_o, up_o, down_o, sems,
):
    pairs = ((output, output_o), (input_grad, input_o), (down_grad, down_o), (out_grad, out_o))
    copies = [pltpu.make_async_copy(src, dst, sems.at[n]) for n, (src, dst) in enumerate(pairs)]
    for copy in copies:
        copy.start()
    scale = attn_gain[...]
    for o in range(SEQ):
        for ref, first, size in ((query_o, 0, OWN_Q), (key_o, OWN_Q, OWN_K), (value_o, OWN_Q + OWN_K, OWN_K)):
            ref[:, o * size : (o + 1) * size] = qkv_grad[o, :, first : first + size].astype(F32) * scale
    scale = ffn_gain[...]
    for ref, first in ((gate_o, 0), (up_o, FF_OWN)):
        parts = []
        for j in range(8):
            for o in range(SEQ):
                part = gu_grad[o, :, first + j * FF_SHARD : first + (j + 1) * FF_SHARD]
                parts.append(part.astype(F32) * scale)
        ref[...] = jnp.concatenate(parts, axis=1)
    size = attn_o.shape[0]
    attn_o[...] = (column(own_lanes(gains[0:1, :], size)) / attn_gain[...]).reshape(size)
    ffn_o[...] = (column(own_lanes(gains[1:2, :], size)) / ffn_gain[...]).reshape(size)
    q_gain_o[...] = (gains[2:3, 0:64] + gains[2:3, 64:128]).reshape(HEAD_SIZE)
    k_gain_o[...] = (gains[2:3, 128:192] + gains[2:3, 192:256]).reshape(HEAD_SIZE)
    for copy in copies:
        copy.wait()


class Names:
    pass


def frequencies():
    steps = np.arange(HEAD_SIZE // 2, dtype=np.float64) * (2.0 / HEAD_SIZE)
    return jnp.asarray(np.tile(THETA ** (-steps), 4)[None], F32)


MAX_COPIES = 300
VMEM_BYTES = 63 * 2**20


def on_device_in_kernels(
    inputs,
    doc_starts,
    cotangent,
    attn_gain,
    w_query,
    key_projection_weight,
    value_projection_weight,
    q_gain,
    k_gain,
    w_out,
    ffn_gain,
    w_gate,
    w_up,
    w_down,
):
    given = dict(
        inputs=inputs,
        cotangent=cotangent,
        attn_gain=attn_gain.astype(F32)[:, None],
        ffn_gain=ffn_gain.astype(F32)[:, None],
        q_gain=jnp.tile(q_gain.astype(F32), 2)[None],
        k_gain=jnp.tile(k_gain.astype(F32), 2)[None],
        w_query=w_query,
        w_key=key_projection_weight,
        w_value=value_projection_weight,
        w_out=w_out,
        w_gate=w_gate,
        w_up=w_up,
        w_down=w_down,
        frequency=frequencies(),
        doc_starts=doc_starts,
    )
    results = dict(
        output=((TOK, WIDTH), BF),
        input_grad=((TOK, WIDTH), F32),
        down_grad=((FF_SHARD, WIDTH), F32),
        out_grad=((32, WIDTH), F32),
        gu_grad=((SEQ, 32, HIDDEN_TWO), BF),
        qkv_grad=((SEQ, 32, QKV), BF),
        gain_grads=((8, WIDTH), F32),
    )
    kept = dict(
        w_qkv=((SEQ, 32, QKV), BF),
        cosine=((ROW, 128), F32),
        sine=((ROW, 128), F32),
        u_rows=((SEQ, TOK, WIDTH), BF),
        cot_rows=((SEQ, TOK, WIDTH), BF),
        mid_rows=((SEQ, TOK, WIDTH), BF),
        qkv_all=((8, 4, 32, QKV), BF),
        gu_all=((8, 4, 32, HIDDEN_TWO), BF),
        down_all=((8, FF_SHARD, WIDTH), BF),
        out_all=((8, 4, 32, WIDTH), BF),
        q_linear=((ROW, OWN_Q), F32),
        k_linear=((ROW, OWN_K), F32),
        q_heads=((2, 2, ROW, HEAD_SIZE), BF),
        k_heads=((2, ROW, HEAD_SIZE), BF),
        v_heads=((2, ROW, HEAD_SIZE), BF),
        log_total=((ROW, 128), F32),
        att_own=((SEQ, TOK, OWN_Q), BF),
        att_local=((SEQ, TOK, OWN_Q), BF),
        middle=((TOK, WIDTH), F32),
        active=((SEQ, TOK, FF_OWN), BF),
        d_gu=((38, 32, HIDDEN_TWO), BF),
        parts=((3, 8, 32, WIDTH), BF),
        slots_a=((3, 8, 32, WIDTH), BF),
        slots_b=((3, 8, 32, WIDTH), BF),
        d_att_rows=((SEQ, TOK, OWN_Q), BF),
        flipped=((FF_OWN, ROW), BF),
        down_part=((8, FF_SHARD, WIDTH), BF),
        down_a_slots=((9, SUM_A, WIDTH), BF),
        down_b_slots=((11, SUM_B, WIDTH), BF),
        out_slots=((9, 32, WIDTH), BF),
        qkv_slots=((9, 4, 32, QKV), BF),
        d_query=((ROW, OWN_Q), BF),
        d_kv=((2, ROW, 128), F32),
        d_qkv=((ROW, QKV), BF),
        head_gain_part=((2, 128), F32),
        gains=((3, 8, WIDTH), F32),
        gain_slots=((7, 8, WIDTH), F32),
    )

    def body(*refs):
        r = Names()
        names = [*given, *results, *kept]
        for name, ref in zip(names, refs):
            setattr(r, name, ref)
        r.send_sems, r.recv_sems, r.free = refs[len(names) :]
        whole_block(r)

    done = pl.pallas_call(
        body,
        out_shape=[jax.ShapeDtypeStruct(*result) for result in results.values()],
        in_specs=[
            pl.BlockSpec(memory_space=pltpu.SMEM if a is doc_starts else pltpu.VMEM) for a in given.values()
        ],
        out_specs=[pl.BlockSpec(memory_space=pltpu.VMEM)] * len(results),
        scratch_shapes=[pltpu.VMEM(*shape) for shape in kept.values()]
        + [
            pltpu.SemaphoreType.DMA((MAX_COPIES,)),
            pltpu.SemaphoreType.DMA((MAX_COPIES,)),
            pltpu.SemaphoreType.REGULAR,
        ],
        compiler_params=pltpu.CompilerParams(
            collective_id=0, has_side_effects=True, vmem_limit_bytes=VMEM_BYTES
        ),
        cost_estimate=pl.CostEstimate(flops=30_000_000_000, bytes_accessed=10_000_000, transcendentals=0),
    )(*given.values())
    rows = w_query.shape[0]
    shapes = [
        ((TOK, WIDTH), BF),
        ((TOK, WIDTH), F32),
        ((rows,), F32),
        ((rows, SEQ * OWN_Q), F32),
        ((rows, SEQ * OWN_K), F32),
        ((rows, SEQ * OWN_K), F32),
        ((HEAD_SIZE,), F32),
        ((HEAD_SIZE,), F32),
        ((rows, WIDTH), F32),
        ((rows,), F32),
        ((rows, FF), F32),
        ((rows, FF), F32),
        ((FF_SHARD, WIDTH), F32),
    ]
    return tuple(
        pl.pallas_call(
            lay_out,
            out_shape=[jax.ShapeDtypeStruct(*shape) for shape in shapes],
            in_specs=[pl.BlockSpec(memory_space=pl.ANY)] * 4 + [pl.BlockSpec(memory_space=pltpu.VMEM)] * 5,
            out_specs=[
                pl.BlockSpec(memory_space=pl.ANY if n in (0, 1, 8, 12) else pltpu.VMEM) for n in range(13)
            ],
            scratch_shapes=[pltpu.SemaphoreType.DMA((4,))],
            compiler_params=pltpu.CompilerParams(vmem_limit_bytes=24 * 2**20),
            cost_estimate=pl.CostEstimate(flops=1_000_000, bytes_accessed=10_000_000, transcendentals=0),
        )(*done, given["attn_gain"], given["ffn_gain"])
    )


def solution(mesh):
    in_kernels = (mesh.shape["dp"], mesh.shape["seq"]) == (8, 4)
    placed = (
        P(("dp", "seq"), None),
        P("dp", None),
        P(("dp", "seq"), None),
        P(("dp", "seq")),
        P(("dp", "seq"), None),
        P(("dp", "seq"), None),
        P(("dp", "seq"), None),
        P(),
        P(),
        P(("dp", "seq"), None),
        P(("dp", "seq")),
        P(("dp", "seq"), None),
        P(("dp", "seq"), None),
        P(("dp", "seq"), None),
    )
    return jax.shard_map(
        on_device_in_kernels if in_kernels else on_device,
        mesh=mesh,
        in_specs=placed,
        out_specs=(
            P(("dp", "seq"), None),
            P(("dp", "seq"), None),
            P(("dp", "seq")),
            P(("dp", "seq"), None),
            P(("dp", "seq"), None),
            P(("dp", "seq"), None),
            P(),
            P(),
            P(("dp", "seq"), None),
            P(("dp", "seq")),
            P(("dp", "seq"), None),
            P(("dp", "seq"), None),
            P(("dp", "seq"), None),
        ),
        check_vma=False,
    )
```

```python
import jax
import jax.numpy as jnp
import numpy as np
from jax import lax
from jax.experimental import pallas as pl
from jax.experimental.pallas import tpu as pltpu
from jax.sharding import PartitionSpec as P

QUERY_HEADS = 16
KEY_VALUE_HEADS = 8
HEAD_SIZE = 64
FF = 4608


EPS = 1e-05
THETA = 1000000.0
MASKED = -1e30
CONTRACT_ROWS = (((0,), (0,)), ((), ()))
CONTRACT_COLS = (((1,), (1,)), ((), ()))


def rms_norm(values, gain_vec):
    return values * lax.rsqrt(jnp.mean(values * values, axis=-1, keepdims=True) + EPS) * gain_vec


def rotate_half(values):
    half_len = values.shape[-1] // 2
    return jnp.concatenate([-values[..., half_len:], values[..., :half_len]], axis=-1)


def unrotate_half(values):
    half_len = values.shape[-1] // 2
    return jnp.concatenate([values[..., half_len:], -values[..., :half_len]], axis=-1)


def row_layout(row_starts, places):
    inside = places[:, None] >= row_starts[None, :]
    doc_ids = jnp.sum(inside.astype(jnp.int32), axis=1) - 1
    begins = jnp.max(jnp.where(inside, row_starts[None, :], 0), axis=1)
    offsets = (places - begins).astype(jnp.float32)
    freq_steps = jnp.arange(HEAD_SIZE // 2, dtype=jnp.float32) * (2.0 / HEAD_SIZE)
    frequency = THETA ** (-freq_steps)
    angles = offsets[:, None] * frequency[None, :]
    angles = jnp.concatenate([angles, angles], axis=-1)
    return (doc_ids, jnp.cos(angles), jnp.sin(angles))


def norm_back(upstream, values, gain_vec):
    inverse = lax.rsqrt(jnp.mean(values * values, axis=-1, keepdims=True) + EPS)
    unit_vec = values * inverse
    gain_part = jnp.sum(upstream * unit_vec, axis=tuple(range(values.ndim - 1)))
    scaled = upstream * gain_vec
    return (
        inverse * (scaled - unit_vec * jnp.mean(scaled * unit_vec, axis=-1, keepdims=True)),
        gain_part,
    )


def head_forward_pass(linear, gain_vec, cosine_table, sine_table, heads):
    local_rows = linear.shape[0]
    shaped = rms_norm(linear.reshape(local_rows, heads, HEAD_SIZE), gain_vec)
    turned = shaped * cosine_table + rotate_half(shaped) * sine_table
    return turned.astype(jnp.bfloat16).reshape(local_rows, heads * HEAD_SIZE)


def head_backward_pass(grad_in, linear, gain_vec, cosine_table, sine_table, heads):
    local_rows = linear.shape[0]
    shaped = linear.reshape(local_rows, heads, HEAD_SIZE)
    upstream = grad_in.astype(jnp.float32).reshape(local_rows, heads, HEAD_SIZE)
    d_normed = upstream * cosine_table + unrotate_half(upstream * sine_table)
    d_linear, gain_part = norm_back(d_normed, shaped, gain_vec)
    return (d_linear.reshape(local_rows, heads * HEAD_SIZE).astype(jnp.bfloat16), gain_part)


def block_scores(q_block, keys_all, block_places, block_docs, places, doc_ids):
    score_scale = HEAD_SIZE ** (-0.5)
    scores = (
        jnp.einsum("qkgd,skd->kgqs", q_block, keys_all, preferred_element_type=jnp.float32)
        * score_scale
    )
    allowed = (places[None, :] <= block_places[:, None]) & (doc_ids[None, :] == block_docs[:, None])
    return jnp.where(allowed[None, None], scores, MASKED)


def attend_forward(query_rows, keys_in, values_in, places, doc_ids):
    total_length = query_rows.shape[0]
    kv_heads = keys_in.shape[1] // HEAD_SIZE
    query_group = QUERY_HEADS // KEY_VALUE_HEADS
    block_length = min(512, total_length)
    number_of_blocks = total_length // block_length
    keys_all = keys_in.reshape(total_length, kv_heads, HEAD_SIZE)
    values_all = values_in.reshape(total_length, kv_heads, HEAD_SIZE)
    grouped_queries = query_rows.reshape(
        number_of_blocks, block_length, kv_heads, query_group, HEAD_SIZE
    )

    def one_block(pieces):
        q_block, block_places, block_docs = pieces
        scores = block_scores(q_block, keys_all, block_places, block_docs, places, doc_ids)
        row_max = jnp.max(scores, axis=-1, keepdims=True)
        weights = jnp.exp(scores - row_max)
        sum_total = jnp.sum(weights, axis=-1, keepdims=True)
        soft_max = (weights / sum_total).astype(jnp.bfloat16)
        mixture = jnp.einsum(
            "kgqs,skd->qkgd", soft_max, values_all, preferred_element_type=jnp.float32
        )
        return (mixture.astype(jnp.bfloat16), row_max[..., 0] + jnp.log(sum_total[..., 0]))

    mixture, log_total = lax.map(
        one_block,
        (
            grouped_queries,
            places.reshape(number_of_blocks, block_length),
            doc_ids.reshape(number_of_blocks, block_length),
        ),
    )
    return (mixture.reshape(total_length, kv_heads * query_group * HEAD_SIZE), log_total)


def attend_back(query_rows, keys_in, values_in, grad_out, log_total, places, doc_ids):
    total_length = query_rows.shape[0]
    kv_heads = keys_in.shape[1] // HEAD_SIZE
    query_group = QUERY_HEADS // KEY_VALUE_HEADS
    block_length = min(512, total_length)
    number_of_blocks = total_length // block_length
    score_scale = HEAD_SIZE ** (-0.5)
    keys_all = keys_in.reshape(total_length, kv_heads, HEAD_SIZE)
    values_all = values_in.reshape(total_length, kv_heads, HEAD_SIZE)
    grouped_queries = query_rows.reshape(
        number_of_blocks, block_length, kv_heads, query_group, HEAD_SIZE
    )
    grads_all = grad_out.reshape(number_of_blocks, block_length, kv_heads, query_group, HEAD_SIZE)

    def one_block(carried, pieces):
        key_total, value_total = carried
        q_block, g_block, block_log, block_places, block_docs = pieces
        scores = block_scores(q_block, keys_all, block_places, block_docs, places, doc_ids)
        chances = jnp.exp(scores - block_log[..., None])
        d_chances = jnp.einsum(
            "qkgd,skd->kgqs", g_block, values_all, preferred_element_type=jnp.float32
        )
        row_dots = jnp.sum(d_chances * chances, axis=-1, keepdims=True)
        d_scores = (chances * (d_chances - row_dots)).astype(jnp.bfloat16)
        d_query = (
            jnp.einsum("kgqs,skd->qkgd", d_scores, keys_all, preferred_element_type=jnp.float32)
            * score_scale
        )
        key_total = (
            key_total
            + jnp.einsum("kgqs,qkgd->skd", d_scores, q_block, preferred_element_type=jnp.float32)
            * score_scale
        )
        value_total = value_total + jnp.einsum(
            "kgqs,qkgd->skd",
            chances.astype(jnp.bfloat16),
            g_block,
            preferred_element_type=jnp.float32,
        )
        return ((key_total, value_total), d_query)

    zero_kv = jnp.zeros((total_length, kv_heads, HEAD_SIZE), jnp.float32)
    inputs_scan = (
        grouped_queries,
        grads_all,
        log_total,
        places.reshape(number_of_blocks, block_length),
        doc_ids.reshape(number_of_blocks, block_length),
    )
    (key_total, value_total), d_query = lax.scan(one_block, (zero_kv, zero_kv), inputs_scan)
    return (
        d_query.reshape(total_length, kv_heads * query_group * HEAD_SIZE).astype(jnp.bfloat16),
        key_total.reshape(total_length, kv_heads * HEAD_SIZE).astype(jnp.bfloat16),
        value_total.reshape(total_length, kv_heads * HEAD_SIZE).astype(jnp.bfloat16),
    )


def on_device(
    inputs,
    doc_starts,
    cotangent,
    attn_gain,
    w_query,
    key_projection_weight,
    value_projection_weight,
    q_gain,
    k_gain,
    w_out,
    ffn_gain,
    w_gate,
    w_up,
    w_down,
):
    local_rows = inputs.shape[0]
    seq_parts = lax.axis_size("seq")
    total_length = local_rows * seq_parts
    row_starts = doc_starts[0]
    local_places = lax.axis_index("seq") * local_rows + jnp.arange(local_rows, dtype=jnp.int32)
    unused_docs, cosine_table, sine_table = row_layout(row_starts, local_places)
    cosine_table = cosine_table[:, None, :]
    sine_table = sine_table[:, None, :]
    all_places = jnp.arange(total_length, dtype=jnp.int32)
    all_docs = jnp.sum((all_places[:, None] >= row_starts[None, :]).astype(jnp.int32), axis=1) - 1
    q_scale = q_gain.astype(jnp.float32)
    key_norm_scale = k_gain.astype(jnp.float32)
    attn_scale, query_full, key_full, value_full, out_full = (
        lax.all_gather(attn_gain, ("dp", "seq"), axis=0, tiled=True),
        lax.all_gather(w_query, ("dp", "seq"), axis=0, tiled=True),
        lax.all_gather(key_projection_weight, ("dp", "seq"), axis=0, tiled=True),
        lax.all_gather(value_projection_weight, ("dp", "seq"), axis=0, tiled=True),
        lax.all_gather(w_out, ("dp", "seq"), axis=0, tiled=True),
    )
    source = inputs.astype(jnp.float32)
    normalized_input = rms_norm(source, attn_scale.astype(jnp.float32)).astype(jnp.bfloat16)
    q_linear = jnp.dot(normalized_input, query_full, preferred_element_type=jnp.float32)
    key_linear_output = jnp.dot(normalized_input, key_full, preferred_element_type=jnp.float32)
    q_sent = head_forward_pass(q_linear, q_scale, cosine_table, sine_table, QUERY_HEADS)
    key_sent_rows = head_forward_pass(
        key_linear_output, key_norm_scale, cosine_table, sine_table, KEY_VALUE_HEADS
    )
    v_sent = jnp.dot(normalized_input, value_full, preferred_element_type=jnp.float32).astype(
        jnp.bfloat16
    )
    q_heads, k_heads, v_heads = (
        lax.all_to_all(q_sent, "seq", split_axis=1, concat_axis=0, tiled=True),
        lax.all_to_all(key_sent_rows, "seq", split_axis=1, concat_axis=0, tiled=True),
        lax.all_to_all(v_sent, "seq", split_axis=1, concat_axis=0, tiled=True),
    )
    mixture, log_total = attend_forward(q_heads, k_heads, v_heads, all_places, all_docs)
    attended = lax.all_to_all(mixture, "seq", split_axis=0, concat_axis=1, tiled=True)
    middle = source + jnp.dot(attended, out_full, preferred_element_type=jnp.float32)
    ffn_scale, gate_full, up_full, down_full = (
        lax.all_gather(ffn_gain, ("dp", "seq"), axis=0, tiled=True),
        lax.all_gather(w_gate, ("dp", "seq"), axis=0, tiled=True),
        lax.all_gather(w_up, ("dp", "seq"), axis=0, tiled=True),
        lax.all_gather(w_down, ("dp", "seq"), axis=0, tiled=True),
    )
    normed_mid = rms_norm(middle, ffn_scale.astype(jnp.float32)).astype(jnp.bfloat16)
    gate_lin = jnp.dot(normed_mid, gate_full, preferred_element_type=jnp.float32)
    upward = jnp.dot(normed_mid, up_full, preferred_element_type=jnp.float32)
    sigmoid_gate = jax.nn.sigmoid(gate_lin)
    swish = gate_lin * sigmoid_gate
    active = (swish * upward).astype(jnp.bfloat16)
    output = (middle + jnp.dot(active, down_full, preferred_element_type=jnp.float32)).astype(
        jnp.bfloat16
    )
    ffn_scale, gate_full, up_full, down_full = (
        lax.all_gather(ffn_gain, ("dp", "seq"), axis=0, tiled=True),
        lax.all_gather(w_gate, ("dp", "seq"), axis=0, tiled=True),
        lax.all_gather(w_up, ("dp", "seq"), axis=0, tiled=True),
        lax.all_gather(w_down, ("dp", "seq"), axis=0, tiled=True),
    )
    d_active = lax.dot_general(
        cotangent, down_full, CONTRACT_COLS, preferred_element_type=jnp.float32
    )
    d_gate = (d_active * upward * (sigmoid_gate * (1.0 + gate_lin * (1.0 - sigmoid_gate)))).astype(
        jnp.bfloat16
    )
    d_up = (d_active * swish).astype(jnp.bfloat16)
    d_normed_mid = lax.dot_general(
        d_gate, gate_full, CONTRACT_COLS, preferred_element_type=jnp.float32
    )
    d_normed_mid = d_normed_mid + lax.dot_general(
        d_up, up_full, CONTRACT_COLS, preferred_element_type=jnp.float32
    )
    d_middle_norm, ffn_gain_part = norm_back(d_normed_mid, middle, ffn_scale.astype(jnp.float32))
    d_middle = cotangent.astype(jnp.float32) + d_middle_norm
    d_branch = d_middle.astype(jnp.bfloat16)
    attn_scale, query_full, key_full, value_full, out_full = (
        lax.all_gather(attn_gain, ("dp", "seq"), axis=0, tiled=True),
        lax.all_gather(w_query, ("dp", "seq"), axis=0, tiled=True),
        lax.all_gather(key_projection_weight, ("dp", "seq"), axis=0, tiled=True),
        lax.all_gather(value_projection_weight, ("dp", "seq"), axis=0, tiled=True),
        lax.all_gather(w_out, ("dp", "seq"), axis=0, tiled=True),
    )
    d_attended = lax.dot_general(
        d_branch, out_full, CONTRACT_COLS, preferred_element_type=jnp.float32
    ).astype(jnp.bfloat16)
    d_mixture = lax.all_to_all(d_attended, "seq", split_axis=1, concat_axis=0, tiled=True)
    d_q_heads, d_k_heads, d_v_heads = attend_back(
        q_heads, k_heads, v_heads, d_mixture, log_total, all_places, all_docs
    )
    d_q_sent, key_sent_gradient, d_v_sent = (
        lax.all_to_all(d_q_heads, "seq", split_axis=0, concat_axis=1, tiled=True),
        lax.all_to_all(d_k_heads, "seq", split_axis=0, concat_axis=1, tiled=True),
        lax.all_to_all(d_v_heads, "seq", split_axis=0, concat_axis=1, tiled=True),
    )
    d_q_linear, q_gain_part = head_backward_pass(
        d_q_sent, q_linear, q_scale, cosine_table, sine_table, QUERY_HEADS
    )
    key_linear_gradient, key_gain_piece = head_backward_pass(
        key_sent_gradient,
        key_linear_output,
        key_norm_scale,
        cosine_table,
        sine_table,
        KEY_VALUE_HEADS,
    )
    d_normed = lax.dot_general(
        d_q_linear, query_full, CONTRACT_COLS, preferred_element_type=jnp.float32
    )
    d_normed = d_normed + lax.dot_general(
        key_linear_gradient, key_full, CONTRACT_COLS, preferred_element_type=jnp.float32
    )
    d_normed = d_normed + lax.dot_general(
        d_v_sent, value_full, CONTRACT_COLS, preferred_element_type=jnp.float32
    )
    d_source_norm, attn_gain_part = norm_back(d_normed, source, attn_scale.astype(jnp.float32))
    input_grad = d_middle + d_source_norm
    attn_columns = jnp.concatenate([d_q_linear, key_linear_gradient, d_v_sent], axis=1)
    ffn_columns = jnp.concatenate([d_gate, d_up], axis=1)
    left = normalized_input
    first_part = lax.dot_general(
        left, attn_columns, CONTRACT_ROWS, preferred_element_type=jnp.float32
    )
    second_part = lax.dot_general(
        normed_mid, ffn_columns, CONTRACT_ROWS, preferred_element_type=jnp.float32
    )
    width_sums = lax.psum_scatter(
        jnp.concatenate([first_part, second_part], axis=1),
        ("dp", "seq"),
        scatter_dimension=0,
        tiled=True,
    )
    left = attended
    out_grad = lax.psum_scatter(
        lax.dot_general(left, d_branch, CONTRACT_ROWS, preferred_element_type=jnp.float32),
        ("dp", "seq"),
        scatter_dimension=0,
        tiled=True,
    )
    left = active
    down_grad = lax.psum_scatter(
        lax.dot_general(left, cotangent, CONTRACT_ROWS, preferred_element_type=jnp.float32),
        ("dp", "seq"),
        scatter_dimension=0,
        tiled=True,
    )
    attn_gain_grad, ffn_gain_grad = (
        lax.psum_scatter(attn_gain_part, ("dp", "seq"), scatter_dimension=0, tiled=True),
        lax.psum_scatter(ffn_gain_part, ("dp", "seq"), scatter_dimension=0, tiled=True),
    )
    q_gain_grad, k_gain_grad = lax.psum((q_gain_part, key_gain_piece), ("dp", "seq"))
    q_cols = QUERY_HEADS * HEAD_SIZE
    kv_cols = KEY_VALUE_HEADS * HEAD_SIZE
    query_grad = width_sums[:, :q_cols]
    key_grad = width_sums[:, q_cols : q_cols + kv_cols]
    value_grad = width_sums[:, q_cols + kv_cols : q_cols + 2 * kv_cols]
    gate_grad = width_sums[:, q_cols + 2 * kv_cols : q_cols + 2 * kv_cols + FF]
    up_grad = width_sums[:, q_cols + 2 * kv_cols + FF :]
    return (
        output,
        input_grad,
        attn_gain_grad,
        query_grad,
        key_grad,
        value_grad,
        q_gain_grad,
        k_gain_grad,
        out_grad,
        ffn_gain_grad,
        gate_grad,
        up_grad,
        down_grad,
    )


BF = jnp.bfloat16
F32 = jnp.float32
MESH = pl.DeviceIdType.MESH
SEQ = 4
PLANES = 4
TOK = 256
WIDTH = 1024
ROW = 1024
OWN_Q = 256
OWN_K = 128
QKV = 512
FF_OWN = 1152
FF_SHARD = 144
HIDDEN_TWO = 2304
DOWN_A = 80
DOWN_B = 64
SUM_A = 80
SUM_B = 64


def flip(value, bit):
    return value + bit - 2 * bit * lax.rem(lax.div(value, bit), 2)


def dot(left, right):
    return lax.dot_general(left, right, (((1,), (0,)), ((), ())), preferred_element_type=F32)


def dot_nt(left, right):
    return lax.dot_general(left, right, (((1,), (1,)), ((), ())), preferred_element_type=F32)


def dot_tn(left, right):
    return lax.dot_general(left, right, (((0,), (0,)), ((), ())), preferred_element_type=F32)


class Links:
    def __init__(self, send_sems, recv_sems):
        self.send_sems, self.recv_sems = send_sems, recv_sems
        self.used = 0
        self.open = []
        self.late = []
        self.dp = lax.axis_index("dp")
        self.s = lax.axis_index("seq")
        self.s1 = flip(self.s, 1)
        self.s2 = flip(self.s, 2)
        self.s3 = flip(self.s1, 2)
        self.others = (self.s1, self.s2, self.s3)
        self.y = lax.rem(self.dp, 2)
        self.z = lax.div(self.dp, 2)
        self.y_peer = flip(self.dp, 1)
        z1 = flip(self.z, 1)
        self.planes = (z1, flip(self.z, 2), flip(z1, 2))
        self.z_peers = tuple(2 * z + self.y for z in self.planes)

    def greet(self, semaphore, partners):
        for place in partners:
            pl.semaphore_signal(semaphore, inc=1, device_id=place, device_id_type=MESH)

    def column(self):
        return [(p, self.s) for p in (self.y_peer,) + self.z_peers]

    def everyone(self):
        return [(self.dp, s) for s in self.others] + self.column()

    def plan(self, src, dst, dp=None, s=None):
        n = self.used
        self.used += 1
        copy = pltpu.make_async_remote_copy(
            src_ref=src,
            dst_ref=dst,
            send_sem=self.send_sems.at[n],
            recv_sem=self.recv_sems.at[n],
            device_id=(self.dp if dp is None else dp, self.s if s is None else s),
            device_id_type=MESH,
        )
        return copy

    def push(self, src, dst, dp=None, s=None, when=None, late=False):
        copy = self.plan(src, dst, dp, s)
        if when is None:
            copy.start()
        else:
            pl.when(when)(copy.start)
        (self.late if late else self.open).append((copy, when))
        return copy

    def settle(self, copies):
        for copy in copies:
            copy.wait_send()
        self.open = [item for item in self.open if all(item[0] is not copy for copy in copies)]

    def drain_late(self):
        self.open, self.late = self.late, []
        self.drain()

    def drain(self):
        for copy, when in self.open:
            if when is None:
                copy.wait_send()
            else:
                pl.when(when)(copy.wait_send)
        self.open = []


class Line:
    def __init__(self, links, view):
        self.links, self.view = links, view
        self.hops = []

    def pass_on(self, step):
        l = self.links
        below, above = l.z - step, l.z + step
        low = self.view(jnp.maximum(below, 0))
        high = self.view(jnp.minimum(above, PLANES - 1))
        up = l.push(
            low, low, dp=jnp.minimum(l.dp + 2, 2 * PLANES - 1), when=(below >= 0) & (l.z < PLANES - 1)
        )
        down = l.push(high, high, dp=jnp.maximum(l.dp - 2, 0), when=(above <= PLANES - 1) & (l.z > 0))
        self.hops.append((up, down))

    def start(self):
        self.pass_on(0)

    def step(self, k):
        l = self.links
        below, above = l.z - 1 - k, l.z + 1 + k
        from_below, from_above = below >= 0, above <= PLANES - 1
        pl.when(from_below)(self.hops[k][0].wait_recv)
        pl.when(from_above)(self.hops[k][1].wait_recv)
        if k < PLANES - 2:
            self.pass_on(k + 1)
        return [
            (from_below, self.view(jnp.maximum(below, 0))),
            (from_above, self.view(jnp.minimum(above, PLANES - 1))),
        ]


class Gather:
    def __init__(self, links, view):
        self.links = links
        self.line = Line(links, lambda z: view(2 * z + links.y))
        self.own = view(links.dp)
        self.over_y = []

    def start_y(self):
        self.over_y.append((None, self.links.push(self.own, self.own, dp=self.links.y_peer)))

    def start_z(self):
        self.line.start()

    def step(self, k):
        for when, block in self.line.step(k):
            copy = self.links.push(block, block, dp=self.links.y_peer, when=when)
            self.over_y.append((when, copy))

    def finish(self):
        for when, copy in self.over_y:
            if when is None:
                copy.wait_recv()
            else:
                pl.when(when)(copy.wait_recv)


class PairGather:
    def __init__(self, links, view):
        self.links = links
        self.near = Line(links, lambda z: view(2 * z + links.y))
        self.far = Line(links, lambda z: view(2 * z + 1 - links.y))
        self.own = view(links.dp)

    def start_y(self):
        self.over_y = self.links.push(self.own, self.own, dp=self.links.y_peer)

    def start_z(self):
        self.near.start()

    def join(self):
        self.over_y.wait_recv()
        self.far.start()

    def step(self, k):
        self.near.step(k)
        self.far.step(k)


class Chain:
    def __init__(self, links, view, slots):
        self.links, self.view, self.slots = links, view, slots
        self.up, self.down = {}, {}

    def start(self):
        l = self.links
        last = PLANES - 1
        for d in range(PLANES):
            if d > 0:
                self.up[d] = l.plan(self.view(d), self.slots(d), dp=jnp.minimum(l.dp + 2, 2 * last + 1))
            if d < last:
                place = jnp.where(l.z == d + 1, PLANES, d)
                self.down[d] = l.plan(self.view(d), self.slots(place), dp=jnp.maximum(l.dp - 2, 0))

    def add(self, d, copy):
        copy.wait_recv()
        block = self.view(d)
        block[...] = (block[...].astype(F32) + self.slots(d)[...].astype(F32)).astype(BF)

    def step(self, j):
        last = PLANES - 1

        @pl.when(self.links.z == j)
        def _():
            for d in range(last, j, -1):
                if j > 0:
                    self.add(d, self.up[d])
                self.up[d].start()

        @pl.when(self.links.z == last - j)
        def _():
            for d in range(last - j):
                if j > 0:
                    self.add(d, self.down[d])
                self.down[d].start()

        for d in range(PLANES):
            if d > j:
                self.links.late.append((self.up[d], self.links.z == j))
            if d < last - j:
                self.links.late.append((self.down[d], self.links.z == last - j))

    def total(self):
        l = self.links
        for d in range(PLANES):
            if d > 0:
                pl.when(l.z == d)(self.up[d].wait_recv)
            if d < PLANES - 1:
                pl.when(l.z == d)(self.down[d].wait_recv)
        own = self.view(l.z)[...].astype(F32)
        below = jnp.where(l.z > 0, self.slots(l.z)[...].astype(F32), 0.0)
        above = jnp.where(l.z < PLANES - 1, self.slots(PLANES)[...].astype(F32), 0.0)
        return own + (below + above)


class Scatter:
    def __init__(self, links, view, y_slots, z_slots):
        self.links, self.view, self.y_slots = links, view, y_slots
        self.chain = Chain(links, lambda z: view(2 * z + links.y), z_slots)

    def start(self):
        l = self.links
        self.order = [jnp.where(l.z < PLANES // 2, PLANES - 1 - k, k) for k in range(PLANES)]
        self.over_y = [
            l.push(self.view(2 * d + 1 - l.y), self.y_slots(k), dp=l.y_peer, late=True) for k, d in enumerate(self.order)
        ]
        self.chain.start()

    def join(self):
        for k, copy in enumerate(self.over_y):
            copy.wait_recv()
            block = self.view(2 * self.order[k] + self.links.y)
            block[...] = (block[...].astype(F32) + self.y_slots(k)[...].astype(F32)).astype(BF)

    def step(self, j):
        self.chain.step(j)

    def total(self):
        return self.chain.total()


class PairScatter:
    def __init__(self, links, view, y_slot, near_slots, far_slots):
        self.links, self.view, self.y_slot = links, view, y_slot
        self.near = Chain(links, lambda z: view(2 * z + links.y), near_slots)
        self.far = Chain(links, lambda z: view(2 * z + 1 - links.y), far_slots)

    def start(self):
        self.far.start()
        self.near.start()

    def step(self, j):
        self.far.step(j)
        self.near.step(j)

    def cross(self):
        l = self.links
        block = self.view(2 * l.z + 1 - l.y)
        block[...] = self.far.total().astype(BF)
        self.over_y = l.push(block, self.y_slot, dp=l.y_peer, late=True)

    def total(self):
        own = self.near.total()
        self.over_y.wait_recv()
        return own + self.y_slot[...].astype(F32)


class RowSum:
    def __init__(self, links, slots):
        self.links, self.slots = links, slots

    def hand_over(self, src):
        self.first = self.links.push(src, self.slots.at[0], s=self.links.s1)

    def cross(self, src):
        self.first.wait_recv()
        src[...] = (src[...].astype(F32) + self.slots[0].astype(F32).reshape(src.shape)).astype(BF)
        self.second = self.links.push(src, self.slots.at[1], s=self.links.s2)

    def near(self, src):
        self.third = self.links.push(src, self.slots.at[2], s=self.links.s1)

    def total(self, own):
        self.third.wait_recv()
        self.second.wait_recv()
        return own + self.slots[1].astype(F32).reshape(own.shape) + self.slots[2].astype(F32).reshape(own.shape)


def lane_masks(rows):
    lane = lax.broadcasted_iota(jnp.int32, (rows, 128), 1)
    return lane < 64, lax.rem(lane, 64) < 32


def turned(values, low):
    return jnp.where(low, -pltpu.roll(values, 96, 1), pltpu.roll(values, 32, 1))


def unturned(values, low):
    return jnp.where(low, pltpu.roll(values, 96, 1), -pltpu.roll(values, 32, 1))


def per_head_mean(values, first):
    left = jnp.sum(jnp.where(first, values, 0.0), axis=-1, keepdims=True)
    right = jnp.sum(jnp.where(first, 0.0, values), axis=-1, keepdims=True)
    return jnp.where(first, left, right) * (1.0 / HEAD_SIZE)


def norm_rope(values, gain, cosine, sine, first, low):
    normed = values * lax.rsqrt(per_head_mean(values * values, first) + EPS) * gain
    return normed * cosine + turned(normed, low) * sine


def norm_rope_back(upstream, values, gain, cosine, sine, first, low):
    d_normed = upstream * cosine + unturned(upstream * sine, low)
    inverse = lax.rsqrt(per_head_mean(values * values, first) + EPS)
    unit = values * inverse
    scaled = d_normed * gain
    d_values = inverse * (scaled - unit * per_head_mean(scaled * unit, first))
    return d_values, jnp.sum(d_normed * unit, axis=0, keepdims=True)


def allowed_block(r, block, keys):
    query = lax.broadcasted_iota(jnp.int32, (TOK, keys), 0) + block * TOK
    key = lax.broadcasted_iota(jnp.int32, (TOK, keys), 1)
    place = lax.broadcasted_iota(jnp.int32, (TOK, 1), 0) + block * TOK
    begin = jnp.zeros((TOK, 1), jnp.int32)
    for k in range(4):
        start = r.doc_starts[0, k]
        begin = jnp.maximum(begin, jnp.where(place >= start, start, 0))
    return (key <= query) & (key >= begin)


SCORE_SCALE = HEAD_SIZE ** (-0.5)


def attention_block(r, pair, block):
    keys = (block + 1) * TOK
    rows = pl.ds(block * TOK, TOK)
    queries = r.q_heads[pair, :, rows, :].reshape(2 * TOK, HEAD_SIZE)
    scores = dot_nt(queries, r.k_heads[pair, :keys, :]).reshape(2, TOK, keys) * SCORE_SCALE
    scores = jnp.where(allowed_block(r, block, keys)[None], scores, MASKED)
    top = jnp.max(scores, axis=-1, keepdims=True)
    weights = jnp.exp(scores - top)
    total = jnp.sum(weights, axis=-1, keepdims=True)
    mixed = dot(weights.astype(BF).reshape(2 * TOK, keys), r.v_heads[pair, :keys, :])
    mixed = mixed.reshape(2, TOK, HEAD_SIZE) / total
    log_total = top + jnp.log(total)
    r.log_total[rows, 2 * pair : 2 * pair + 1] = log_total[0]
    r.log_total[rows, 2 * pair + 1 : 2 * pair + 2] = log_total[1]
    r.att_own[block, :, pair * 128 : (pair + 1) * 128] = jnp.concatenate(
        [mixed[0], mixed[1]], axis=-1
    ).astype(BF)


def attention_block_back(r, pair, block):
    keys = (block + 1) * TOK
    rows = pl.ds(block * TOK, TOK)
    queries = r.q_heads[pair, :, rows, :].reshape(2 * TOK, HEAD_SIZE)
    grads = r.d_att_rows[block, :, pair * 128 : (pair + 1) * 128]
    grads = jnp.concatenate([grads[:, :HEAD_SIZE], grads[:, HEAD_SIZE:]], axis=0)
    keys_in, values_in = r.k_heads[pair, :keys, :], r.v_heads[pair, :keys, :]
    scores = dot_nt(queries, keys_in).reshape(2, TOK, keys) * SCORE_SCALE
    log_total = jnp.stack([r.log_total[rows, 2 * pair + g : 2 * pair + g + 1] for g in range(2)])
    chances = jnp.exp(scores - log_total)
    chances = jnp.where(allowed_block(r, block, keys)[None], chances, 0.0)
    d_chances = dot_nt(grads, values_in).reshape(2, TOK, keys)
    row_dots = jnp.sum(d_chances * chances, axis=-1, keepdims=True)
    d_scores = (chances * (d_chances - row_dots)).astype(BF).reshape(2 * TOK, keys)
    d_query = (dot(d_scores, keys_in) * SCORE_SCALE).astype(BF)
    r.d_query[rows, pair * 128 : (pair + 1) * 128] = jnp.concatenate(
        [d_query[:TOK], d_query[TOK:]], axis=-1
    )
    d_key = dot_tn(d_scores, queries) * SCORE_SCALE
    d_value = dot_tn(chances.astype(BF).reshape(2 * TOK, keys), grads)
    if block == ROW // TOK - 1:
        r.d_kv[pair, :, :HEAD_SIZE] = d_key
        r.d_kv[pair, :, HEAD_SIZE:] = d_value
    else:
        r.d_kv[pair, :keys, :HEAD_SIZE] += d_key
        r.d_kv[pair, :keys, HEAD_SIZE:] += d_value


def norm_back_unit(upstream, values):
    inverse = lax.rsqrt(jnp.mean(values * values, axis=-1, keepdims=True) + EPS)
    unit = values * inverse
    d_values = inverse * (
        upstream - unit * jnp.mean(upstream * unit, axis=-1, keepdims=True)
    )
    return d_values, jnp.sum(upstream * unit, axis=0, keepdims=True)


def unit_norm(values):
    return values * lax.rsqrt(jnp.mean(values * values, axis=-1, keepdims=True) + EPS)


def as_row(vector):
    return vector[...].astype(F32).reshape(1, vector.shape[0])


def twice(vector):
    row = as_row(vector)
    return jnp.concatenate([row, row], axis=1)


def column(row):
    n = row.shape[1]
    same = lax.broadcasted_iota(jnp.int32, (n, n), 0) == lax.broadcasted_iota(jnp.int32, (n, n), 1)
    return jnp.sum(jnp.where(same, row, 0.0), axis=1, keepdims=True)


def own_parts(r):
    scale = column(as_row(r.attn_gain))
    for o in range(SEQ):
        for ref, first, size in ((r.w_query, 0, OWN_Q), (r.w_key, OWN_Q, OWN_K), (r.w_value, OWN_Q + OWN_K, OWN_K)):
            part = ref[:, o * size : (o + 1) * size].astype(F32) * scale
            r.w_qkv[o, :, first : first + size] = part.astype(BF)


def own_units(r):
    scale = column(as_row(r.ffn_gain))
    for ref, first in ((r.w_gate, 0), (r.w_up, FF_OWN)):
        scaled = ref[...].astype(F32) * scale
        for o in range(SEQ):
            parts = [scaled[:, (4 * j + o) * FF_SHARD : (4 * j + o + 1) * FF_SHARD] for j in range(8)]
            r.d_gu[32 + o, :, first : first + FF_OWN] = jnp.concatenate(parts, axis=1).astype(BF)


def rotation_tables(r, half):
    size = ROW // 2
    rows = pl.ds(half * size, size)
    place = lax.broadcasted_iota(jnp.int32, (size, 1), 0) + half * size
    begin = jnp.zeros((size, 1), jnp.int32)
    for k in range(4):
        start = r.doc_starts[0, k]
        begin = jnp.maximum(begin, jnp.where(place >= start, start, 0))
    angles = (place - begin).astype(F32) * r.frequency[...]
    r.cosine[rows, :] = jnp.cos(angles)
    r.sine[rows, :] = jnp.sin(angles)


def head_forward(r):
    first, low = lane_masks(TOK)

    @pl.loop(0, SEQ)
    def _(t):
        rows = pl.ds(pl.multiple_of(t * TOK, TOK), TOK)
        linear = dot(r.u_rows[t], r.qkv_all[...].reshape(WIDTH, QKV))
        r.q_linear[rows, :] = linear[:, :OWN_Q]
        r.k_linear[rows, :] = linear[:, OWN_Q : OWN_Q + OWN_K]
        cosine, sine = r.cosine[rows, :], r.sine[rows, :]
        for pair in range(2):
            part = linear[:, pair * 128 : (pair + 1) * 128]
            part = norm_rope(part, twice(r.q_gain), cosine, sine, first, low).astype(BF)
            r.q_heads[pair, 0, rows, :] = part[:, :HEAD_SIZE]
            r.q_heads[pair, 1, rows, :] = part[:, HEAD_SIZE:]
        part = linear[:, OWN_Q : OWN_Q + OWN_K]
        part = norm_rope(part, twice(r.k_gain), cosine, sine, first, low).astype(BF)
        r.k_heads[0, rows, :] = part[:, :HEAD_SIZE]
        r.k_heads[1, rows, :] = part[:, HEAD_SIZE:]
        part = linear[:, OWN_Q + OWN_K :].astype(BF)
        r.v_heads[0, rows, :] = part[:, :HEAD_SIZE]
        r.v_heads[1, rows, :] = part[:, HEAD_SIZE:]


def head_backward(r):
    first, low = lane_masks(TOK)
    r.head_gain_part[...] = jnp.zeros((2, 128), F32)

    @pl.loop(0, SEQ)
    def _(t):
        rows = pl.ds(pl.multiple_of(t * TOK, TOK), TOK)
        cosine, sine = r.cosine[rows, :], r.sine[rows, :]
        for pair in range(2):
            cols = slice(pair * 128, (pair + 1) * 128)
            up = r.d_query[rows, cols].astype(F32)
            back, gain_part = norm_rope_back(up, r.q_linear[rows, cols], twice(r.q_gain), cosine, sine, first, low)
            r.d_qkv[rows, cols] = back.astype(BF)
            r.head_gain_part[0:1] += gain_part
        up = jnp.concatenate([r.d_kv[0, rows, :HEAD_SIZE], r.d_kv[1, rows, :HEAD_SIZE]], axis=-1)
        up = up.astype(BF).astype(F32)
        back, gain_part = norm_rope_back(up, r.k_linear[rows, :], twice(r.k_gain), cosine, sine, first, low)
        r.d_qkv[rows, OWN_Q : OWN_Q + OWN_K] = back.astype(BF)
        r.head_gain_part[1:2] += gain_part
        up = jnp.concatenate([r.d_kv[0, rows, HEAD_SIZE:], r.d_kv[1, rows, HEAD_SIZE:]], axis=-1)
        r.d_qkv[rows, OWN_Q + OWN_K :] = up.astype(BF)


def units_up(r, t):
    gate_up = dot(r.mid_rows[t], r.gu_all[...].reshape(WIDTH, HIDDEN_TWO))
    gate, up = gate_up[:, :FF_OWN], gate_up[:, FF_OWN:]
    sigmoid = 1.0 / (1.0 + jnp.exp(-gate))
    swish = gate * sigmoid
    r.active[t] = (swish * up).astype(BF)
    blocks = pl.ds(8 * t, 8)
    by_gate = up * (sigmoid * (1.0 + gate * (1.0 - sigmoid)))
    r.d_gu[blocks, :, :FF_OWN] = by_gate.astype(BF).reshape(8, 32, FF_OWN)
    r.d_gu[blocks, :, FF_OWN:] = swish.astype(BF).reshape(8, 32, FF_OWN)


def units_down(r, t):
    d_active = dot_nt(r.cot_rows[t], r.down_all[...].reshape(FF_OWN, WIDTH)).reshape(8, 32, FF_OWN)
    blocks = pl.ds(8 * t, 8)
    r.d_gu[blocks, :, :FF_OWN] = (d_active * r.d_gu[blocks, :, :FF_OWN].astype(F32)).astype(BF)
    r.d_gu[blocks, :, FF_OWN:] = (d_active * r.d_gu[blocks, :, FF_OWN:].astype(F32)).astype(BF)
    d_gu = r.d_gu[blocks].reshape(TOK, HIDDEN_TWO)
    return dot_nt(d_gu, r.gu_all[...].reshape(WIDTH, HIDDEN_TWO))


def whole_block(r):
    l = r.links = Links(r.send_sems, r.recv_sems)
    l.greet(pltpu.get_barrier_semaphore(), l.everyone())
    x = r.inputs[...].astype(F32)
    r.u_rows[l.s] = unit_norm(x).astype(BF)
    own_parts(r)
    own_units(r)
    r.out_all[l.dp, l.s] = r.w_out[...]
    r.qkv_all[l.dp, l.s] = r.w_qkv[l.s]
    r.gu_all[l.dp, l.s] = r.d_gu[32 + l.s]
    r.down_all[l.dp] = r.w_down[...]
    r.cot_rows[l.s] = r.cotangent[...]
    pl.semaphore_wait(pltpu.get_barrier_semaphore(), len(l.everyone()))
    out = PairGather(l, lambda b: r.out_all.at[b, l.s])
    qkv = Gather(l, lambda b: r.qkv_all.at[b])
    gate_up = [Gather(l, lambda b, g=g: r.gu_all.at[b, g]) for g in (l.s,) + l.others]
    down_a = Gather(l, lambda b: r.down_all.at[b, pl.ds(0, DOWN_A)])
    down_b = PairGather(l, lambda b: r.down_all.at[b, pl.ds(DOWN_A, DOWN_B)])
    qkv_cols = [l.push(r.w_qkv.at[o], r.qkv_all.at[l.dp, l.s], s=o) for o in l.others]
    gate_up[0].start_z()
    gate_up[0].start_y()
    for copy in qkv_cols:
        copy.wait_recv()
    qkv.start_z()
    out.start_y()
    gu_cols = [l.push(r.d_gu.at[32 + o], r.gu_all.at[l.dp, l.s], s=o) for o in l.others]
    out.start_z()
    rotation_tables(r, 0)
    down_b.start_y()
    qkv.start_y()
    out.join()
    u_far = l.push(r.u_rows.at[l.s], r.u_rows.at[l.s], s=l.s2)
    u_near = l.push(r.u_rows.at[l.s], r.u_rows.at[l.s], s=l.s1)
    qkv.step(0)
    gu_cols[1].wait_recv()
    gu_cols[2].wait_recv()
    gu_cols[0].wait_recv()
    out.step(0)
    gate_up[2].start_y()
    rotation_tables(r, 1)
    out.step(1)
    gate_up[1].start_y()
    qkv.step(1)
    gate_up[1].start_z()
    u_far.wait_recv()
    u_more = l.push(r.u_rows.at[l.s2], r.u_rows.at[l.s2], s=l.s1)
    out.step(2)
    gate_up[3].start_z()
    qkv.step(2)
    gate_up[0].step(0)
    gate_up[3].step(0)
    gate_up[3].start_y()
    qkv.finish()
    gate_up[1].step(0)
    out_far = l.push(r.out_all.at[:, l.s], r.out_all.at[:, l.s], s=l.s2)
    out_near = l.push(r.out_all.at[:, l.s], r.out_all.at[:, l.s], s=l.s1)
    u_near.wait_recv()
    u_more.wait_recv()
    gate_up[0].step(1)
    head_forward(r)
    down_a.start_z()
    attention_block(r, 0, 3)
    attention_block(r, 1, 3)
    attention_block(r, 0, 2)
    attention_block(r, 1, 2)
    attention_block(r, 0, 1)
    gate_up[0].step(2)
    gate_up[3].step(1)
    attention_block(r, 1, 1)
    gate_up[2].start_z()
    attention_block(r, 0, 0)
    attention_block(r, 1, 0)
    att = [l.push(r.att_own.at[o], r.att_local.at[l.s], s=o) for o in l.others]
    r.att_local[l.s] = r.att_own[l.s]
    gate_up[3].step(2)
    gate_up[1].step(1)
    out_far.wait_recv()
    out_more = l.push(r.out_all.at[:, l.s2], r.out_all.at[:, l.s2], s=l.s1)
    out_near.wait_recv()
    out_more.wait_recv()
    for copy in att:
        copy.wait_recv()
    middle = x
    for part in range(SEQ):
        rows = r.out_all[part * 2 : (part + 1) * 2].reshape(OWN_Q, WIDTH)
        middle = middle + dot(r.att_local[part], rows)
    r.middle[...] = middle
    r.mid_rows[l.s] = unit_norm(middle).astype(BF)
    mid_far = l.push(r.mid_rows.at[l.s], r.mid_rows.at[l.s], s=l.s2)
    mid_near = l.push(r.mid_rows.at[l.s], r.mid_rows.at[l.s], s=l.s1)
    down_b.start_z()
    gate_up[1].step(2)
    cot_far = l.push(r.cot_rows.at[l.s], r.cot_rows.at[l.s], s=l.s2)
    cot_near = l.push(r.cot_rows.at[l.s], r.cot_rows.at[l.s], s=l.s1)
    gate_up[2].step(0)
    gate_up[2].step(1)
    gate_up[2].step(2)
    down_b.join()
    down_a.start_y()
    gate_up[1].finish()
    gate_up[3].finish()
    mid_far.wait_recv()
    mid_more = l.push(r.mid_rows.at[l.s2], r.mid_rows.at[l.s2], s=l.s1)
    mid_near.wait_recv()
    mid_more.wait_recv()
    down_a.step(0)
    down_b.step(0)
    gate_up[0].finish()
    gate_up[2].finish()
    units_up(r, l.s3)
    down_a.step(1)
    units_up(r, l.s2)
    units_up(r, l.s1)
    units_up(r, l.s)
    cot_far.wait_recv()
    cot_more = l.push(r.cot_rows.at[l.s2], r.cot_rows.at[l.s2], s=l.s1)
    down_b.step(1)
    cot_near.wait_recv()
    cot_more.wait_recv()
    for t in range(SEQ):
        r.flipped[:, t * TOK : (t + 1) * TOK] = r.active[t].T
    cot = r.cot_rows[...].reshape(ROW, WIDTH)

    @pl.loop(0, 4)
    def _(k):
        rows = pl.ds(pl.multiple_of(k * 288, 32), 288)
        grad = dot(r.flipped[rows, :], cot).astype(BF)
        r.down_part[pl.ds(2 * k, 2)] = grad.reshape(2, FF_SHARD, WIDTH)

    down_a_sum = Scatter(
        l, lambda b: r.down_part.at[b, pl.ds(0, SUM_A)], lambda k: r.down_a_slots.at[k], lambda k: r.down_a_slots.at[4 + k]
    )
    down_b_sum = PairScatter(
        l,
        lambda b: r.down_part.at[b, pl.ds(SUM_A, SUM_B)],
        r.down_b_slots.at[10],
        lambda k: r.down_b_slots.at[k],
        lambda k: r.down_b_slots.at[5 + k],
    )
    d_mid = RowSum(l, r.slots_a)
    home = []
    down_a.step(2)
    down_a_sum.start()
    down_b_sum.start()
    down_b_sum.step(0)
    down_a.finish()
    down_b.step(2)
    l.drain()
    r.parts[0] = units_down(r, l.s3).astype(BF).reshape(8, 32, WIDTH)
    d_mid.hand_over(r.parts.at[0])
    r.parts[1] = units_down(r, l.s2).astype(BF).reshape(8, 32, WIDTH)
    d_mid.cross(r.parts.at[1])
    r.parts[2] = units_down(r, l.s1).astype(BF).reshape(8, 32, WIDTH)
    d_mid.near(r.parts.at[2])
    r.input_grad[...] = units_down(r, l.s)
    for t in range(SEQ):
        r.flipped[:WIDTH, t * TOK : (t + 1) * TOK] = r.mid_rows[t].T
    d_gu = r.d_gu[0:32].reshape(ROW, HIDDEN_TWO)

    @pl.loop(0, 4)
    def _(k):
        rows = pl.ds(pl.multiple_of(k * 256, 256), 256)
        grad = dot(r.flipped[rows, :], d_gu).astype(BF)
        r.gu_all[pl.ds(2 * k, 2)] = grad.reshape(2, 4, 32, HIDDEN_TWO)

    l.greet(r.free, l.column())
    pl.semaphore_wait(r.free, len(l.column()))
    gu_sums = [
        Scatter(
            l,
            lambda b, g=g: r.gu_all.at[b, g],
            lambda k, n=n: r.d_gu.at[9 * n + k],
            lambda k, n=n: r.d_gu.at[9 * n + 4 + k],
        )
        for n, g in enumerate(l.others)
    ]
    own_gu_sum = PairScatter(
        l,
        lambda b: r.gu_all.at[b, l.s],
        r.d_gu.at[37],
        lambda k: r.d_gu.at[27 + k],
        lambda k: r.d_gu.at[32 + k],
    )
    own_gu_sum.start()
    own_gu_sum.step(0)
    gu_sums[1].start()
    d_values, ffn_gain_part = norm_back_unit(d_mid.total(r.input_grad[...]), r.middle[...])
    d_middle = r.cotangent[...].astype(F32) + d_values
    r.input_grad[...] = d_middle
    d_branch = d_middle.astype(BF)
    r.gains[0, 1:2, :] = ffn_gain_part
    for part in range(SEQ):
        rows = r.out_all[part * 2 : (part + 1) * 2].reshape(OWN_Q, WIDTH)
        r.att_own[part] = dot_nt(d_branch, rows).astype(BF)
    d_att = [l.push(r.att_own.at[o], r.d_att_rows.at[l.s], s=o) for o in l.others]
    r.d_att_rows[l.s] = r.att_own[l.s]
    down_b_sum.step(1)
    down_a_sum.join()
    down_a_sum.step(0)
    for part in range(SEQ):
        grad = dot_tn(r.att_local[part], d_branch).astype(BF)
        r.out_all[2 * part : 2 * part + 2] = grad.reshape(2, 4, 32, WIDTH)
    out_row = RowSum(l, r.slots_b)
    out_row.hand_over(r.out_all.at[:, l.s3])
    gu_sums[1].join()
    gu_sums[1].step(0)
    gu_sums[2].start()
    out_row.cross(r.out_all.at[:, l.s2])
    out_row.near(r.out_all.at[:, l.s1])
    for copy in d_att:
        copy.wait_recv()
    l.settle((d_mid.first, d_mid.second, d_mid.third))
    attention_block_back(r, 0, 3)
    attention_block_back(r, 1, 3)
    attention_block_back(r, 0, 2)
    attention_block_back(r, 1, 2)
    down_b_sum.step(2)
    attention_block_back(r, 0, 1)
    own_gu_sum.step(1)
    attention_block_back(r, 1, 1)
    attention_block_back(r, 0, 0)
    attention_block_back(r, 1, 0)
    gu_sums[0].start()
    head_backward(r)
    out_total = out_row.total(r.out_all[:, l.s].astype(F32))
    r.out_all[:, l.s] = out_total.astype(BF)
    out_sum = Scatter(
        l, lambda b: r.out_all.at[b, l.s], lambda k: r.out_slots.at[k], lambda k: r.out_slots.at[4 + k]
    )
    d_u = RowSum(l, r.slots_a)
    weights = r.qkv_all[...].reshape(WIDTH, QKV)

    def d_u_part(t):
        return dot_nt(r.d_qkv[pl.ds(pl.multiple_of(t * TOK, TOK), TOK), :], weights)

    r.parts[0] = d_u_part(l.s3).astype(BF).reshape(8, 32, WIDTH)
    d_u.hand_over(r.parts.at[0])
    r.parts[1] = d_u_part(l.s2).astype(BF).reshape(8, 32, WIDTH)
    d_u.cross(r.parts.at[1])
    r.parts[2] = d_u_part(l.s1).astype(BF).reshape(8, 32, WIDTH)
    d_u.near(r.parts.at[2])
    own = d_u_part(l.s)
    gu_sums[2].join()
    gu_sums[2].step(0)
    down_a_sum.step(1)
    for t in range(SEQ):
        r.flipped[:WIDTH, t * TOK : (t + 1) * TOK] = r.u_rows[t].T
    grad = dot(r.flipped[:WIDTH, :], r.d_qkv[...]).astype(BF)
    r.qkv_all[...] = grad.reshape(8, 4, 32, QKV)
    qkv_sum = Scatter(l, lambda b: r.qkv_all.at[b], lambda k: r.qkv_slots.at[k], lambda k: r.qkv_slots.at[4 + k])
    down_a_sum.step(2)
    qkv_sum.start()
    gu_sums[1].step(1)
    own_gu_sum.step(2)
    gu_sums[1].step(2)
    gu_sums[2].step(1)
    x = r.inputs[...].astype(F32)
    d_values, attn_gain_part = norm_back_unit(d_u.total(own), x)
    r.input_grad[...] += d_values
    r.gains[0, 0:1, :] = attn_gain_part
    r.gains[0, 2:3, 0:128] = r.head_gain_part[0:1]
    r.gains[0, 2:3, 128:256] = r.head_gain_part[1:2]
    r.gains[0, 2:3, 256:] = jnp.zeros((1, WIDTH - 256), F32)
    r.gains[0, 3:8, :] = jnp.zeros((5, WIDTH), F32)
    gains = [l.push(r.gains.at[0], r.gain_slots.at[k], s=o) for k, o in enumerate(l.others)]
    l.settle((d_u.first, d_u.second, d_u.third))
    gu_sums[0].join()
    gu_sums[0].step(0)
    out_sum.start()
    down_all = r.down_all[...].reshape(FF_OWN, WIDTH)
    last = RowSum(l, r.slots_b)
    r.parts[0] = dot(r.active[l.s3], down_all).astype(BF).reshape(8, 32, WIDTH)
    last.hand_over(r.parts.at[0])
    r.parts[1] = dot(r.active[l.s2], down_all).astype(BF).reshape(8, 32, WIDTH)
    last.cross(r.parts.at[1])
    r.parts[2] = dot(r.active[l.s1], down_all).astype(BF).reshape(8, 32, WIDTH)
    last.near(r.parts.at[2])
    own = r.middle[...] + dot(r.active[l.s], down_all)
    for copy in gains:
        copy.wait_recv()
    r.gains[1] = r.gains[0] + r.gain_slots[0] + r.gain_slots[1] + r.gain_slots[2]
    gains_y = l.push(r.gains.at[1], r.gain_slots.at[3], dp=l.y_peer)
    gu_sums[2].step(2)
    gu_sums[0].step(1)
    down_b_sum.cross()
    r.down_grad[0:SUM_A] = down_a_sum.total()
    qkv_sum.join()
    qkv_sum.step(0)
    own_gu_sum.cross()
    out_sum.join()
    out_sum.step(0)
    gu_sums[0].step(2)
    r.gu_all[l.dp, l.s3] = gu_sums[2].total().astype(BF)
    home.append(l.push(r.gu_all.at[l.dp, l.s3], r.gu_grad.at[l.s], s=l.s3))
    r.gu_all[l.dp, l.s2] = gu_sums[1].total().astype(BF)
    home.append(l.push(r.gu_all.at[l.dp, l.s2], r.gu_grad.at[l.s], s=l.s2))
    qkv_sum.step(1)
    r.down_grad[SUM_A:] = down_b_sum.total()
    r.gu_all[l.dp, l.s1] = gu_sums[0].total().astype(BF)
    home.append(l.push(r.gu_all.at[l.dp, l.s1], r.gu_grad.at[l.s], s=l.s1))
    qkv_sum.step(2)
    r.output[...] = last.total(own).astype(BF)
    gains_y.wait_recv()
    r.gains[2] = r.gains[1] + r.gain_slots[3]
    gains_z = [l.push(r.gains.at[2], r.gain_slots.at[4 + k], dp=p) for k, p in enumerate(l.z_peers)]
    r.gu_grad[l.s] = own_gu_sum.total().astype(BF)
    out_sum.step(1)
    r.qkv_all[l.dp] = qkv_sum.total().astype(BF)
    home += [l.push(r.qkv_all.at[l.dp, o], r.qkv_grad.at[l.s], s=o) for o in l.others]
    r.qkv_grad[l.s] = r.qkv_all[l.dp, l.s]
    out_sum.step(2)
    r.out_grad[...] = out_sum.total()
    for copy in gains_z + home:
        copy.wait_recv()
    r.gain_grads[...] = r.gains[2] + r.gain_slots[4] + r.gain_slots[5] + r.gain_slots[6]
    l.drain()
    l.drain_late()


def own_lanes(row, size):
    place = (lax.axis_index("dp") * SEQ + lax.axis_index("seq")) * size
    return pltpu.roll(row, lax.rem(WIDTH - place, WIDTH), 1)[:, :size]


def lay_out(
    output, input_grad, down_grad, out_grad, gu_grad, qkv_grad, gains, attn_gain, ffn_gain,
    output_o, input_o, attn_o, query_o, key_o, value_o, q_gain_o, k_gain_o, out_o, ffn_o, gate_o, up_o, down_o,
):
    for src, dst in ((output, output_o), (input_grad, input_o), (down_grad, down_o), (out_grad, out_o)):
        dst[...] = src[...]
    attn_scale = scale = column(as_row(attn_gain))
    for o in range(SEQ):
        for ref, first, size in ((query_o, 0, OWN_Q), (key_o, OWN_Q, OWN_K), (value_o, OWN_Q + OWN_K, OWN_K)):
            ref[:, o * size : (o + 1) * size] = qkv_grad[o, :, first : first + size].astype(F32) * scale
    scale = column(as_row(ffn_gain))
    for ref, first in ((gate_o, 0), (up_o, FF_OWN)):
        parts = []
        for j in range(8):
            for o in range(SEQ):
                part = gu_grad[o, :, first + j * FF_SHARD : first + (j + 1) * FF_SHARD]
                parts.append(part.astype(F32) * scale)
        ref[...] = jnp.concatenate(parts, axis=1)
    size = attn_o.shape[0]
    attn_o[...] = (column(own_lanes(gains[0:1, :], size)) / attn_scale).reshape(size)
    ffn_o[...] = (column(own_lanes(gains[1:2, :], size)) / scale).reshape(size)
    q_gain_o[...] = (gains[2:3, 0:64] + gains[2:3, 64:128]).reshape(HEAD_SIZE)
    k_gain_o[...] = (gains[2:3, 128:192] + gains[2:3, 192:256]).reshape(HEAD_SIZE)


class Names:
    pass


def frequencies():
    steps = np.arange(HEAD_SIZE // 2, dtype=np.float64) * (2.0 / HEAD_SIZE)
    return jnp.asarray(np.tile(THETA ** (-steps), 4)[None], F32)


MAX_COPIES = 300
VMEM_BYTES = 63 * 2**20


def on_device_in_kernels(
    inputs,
    doc_starts,
    cotangent,
    attn_gain,
    w_query,
    key_projection_weight,
    value_projection_weight,
    q_gain,
    k_gain,
    w_out,
    ffn_gain,
    w_gate,
    w_up,
    w_down,
):
    given = dict(
        inputs=inputs,
        cotangent=cotangent,
        attn_gain=attn_gain,
        ffn_gain=ffn_gain,
        q_gain=q_gain,
        k_gain=k_gain,
        w_query=w_query,
        w_key=key_projection_weight,
        w_value=value_projection_weight,
        w_out=w_out,
        w_gate=w_gate,
        w_up=w_up,
        w_down=w_down,
        frequency=frequencies(),
        doc_starts=doc_starts,
    )
    results = dict(
        output=((TOK, WIDTH), BF),
        input_grad=((TOK, WIDTH), F32),
        down_grad=((FF_SHARD, WIDTH), F32),
        out_grad=((32, WIDTH), F32),
        gu_grad=((SEQ, 32, HIDDEN_TWO), BF),
        qkv_grad=((SEQ, 32, QKV), BF),
        gain_grads=((8, WIDTH), F32),
    )
    kept = dict(
        w_qkv=((SEQ, 32, QKV), BF),
        cosine=((ROW, 128), F32),
        sine=((ROW, 128), F32),
        u_rows=((SEQ, TOK, WIDTH), BF),
        cot_rows=((SEQ, TOK, WIDTH), BF),
        mid_rows=((SEQ, TOK, WIDTH), BF),
        qkv_all=((8, 4, 32, QKV), BF),
        gu_all=((8, 4, 32, HIDDEN_TWO), BF),
        down_all=((8, FF_SHARD, WIDTH), BF),
        out_all=((8, 4, 32, WIDTH), BF),
        q_linear=((ROW, OWN_Q), F32),
        k_linear=((ROW, OWN_K), F32),
        q_heads=((2, 2, ROW, HEAD_SIZE), BF),
        k_heads=((2, ROW, HEAD_SIZE), BF),
        v_heads=((2, ROW, HEAD_SIZE), BF),
        log_total=((ROW, 128), F32),
        att_own=((SEQ, TOK, OWN_Q), BF),
        att_local=((SEQ, TOK, OWN_Q), BF),
        middle=((TOK, WIDTH), F32),
        active=((SEQ, TOK, FF_OWN), BF),
        d_gu=((38, 32, HIDDEN_TWO), BF),
        parts=((3, 8, 32, WIDTH), BF),
        slots_a=((3, 8, 32, WIDTH), BF),
        slots_b=((3, 8, 32, WIDTH), BF),
        d_att_rows=((SEQ, TOK, OWN_Q), BF),
        flipped=((FF_OWN, ROW), BF),
        down_part=((8, FF_SHARD, WIDTH), BF),
        down_a_slots=((9, SUM_A, WIDTH), BF),
        down_b_slots=((11, SUM_B, WIDTH), BF),
        out_slots=((9, 32, WIDTH), BF),
        qkv_slots=((9, 4, 32, QKV), BF),
        d_query=((ROW, OWN_Q), BF),
        d_kv=((2, ROW, 128), F32),
        d_qkv=((ROW, QKV), BF),
        head_gain_part=((2, 128), F32),
        gains=((3, 8, WIDTH), F32),
        gain_slots=((7, 8, WIDTH), F32),
    )

    def body(*refs):
        r = Names()
        names = [*given, *results, *kept]
        for name, ref in zip(names, refs):
            setattr(r, name, ref)
        r.send_sems, r.recv_sems, r.free = refs[len(names) :]
        whole_block(r)

    done = pl.pallas_call(
        body,
        out_shape=[jax.ShapeDtypeStruct(*result) for result in results.values()],
        in_specs=[
            pl.BlockSpec(memory_space=pltpu.SMEM if a is doc_starts else pltpu.VMEM) for a in given.values()
        ],
        out_specs=[pl.BlockSpec(memory_space=pltpu.VMEM)] * len(results),
        scratch_shapes=[pltpu.VMEM(*shape) for shape in kept.values()]
        + [
            pltpu.SemaphoreType.DMA((MAX_COPIES,)),
            pltpu.SemaphoreType.DMA((MAX_COPIES,)),
            pltpu.SemaphoreType.REGULAR,
        ],
        compiler_params=pltpu.CompilerParams(
            collective_id=0, has_side_effects=True, vmem_limit_bytes=VMEM_BYTES
        ),
        cost_estimate=pl.CostEstimate(flops=30_000_000_000, bytes_accessed=10_000_000, transcendentals=0),
    )(*given.values())
    rows = w_query.shape[0]
    shapes = [
        ((TOK, WIDTH), BF),
        ((TOK, WIDTH), F32),
        ((rows,), F32),
        ((rows, SEQ * OWN_Q), F32),
        ((rows, SEQ * OWN_K), F32),
        ((rows, SEQ * OWN_K), F32),
        ((HEAD_SIZE,), F32),
        ((HEAD_SIZE,), F32),
        ((rows, WIDTH), F32),
        ((rows,), F32),
        ((rows, FF), F32),
        ((rows, FF), F32),
        ((FF_SHARD, WIDTH), F32),
    ]
    return tuple(
        pl.pallas_call(
            lay_out,
            out_shape=[jax.ShapeDtypeStruct(*shape) for shape in shapes],
            in_specs=[pl.BlockSpec(memory_space=pltpu.VMEM)] * 9,
            out_specs=[pl.BlockSpec(memory_space=pltpu.VMEM)] * 13,
            compiler_params=pltpu.CompilerParams(vmem_limit_bytes=VMEM_BYTES),
            cost_estimate=pl.CostEstimate(flops=1_000_000, bytes_accessed=10_000_000, transcendentals=0),
        )(*done, given["attn_gain"], given["ffn_gain"])
    )


def solution(mesh):
    in_kernels = (mesh.shape["dp"], mesh.shape["seq"]) == (8, 4)
    placed = (
        P(("dp", "seq"), None),
        P("dp", None),
        P(("dp", "seq"), None),
        P(("dp", "seq")),
        P(("dp", "seq"), None),
        P(("dp", "seq"), None),
        P(("dp", "seq"), None),
        P(),
        P(),
        P(("dp", "seq"), None),
        P(("dp", "seq")),
        P(("dp", "seq"), None),
        P(("dp", "seq"), None),
        P(("dp", "seq"), None),
    )
    return jax.shard_map(
        on_device_in_kernels if in_kernels else on_device,
        mesh=mesh,
        in_specs=placed,
        out_specs=(
            P(("dp", "seq"), None),
            P(("dp", "seq"), None),
            P(("dp", "seq")),
            P(("dp", "seq"), None),
            P(("dp", "seq"), None),
            P(("dp", "seq"), None),
            P(),
            P(),
            P(("dp", "seq"), None),
            P(("dp", "seq")),
            P(("dp", "seq"), None),
            P(("dp", "seq"), None),
            P(("dp", "seq"), None),
        ),
        check_vma=False,
    )
```

```python
import jax
import jax.numpy as jnp
import numpy as np
from jax import lax
from jax.experimental import pallas as pl
from jax.experimental.pallas import tpu as pltpu
from jax.sharding import PartitionSpec as P

QUERY_HEADS = 16
KEY_VALUE_HEADS = 8
HEAD_SIZE = 64
FF = 4608


EPS = 1e-05
THETA = 1000000.0
MASKED = -1e30
CONTRACT_ROWS = (((0,), (0,)), ((), ()))
CONTRACT_COLS = (((1,), (1,)), ((), ()))


def rms_norm(values, gain_vec):
    return values * lax.rsqrt(jnp.mean(values * values, axis=-1, keepdims=True) + EPS) * gain_vec


def rotate_half(values):
    half_len = values.shape[-1] // 2
    return jnp.concatenate([-values[..., half_len:], values[..., :half_len]], axis=-1)


def unrotate_half(values):
    half_len = values.shape[-1] // 2
    return jnp.concatenate([values[..., half_len:], -values[..., :half_len]], axis=-1)


def row_layout(row_starts, places):
    inside = places[:, None] >= row_starts[None, :]
    doc_ids = jnp.sum(inside.astype(jnp.int32), axis=1) - 1
    begins = jnp.max(jnp.where(inside, row_starts[None, :], 0), axis=1)
    offsets = (places - begins).astype(jnp.float32)
    freq_steps = jnp.arange(HEAD_SIZE // 2, dtype=jnp.float32) * (2.0 / HEAD_SIZE)
    frequency = THETA ** (-freq_steps)
    angles = offsets[:, None] * frequency[None, :]
    angles = jnp.concatenate([angles, angles], axis=-1)
    return (doc_ids, jnp.cos(angles), jnp.sin(angles))


def norm_back(upstream, values, gain_vec):
    inverse = lax.rsqrt(jnp.mean(values * values, axis=-1, keepdims=True) + EPS)
    unit_vec = values * inverse
    gain_part = jnp.sum(upstream * unit_vec, axis=tuple(range(values.ndim - 1)))
    scaled = upstream * gain_vec
    return (
        inverse * (scaled - unit_vec * jnp.mean(scaled * unit_vec, axis=-1, keepdims=True)),
        gain_part,
    )


def head_forward_pass(linear, gain_vec, cosine_table, sine_table, heads):
    local_rows = linear.shape[0]
    shaped = rms_norm(linear.reshape(local_rows, heads, HEAD_SIZE), gain_vec)
    turned = shaped * cosine_table + rotate_half(shaped) * sine_table
    return turned.astype(jnp.bfloat16).reshape(local_rows, heads * HEAD_SIZE)


def head_backward_pass(grad_in, linear, gain_vec, cosine_table, sine_table, heads):
    local_rows = linear.shape[0]
    shaped = linear.reshape(local_rows, heads, HEAD_SIZE)
    upstream = grad_in.astype(jnp.float32).reshape(local_rows, heads, HEAD_SIZE)
    d_normed = upstream * cosine_table + unrotate_half(upstream * sine_table)
    d_linear, gain_part = norm_back(d_normed, shaped, gain_vec)
    return (d_linear.reshape(local_rows, heads * HEAD_SIZE).astype(jnp.bfloat16), gain_part)


def block_scores(q_block, keys_all, block_places, block_docs, places, doc_ids):
    score_scale = HEAD_SIZE ** (-0.5)
    scores = (
        jnp.einsum("qkgd,skd->kgqs", q_block, keys_all, preferred_element_type=jnp.float32)
        * score_scale
    )
    allowed = (places[None, :] <= block_places[:, None]) & (doc_ids[None, :] == block_docs[:, None])
    return jnp.where(allowed[None, None], scores, MASKED)


def attend_forward(query_rows, keys_in, values_in, places, doc_ids):
    total_length = query_rows.shape[0]
    kv_heads = keys_in.shape[1] // HEAD_SIZE
    query_group = QUERY_HEADS // KEY_VALUE_HEADS
    block_length = min(512, total_length)
    number_of_blocks = total_length // block_length
    keys_all = keys_in.reshape(total_length, kv_heads, HEAD_SIZE)
    values_all = values_in.reshape(total_length, kv_heads, HEAD_SIZE)
    grouped_queries = query_rows.reshape(
        number_of_blocks, block_length, kv_heads, query_group, HEAD_SIZE
    )

    def one_block(pieces):
        q_block, block_places, block_docs = pieces
        scores = block_scores(q_block, keys_all, block_places, block_docs, places, doc_ids)
        row_max = jnp.max(scores, axis=-1, keepdims=True)
        weights = jnp.exp(scores - row_max)
        sum_total = jnp.sum(weights, axis=-1, keepdims=True)
        soft_max = (weights / sum_total).astype(jnp.bfloat16)
        mixture = jnp.einsum(
            "kgqs,skd->qkgd", soft_max, values_all, preferred_element_type=jnp.float32
        )
        return (mixture.astype(jnp.bfloat16), row_max[..., 0] + jnp.log(sum_total[..., 0]))

    mixture, log_total = lax.map(
        one_block,
        (
            grouped_queries,
            places.reshape(number_of_blocks, block_length),
            doc_ids.reshape(number_of_blocks, block_length),
        ),
    )
    return (mixture.reshape(total_length, kv_heads * query_group * HEAD_SIZE), log_total)


def attend_back(query_rows, keys_in, values_in, grad_out, log_total, places, doc_ids):
    total_length = query_rows.shape[0]
    kv_heads = keys_in.shape[1] // HEAD_SIZE
    query_group = QUERY_HEADS // KEY_VALUE_HEADS
    block_length = min(512, total_length)
    number_of_blocks = total_length // block_length
    score_scale = HEAD_SIZE ** (-0.5)
    keys_all = keys_in.reshape(total_length, kv_heads, HEAD_SIZE)
    values_all = values_in.reshape(total_length, kv_heads, HEAD_SIZE)
    grouped_queries = query_rows.reshape(
        number_of_blocks, block_length, kv_heads, query_group, HEAD_SIZE
    )
    grads_all = grad_out.reshape(number_of_blocks, block_length, kv_heads, query_group, HEAD_SIZE)

    def one_block(carried, pieces):
        key_total, value_total = carried
        q_block, g_block, block_log, block_places, block_docs = pieces
        scores = block_scores(q_block, keys_all, block_places, block_docs, places, doc_ids)
        chances = jnp.exp(scores - block_log[..., None])
        d_chances = jnp.einsum(
            "qkgd,skd->kgqs", g_block, values_all, preferred_element_type=jnp.float32
        )
        row_dots = jnp.sum(d_chances * chances, axis=-1, keepdims=True)
        d_scores = (chances * (d_chances - row_dots)).astype(jnp.bfloat16)
        d_query = (
            jnp.einsum("kgqs,skd->qkgd", d_scores, keys_all, preferred_element_type=jnp.float32)
            * score_scale
        )
        key_total = (
            key_total
            + jnp.einsum("kgqs,qkgd->skd", d_scores, q_block, preferred_element_type=jnp.float32)
            * score_scale
        )
        value_total = value_total + jnp.einsum(
            "kgqs,qkgd->skd",
            chances.astype(jnp.bfloat16),
            g_block,
            preferred_element_type=jnp.float32,
        )
        return ((key_total, value_total), d_query)

    zero_kv = jnp.zeros((total_length, kv_heads, HEAD_SIZE), jnp.float32)
    inputs_scan = (
        grouped_queries,
        grads_all,
        log_total,
        places.reshape(number_of_blocks, block_length),
        doc_ids.reshape(number_of_blocks, block_length),
    )
    (key_total, value_total), d_query = lax.scan(one_block, (zero_kv, zero_kv), inputs_scan)
    return (
        d_query.reshape(total_length, kv_heads * query_group * HEAD_SIZE).astype(jnp.bfloat16),
        key_total.reshape(total_length, kv_heads * HEAD_SIZE).astype(jnp.bfloat16),
        value_total.reshape(total_length, kv_heads * HEAD_SIZE).astype(jnp.bfloat16),
    )


def on_device(
    inputs,
    doc_starts,
    cotangent,
    attn_gain,
    w_query,
    key_projection_weight,
    value_projection_weight,
    q_gain,
    k_gain,
    w_out,
    ffn_gain,
    w_gate,
    w_up,
    w_down,
):
    local_rows = inputs.shape[0]
    seq_parts = lax.axis_size("seq")
    total_length = local_rows * seq_parts
    row_starts = doc_starts[0]
    local_places = lax.axis_index("seq") * local_rows + jnp.arange(local_rows, dtype=jnp.int32)
    unused_docs, cosine_table, sine_table = row_layout(row_starts, local_places)
    cosine_table = cosine_table[:, None, :]
    sine_table = sine_table[:, None, :]
    all_places = jnp.arange(total_length, dtype=jnp.int32)
    all_docs = jnp.sum((all_places[:, None] >= row_starts[None, :]).astype(jnp.int32), axis=1) - 1
    q_scale = q_gain.astype(jnp.float32)
    key_norm_scale = k_gain.astype(jnp.float32)
    attn_scale, query_full, key_full, value_full, out_full = (
        lax.all_gather(attn_gain, ("dp", "seq"), axis=0, tiled=True),
        lax.all_gather(w_query, ("dp", "seq"), axis=0, tiled=True),
        lax.all_gather(key_projection_weight, ("dp", "seq"), axis=0, tiled=True),
        lax.all_gather(value_projection_weight, ("dp", "seq"), axis=0, tiled=True),
        lax.all_gather(w_out, ("dp", "seq"), axis=0, tiled=True),
    )
    source = inputs.astype(jnp.float32)
    normalized_input = rms_norm(source, attn_scale.astype(jnp.float32)).astype(jnp.bfloat16)
    q_linear = jnp.dot(normalized_input, query_full, preferred_element_type=jnp.float32)
    key_linear_output = jnp.dot(normalized_input, key_full, preferred_element_type=jnp.float32)
    q_sent = head_forward_pass(q_linear, q_scale, cosine_table, sine_table, QUERY_HEADS)
    key_sent_rows = head_forward_pass(
        key_linear_output, key_norm_scale, cosine_table, sine_table, KEY_VALUE_HEADS
    )
    v_sent = jnp.dot(normalized_input, value_full, preferred_element_type=jnp.float32).astype(
        jnp.bfloat16
    )
    q_heads, k_heads, v_heads = (
        lax.all_to_all(q_sent, "seq", split_axis=1, concat_axis=0, tiled=True),
        lax.all_to_all(key_sent_rows, "seq", split_axis=1, concat_axis=0, tiled=True),
        lax.all_to_all(v_sent, "seq", split_axis=1, concat_axis=0, tiled=True),
    )
    mixture, log_total = attend_forward(q_heads, k_heads, v_heads, all_places, all_docs)
    attended = lax.all_to_all(mixture, "seq", split_axis=0, concat_axis=1, tiled=True)
    middle = source + jnp.dot(attended, out_full, preferred_element_type=jnp.float32)
    ffn_scale, gate_full, up_full, down_full = (
        lax.all_gather(ffn_gain, ("dp", "seq"), axis=0, tiled=True),
        lax.all_gather(w_gate, ("dp", "seq"), axis=0, tiled=True),
        lax.all_gather(w_up, ("dp", "seq"), axis=0, tiled=True),
        lax.all_gather(w_down, ("dp", "seq"), axis=0, tiled=True),
    )
    normed_mid = rms_norm(middle, ffn_scale.astype(jnp.float32)).astype(jnp.bfloat16)
    gate_lin = jnp.dot(normed_mid, gate_full, preferred_element_type=jnp.float32)
    upward = jnp.dot(normed_mid, up_full, preferred_element_type=jnp.float32)
    sigmoid_gate = jax.nn.sigmoid(gate_lin)
    swish = gate_lin * sigmoid_gate
    active = (swish * upward).astype(jnp.bfloat16)
    output = (middle + jnp.dot(active, down_full, preferred_element_type=jnp.float32)).astype(
        jnp.bfloat16
    )
    ffn_scale, gate_full, up_full, down_full = (
        lax.all_gather(ffn_gain, ("dp", "seq"), axis=0, tiled=True),
        lax.all_gather(w_gate, ("dp", "seq"), axis=0, tiled=True),
        lax.all_gather(w_up, ("dp", "seq"), axis=0, tiled=True),
        lax.all_gather(w_down, ("dp", "seq"), axis=0, tiled=True),
    )
    d_active = lax.dot_general(
        cotangent, down_full, CONTRACT_COLS, preferred_element_type=jnp.float32
    )
    d_gate = (d_active * upward * (sigmoid_gate * (1.0 + gate_lin * (1.0 - sigmoid_gate)))).astype(
        jnp.bfloat16
    )
    d_up = (d_active * swish).astype(jnp.bfloat16)
    d_normed_mid = lax.dot_general(
        d_gate, gate_full, CONTRACT_COLS, preferred_element_type=jnp.float32
    )
    d_normed_mid = d_normed_mid + lax.dot_general(
        d_up, up_full, CONTRACT_COLS, preferred_element_type=jnp.float32
    )
    d_middle_norm, ffn_gain_part = norm_back(d_normed_mid, middle, ffn_scale.astype(jnp.float32))
    d_middle = cotangent.astype(jnp.float32) + d_middle_norm
    d_branch = d_middle.astype(jnp.bfloat16)
    attn_scale, query_full, key_full, value_full, out_full = (
        lax.all_gather(attn_gain, ("dp", "seq"), axis=0, tiled=True),
        lax.all_gather(w_query, ("dp", "seq"), axis=0, tiled=True),
        lax.all_gather(key_projection_weight, ("dp", "seq"), axis=0, tiled=True),
        lax.all_gather(value_projection_weight, ("dp", "seq"), axis=0, tiled=True),
        lax.all_gather(w_out, ("dp", "seq"), axis=0, tiled=True),
    )
    d_attended = lax.dot_general(
        d_branch, out_full, CONTRACT_COLS, preferred_element_type=jnp.float32
    ).astype(jnp.bfloat16)
    d_mixture = lax.all_to_all(d_attended, "seq", split_axis=1, concat_axis=0, tiled=True)
    d_q_heads, d_k_heads, d_v_heads = attend_back(
        q_heads, k_heads, v_heads, d_mixture, log_total, all_places, all_docs
    )
    d_q_sent, key_sent_gradient, d_v_sent = (
        lax.all_to_all(d_q_heads, "seq", split_axis=0, concat_axis=1, tiled=True),
        lax.all_to_all(d_k_heads, "seq", split_axis=0, concat_axis=1, tiled=True),
        lax.all_to_all(d_v_heads, "seq", split_axis=0, concat_axis=1, tiled=True),
    )
    d_q_linear, q_gain_part = head_backward_pass(
        d_q_sent, q_linear, q_scale, cosine_table, sine_table, QUERY_HEADS
    )
    key_linear_gradient, key_gain_piece = head_backward_pass(
        key_sent_gradient,
        key_linear_output,
        key_norm_scale,
        cosine_table,
        sine_table,
        KEY_VALUE_HEADS,
    )
    d_normed = lax.dot_general(
        d_q_linear, query_full, CONTRACT_COLS, preferred_element_type=jnp.float32
    )
    d_normed = d_normed + lax.dot_general(
        key_linear_gradient, key_full, CONTRACT_COLS, preferred_element_type=jnp.float32
    )
    d_normed = d_normed + lax.dot_general(
        d_v_sent, value_full, CONTRACT_COLS, preferred_element_type=jnp.float32
    )
    d_source_norm, attn_gain_part = norm_back(d_normed, source, attn_scale.astype(jnp.float32))
    input_grad = d_middle + d_source_norm
    attn_columns = jnp.concatenate([d_q_linear, key_linear_gradient, d_v_sent], axis=1)
    ffn_columns = jnp.concatenate([d_gate, d_up], axis=1)
    left = normalized_input
    first_part = lax.dot_general(
        left, attn_columns, CONTRACT_ROWS, preferred_element_type=jnp.float32
    )
    second_part = lax.dot_general(
        normed_mid, ffn_columns, CONTRACT_ROWS, preferred_element_type=jnp.float32
    )
    width_sums = lax.psum_scatter(
        jnp.concatenate([first_part, second_part], axis=1),
        ("dp", "seq"),
        scatter_dimension=0,
        tiled=True,
    )
    left = attended
    out_grad = lax.psum_scatter(
        lax.dot_general(left, d_branch, CONTRACT_ROWS, preferred_element_type=jnp.float32),
        ("dp", "seq"),
        scatter_dimension=0,
        tiled=True,
    )
    left = active
    down_grad = lax.psum_scatter(
        lax.dot_general(left, cotangent, CONTRACT_ROWS, preferred_element_type=jnp.float32),
        ("dp", "seq"),
        scatter_dimension=0,
        tiled=True,
    )
    attn_gain_grad, ffn_gain_grad = (
        lax.psum_scatter(attn_gain_part, ("dp", "seq"), scatter_dimension=0, tiled=True),
        lax.psum_scatter(ffn_gain_part, ("dp", "seq"), scatter_dimension=0, tiled=True),
    )
    q_gain_grad, k_gain_grad = lax.psum((q_gain_part, key_gain_piece), ("dp", "seq"))
    q_cols = QUERY_HEADS * HEAD_SIZE
    kv_cols = KEY_VALUE_HEADS * HEAD_SIZE
    query_grad = width_sums[:, :q_cols]
    key_grad = width_sums[:, q_cols : q_cols + kv_cols]
    value_grad = width_sums[:, q_cols + kv_cols : q_cols + 2 * kv_cols]
    gate_grad = width_sums[:, q_cols + 2 * kv_cols : q_cols + 2 * kv_cols + FF]
    up_grad = width_sums[:, q_cols + 2 * kv_cols + FF :]
    return (
        output,
        input_grad,
        attn_gain_grad,
        query_grad,
        key_grad,
        value_grad,
        q_gain_grad,
        k_gain_grad,
        out_grad,
        ffn_gain_grad,
        gate_grad,
        up_grad,
        down_grad,
    )


BF = jnp.bfloat16
F32 = jnp.float32
MESH = pl.DeviceIdType.MESH
SEQ = 4
PLANES = 4
TOK = 256
WIDTH = 1024
ROW = 1024
OWN_Q = 256
OWN_K = 128
QKV = 512
FF_OWN = 1152
FF_SHARD = 144
HIDDEN_TWO = 2304
DOWN_A = 80
DOWN_B = 64
SUM_A = 80
SUM_B = 64


def flip(value, bit):
    return value + bit - 2 * bit * lax.rem(lax.div(value, bit), 2)


def dot(left, right):
    return lax.dot_general(left, right, (((1,), (0,)), ((), ())), preferred_element_type=F32)


def dot_nt(left, right):
    return lax.dot_general(left, right, (((1,), (1,)), ((), ())), preferred_element_type=F32)


def dot_tn(left, right):
    return lax.dot_general(left, right, (((0,), (0,)), ((), ())), preferred_element_type=F32)


class Links:
    def __init__(self, send_sems, recv_sems, local_sems):
        self.send_sems, self.recv_sems, self.local_sems = send_sems, recv_sems, local_sems
        self.column_copies = 0
        self.row_copies = COLUMN_COPIES
        self.local_copies = []
        self.open = []
        self.late = []
        self.dp = lax.axis_index("dp")
        self.s = lax.axis_index("seq")
        self.s1 = flip(self.s, 1)
        self.s2 = flip(self.s, 2)
        self.s3 = flip(self.s1, 2)
        self.others = (self.s1, self.s2, self.s3)
        self.y = lax.rem(self.dp, 2)
        self.z = lax.div(self.dp, 2)
        self.y_peer = flip(self.dp, 1)
        z1 = flip(self.z, 1)
        self.planes = (z1, flip(self.z, 2), flip(z1, 2))
        self.z_peers = tuple(2 * z + self.y for z in self.planes)

    def greet(self, semaphore, partners):
        for place in partners:
            pl.semaphore_signal(semaphore, inc=1, device_id=place, device_id_type=MESH)

    def column(self):
        return [(p, self.s) for p in (self.y_peer,) + self.z_peers]

    def everyone(self):
        return [(self.dp, s) for s in self.others] + self.column()

    def plan(self, src, dst, dp=None, s=None):
        if dp is None:
            n = self.row_copies
            self.row_copies += 1
        else:
            n = self.column_copies
            self.column_copies += 1
        copy = pltpu.make_async_remote_copy(
            src_ref=src,
            dst_ref=dst,
            send_sem=self.send_sems.at[n],
            recv_sem=self.recv_sems.at[n],
            device_id=(self.dp if dp is None else dp, self.s if s is None else s),
            device_id_type=MESH,
        )
        return copy

    def push(self, src, dst, dp=None, s=None, when=None, late=False):
        copy = self.plan(src, dst, dp, s)
        if when is None:
            copy.start()
        else:
            pl.when(when)(copy.start)
        (self.late if late else self.open).append((copy, when))
        return copy

    def start_over(self):
        self.column_copies = 0

    def keep(self, src, dst):
        copy = pltpu.make_async_copy(src, dst, self.local_sems.at[len(self.local_copies)])
        copy.start()
        self.local_copies.append(copy)
        return copy

    def settle(self, copies):
        for copy in copies:
            copy.wait_send()
        self.open = [item for item in self.open if all(item[0] is not copy for copy in copies)]

    def drain_late(self):
        self.open, self.late = self.late, []
        self.drain()

    def drain(self):
        for copy, when in self.open:
            if when is None:
                copy.wait_send()
            else:
                pl.when(when)(copy.wait_send)
        self.open = []


class Line:
    def __init__(self, links, view):
        self.links, self.view = links, view
        self.hops = []

    def pass_on(self, step):
        l = self.links
        below, above = l.z - step, l.z + step
        low = self.view(jnp.maximum(below, 0))
        high = self.view(jnp.minimum(above, PLANES - 1))
        up = l.push(
            low, low, dp=jnp.minimum(l.dp + 2, 2 * PLANES - 1), when=(below >= 0) & (l.z < PLANES - 1)
        )
        down = l.push(high, high, dp=jnp.maximum(l.dp - 2, 0), when=(above <= PLANES - 1) & (l.z > 0))
        self.hops.append((up, down))

    def start(self):
        self.pass_on(0)

    def step(self, k):
        l = self.links
        below, above = l.z - 1 - k, l.z + 1 + k
        from_below, from_above = below >= 0, above <= PLANES - 1
        pl.when(from_below)(self.hops[k][0].wait_recv)
        pl.when(from_above)(self.hops[k][1].wait_recv)
        if k < PLANES - 2:
            self.pass_on(k + 1)
        return [
            (from_below, self.view(jnp.maximum(below, 0))),
            (from_above, self.view(jnp.minimum(above, PLANES - 1))),
        ]


class Gather:
    def __init__(self, links, view):
        self.links = links
        self.line = Line(links, lambda z: view(2 * z + links.y))
        self.own = view(links.dp)
        self.over_y = []

    def start_y(self):
        self.over_y.append((None, self.links.push(self.own, self.own, dp=self.links.y_peer)))

    def start_z(self):
        self.line.start()

    def step(self, k):
        for when, block in self.line.step(k):
            copy = self.links.push(block, block, dp=self.links.y_peer, when=when)
            self.over_y.append((when, copy))

    def finish(self):
        for when, copy in self.over_y:
            if when is None:
                copy.wait_recv()
            else:
                pl.when(when)(copy.wait_recv)


class PairGather:
    def __init__(self, links, view):
        self.links = links
        self.near = Line(links, lambda z: view(2 * z + links.y))
        self.far = Line(links, lambda z: view(2 * z + 1 - links.y))
        self.own = view(links.dp)

    def start_y(self):
        self.over_y = self.links.push(self.own, self.own, dp=self.links.y_peer)

    def start_z(self):
        self.near.start()

    def join(self):
        self.over_y.wait_recv()
        self.far.start()

    def step(self, k):
        self.near.step(k)
        self.far.step(k)


class Chain:
    def __init__(self, links, view, slots):
        self.links, self.view, self.slots = links, view, slots
        self.up, self.down = {}, {}

    def start(self):
        l = self.links
        last = PLANES - 1
        for d in range(PLANES):
            if d > 0:
                self.up[d] = l.plan(self.view(d), self.slots(d), dp=jnp.minimum(l.dp + 2, 2 * last + 1))
            if d < last:
                place = jnp.where(l.z == d + 1, PLANES, d)
                self.down[d] = l.plan(self.view(d), self.slots(place), dp=jnp.maximum(l.dp - 2, 0))

    def add(self, d, copy):
        copy.wait_recv()
        block = self.view(d)
        block[...] = (block[...].astype(F32) + self.slots(d)[...].astype(F32)).astype(BF)

    def step(self, j):
        last = PLANES - 1

        @pl.when(self.links.z == j)
        def _():
            for d in range(last, j, -1):
                if j > 0:
                    self.add(d, self.up[d])
                self.up[d].start()

        @pl.when(self.links.z == last - j)
        def _():
            for d in range(last - j):
                if j > 0:
                    self.add(d, self.down[d])
                self.down[d].start()

        for d in range(PLANES):
            if d > j:
                self.links.late.append((self.up[d], self.links.z == j))
            if d < last - j:
                self.links.late.append((self.down[d], self.links.z == last - j))

    def total(self):
        l = self.links
        for d in range(PLANES):
            if d > 0:
                pl.when(l.z == d)(self.up[d].wait_recv)
            if d < PLANES - 1:
                pl.when(l.z == d)(self.down[d].wait_recv)
        own = self.view(l.z)[...].astype(F32)
        below = jnp.where(l.z > 0, self.slots(l.z)[...].astype(F32), 0.0)
        above = jnp.where(l.z < PLANES - 1, self.slots(PLANES)[...].astype(F32), 0.0)
        return own + (below + above)


class Scatter:
    def __init__(self, links, view, y_slots, z_slots):
        self.links, self.view, self.y_slots = links, view, y_slots
        self.chain = Chain(links, lambda z: view(2 * z + links.y), z_slots)

    def start(self):
        l = self.links
        self.order = [jnp.where(l.z < PLANES // 2, PLANES - 1 - k, k) for k in range(PLANES)]
        self.over_y = [
            l.push(self.view(2 * d + 1 - l.y), self.y_slots(k), dp=l.y_peer, late=True) for k, d in enumerate(self.order)
        ]
        self.chain.start()

    def join(self):
        for k, copy in enumerate(self.over_y):
            copy.wait_recv()
            block = self.view(2 * self.order[k] + self.links.y)
            block[...] = (block[...].astype(F32) + self.y_slots(k)[...].astype(F32)).astype(BF)

    def step(self, j):
        self.chain.step(j)

    def total(self):
        return self.chain.total()


class PairScatter:
    def __init__(self, links, view, y_slot, near_slots, far_slots):
        self.links, self.view, self.y_slot = links, view, y_slot
        self.near = Chain(links, lambda z: view(2 * z + links.y), near_slots)
        self.far = Chain(links, lambda z: view(2 * z + 1 - links.y), far_slots)

    def start(self):
        self.far.start()
        self.near.start()

    def step(self, j):
        self.far.step(j)
        self.near.step(j)

    def cross(self):
        l = self.links
        block = self.view(2 * l.z + 1 - l.y)
        block[...] = self.far.total().astype(BF)
        self.over_y = l.push(block, self.y_slot, dp=l.y_peer, late=True)

    def total(self):
        own = self.near.total()
        self.over_y.wait_recv()
        return own + self.y_slot[...].astype(F32)


class RowSum:
    def __init__(self, links, slots):
        self.links, self.slots = links, slots

    def hand_over(self, src):
        self.first = self.links.push(src, self.slots.at[0], s=self.links.s1)

    def cross(self, src):
        self.first.wait_recv()
        src[...] = (src[...].astype(F32) + self.slots[0].astype(F32).reshape(src.shape)).astype(BF)
        self.second = self.links.push(src, self.slots.at[1], s=self.links.s2)

    def near(self, src):
        self.third = self.links.push(src, self.slots.at[2], s=self.links.s1)

    def total(self, own):
        self.third.wait_recv()
        self.second.wait_recv()
        return own + self.slots[1].astype(F32).reshape(own.shape) + self.slots[2].astype(F32).reshape(own.shape)


def lane_masks(rows):
    lane = lax.broadcasted_iota(jnp.int32, (rows, 128), 1)
    return lane < 64, lax.rem(lane, 64) < 32


def turned(values, low):
    return jnp.where(low, -pltpu.roll(values, 96, 1), pltpu.roll(values, 32, 1))


def unturned(values, low):
    return jnp.where(low, pltpu.roll(values, 96, 1), -pltpu.roll(values, 32, 1))


def per_head_mean(values, first):
    left = jnp.sum(jnp.where(first, values, 0.0), axis=-1, keepdims=True)
    right = jnp.sum(jnp.where(first, 0.0, values), axis=-1, keepdims=True)
    return jnp.where(first, left, right) * (1.0 / HEAD_SIZE)


def norm_rope(values, gain, cosine, sine, first, low):
    normed = values * lax.rsqrt(per_head_mean(values * values, first) + EPS) * gain
    return normed * cosine + turned(normed, low) * sine


def norm_rope_back(upstream, values, gain, cosine, sine, first, low):
    d_normed = upstream * cosine + unturned(upstream * sine, low)
    inverse = lax.rsqrt(per_head_mean(values * values, first) + EPS)
    unit = values * inverse
    scaled = d_normed * gain
    d_values = inverse * (scaled - unit * per_head_mean(scaled * unit, first))
    return d_values, jnp.sum(d_normed * unit, axis=0, keepdims=True)


def allowed_block(r, block, keys):
    query = lax.broadcasted_iota(jnp.int32, (TOK, keys), 0) + block * TOK
    key = lax.broadcasted_iota(jnp.int32, (TOK, keys), 1)
    place = lax.broadcasted_iota(jnp.int32, (TOK, 1), 0) + block * TOK
    begin = jnp.zeros((TOK, 1), jnp.int32)
    for k in range(4):
        start = r.doc_starts[0, k]
        begin = jnp.maximum(begin, jnp.where(place >= start, start, 0))
    return (key <= query) & (key >= begin)


SCORE_SCALE = HEAD_SIZE ** (-0.5)


def attention_block(r, pair, block):
    keys = (block + 1) * TOK
    rows = pl.ds(block * TOK, TOK)
    queries = r.q_heads[pair, :, rows, :].reshape(2 * TOK, HEAD_SIZE)
    scores = dot_nt(queries, r.k_heads[pair, :keys, :]).reshape(2, TOK, keys) * SCORE_SCALE
    scores = jnp.where(allowed_block(r, block, keys)[None], scores, MASKED)
    top = jnp.max(scores, axis=-1, keepdims=True)
    weights = jnp.exp(scores - top)
    total = jnp.sum(weights, axis=-1, keepdims=True)
    mixed = dot(weights.astype(BF).reshape(2 * TOK, keys), r.v_heads[pair, :keys, :])
    mixed = mixed.reshape(2, TOK, HEAD_SIZE) / total
    log_total = top + jnp.log(total)
    r.log_total[rows, 2 * pair : 2 * pair + 1] = log_total[0]
    r.log_total[rows, 2 * pair + 1 : 2 * pair + 2] = log_total[1]
    r.att_own[block, :, pair * 128 : (pair + 1) * 128] = jnp.concatenate(
        [mixed[0], mixed[1]], axis=-1
    ).astype(BF)


def attention_block_back(r, pair, block):
    keys = (block + 1) * TOK
    rows = pl.ds(block * TOK, TOK)
    queries = r.q_heads[pair, :, rows, :].reshape(2 * TOK, HEAD_SIZE)
    grads = r.d_att_rows[block, :, pair * 128 : (pair + 1) * 128]
    grads = jnp.concatenate([grads[:, :HEAD_SIZE], grads[:, HEAD_SIZE:]], axis=0)
    keys_in, values_in = r.k_heads[pair, :keys, :], r.v_heads[pair, :keys, :]
    scores = dot_nt(queries, keys_in).reshape(2, TOK, keys) * SCORE_SCALE
    log_total = jnp.stack([r.log_total[rows, 2 * pair + g : 2 * pair + g + 1] for g in range(2)])
    chances = jnp.exp(scores - log_total)
    chances = jnp.where(allowed_block(r, block, keys)[None], chances, 0.0)
    d_chances = dot_nt(grads, values_in).reshape(2, TOK, keys)
    row_dots = jnp.sum(d_chances * chances, axis=-1, keepdims=True)
    d_scores = (chances * (d_chances - row_dots)).astype(BF).reshape(2 * TOK, keys)
    d_query = (dot(d_scores, keys_in) * SCORE_SCALE).astype(BF)
    r.d_query[rows, pair * 128 : (pair + 1) * 128] = jnp.concatenate(
        [d_query[:TOK], d_query[TOK:]], axis=-1
    )
    d_key = dot_tn(d_scores, queries) * SCORE_SCALE
    d_value = dot_tn(chances.astype(BF).reshape(2 * TOK, keys), grads)
    if block == ROW // TOK - 1:
        r.d_kv[pair, :, :HEAD_SIZE] = d_key
        r.d_kv[pair, :, HEAD_SIZE:] = d_value
    else:
        r.d_kv[pair, :keys, :HEAD_SIZE] += d_key
        r.d_kv[pair, :keys, HEAD_SIZE:] += d_value


def norm_back_unit(upstream, values):
    inverse = lax.rsqrt(jnp.mean(values * values, axis=-1, keepdims=True) + EPS)
    unit = values * inverse
    d_values = inverse * (
        upstream - unit * jnp.mean(upstream * unit, axis=-1, keepdims=True)
    )
    return d_values, jnp.sum(upstream * unit, axis=0, keepdims=True)


def unit_norm(values):
    return values * lax.rsqrt(jnp.mean(values * values, axis=-1, keepdims=True) + EPS)


def as_row(vector):
    return vector[...].astype(F32).reshape(1, vector.shape[0])


def twice(vector):
    row = as_row(vector)
    return jnp.concatenate([row, row], axis=1)


def column(row):
    n = row.shape[1]
    same = lax.broadcasted_iota(jnp.int32, (n, n), 0) == lax.broadcasted_iota(jnp.int32, (n, n), 1)
    return jnp.sum(jnp.where(same, row, 0.0), axis=1, keepdims=True)


def own_parts(r):
    scale = column(as_row(r.attn_gain))
    for o in range(SEQ):
        for ref, first, size in ((r.wq, 0, OWN_Q), (r.wk, OWN_Q, OWN_K), (r.wv, OWN_Q + OWN_K, OWN_K)):
            part = ref[:, o * size : (o + 1) * size].astype(F32) * scale
            r.w_qkv[o, :, first : first + size] = part.astype(BF)


def own_units(r):
    scale = column(as_row(r.ffn_gain))
    for ref, first in ((r.wg, 0), (r.wu, FF_OWN)):
        scaled = ref[...].astype(F32) * scale
        for o in range(SEQ):
            parts = [scaled[:, (4 * j + o) * FF_SHARD : (4 * j + o + 1) * FF_SHARD] for j in range(8)]
            r.d_gu[32 + o, :, first : first + FF_OWN] = jnp.concatenate(parts, axis=1).astype(BF)


def rotation_tables(r, half):
    size = ROW // 2
    rows = pl.ds(half * size, size)
    place = lax.broadcasted_iota(jnp.int32, (size, 1), 0) + half * size
    begin = jnp.zeros((size, 1), jnp.int32)
    for k in range(4):
        start = r.doc_starts[0, k]
        begin = jnp.maximum(begin, jnp.where(place >= start, start, 0))
    angles = (place - begin).astype(F32) * r.frequency[...]
    r.cosine[rows, :] = jnp.cos(angles)
    r.sine[rows, :] = jnp.sin(angles)


def head_forward(r):
    first, low = lane_masks(TOK)

    @pl.loop(0, SEQ)
    def _(t):
        rows = pl.ds(pl.multiple_of(t * TOK, TOK), TOK)
        linear = dot(r.u_rows[t], r.qkv_all[...].reshape(WIDTH, QKV))
        r.q_linear[rows, :] = linear[:, :OWN_Q]
        r.k_linear[rows, :] = linear[:, OWN_Q : OWN_Q + OWN_K]
        cosine, sine = r.cosine[rows, :], r.sine[rows, :]
        for pair in range(2):
            part = linear[:, pair * 128 : (pair + 1) * 128]
            part = norm_rope(part, twice(r.q_gain), cosine, sine, first, low).astype(BF)
            r.q_heads[pair, 0, rows, :] = part[:, :HEAD_SIZE]
            r.q_heads[pair, 1, rows, :] = part[:, HEAD_SIZE:]
        part = linear[:, OWN_Q : OWN_Q + OWN_K]
        part = norm_rope(part, twice(r.k_gain), cosine, sine, first, low).astype(BF)
        r.k_heads[0, rows, :] = part[:, :HEAD_SIZE]
        r.k_heads[1, rows, :] = part[:, HEAD_SIZE:]
        part = linear[:, OWN_Q + OWN_K :].astype(BF)
        r.v_heads[0, rows, :] = part[:, :HEAD_SIZE]
        r.v_heads[1, rows, :] = part[:, HEAD_SIZE:]


def head_backward(r):
    first, low = lane_masks(TOK)
    r.head_gain_part[...] = jnp.zeros((2, 128), F32)

    @pl.loop(0, SEQ)
    def _(t):
        rows = pl.ds(pl.multiple_of(t * TOK, TOK), TOK)
        cosine, sine = r.cosine[rows, :], r.sine[rows, :]
        for pair in range(2):
            cols = slice(pair * 128, (pair + 1) * 128)
            up = r.d_query[rows, cols].astype(F32)
            back, gain_part = norm_rope_back(up, r.q_linear[rows, cols], twice(r.q_gain), cosine, sine, first, low)
            r.d_qkv[rows, cols] = back.astype(BF)
            r.head_gain_part[0:1] += gain_part
        up = jnp.concatenate([r.d_kv[0, rows, :HEAD_SIZE], r.d_kv[1, rows, :HEAD_SIZE]], axis=-1)
        up = up.astype(BF).astype(F32)
        back, gain_part = norm_rope_back(up, r.k_linear[rows, :], twice(r.k_gain), cosine, sine, first, low)
        r.d_qkv[rows, OWN_Q : OWN_Q + OWN_K] = back.astype(BF)
        r.head_gain_part[1:2] += gain_part
        up = jnp.concatenate([r.d_kv[0, rows, HEAD_SIZE:], r.d_kv[1, rows, HEAD_SIZE:]], axis=-1)
        r.d_qkv[rows, OWN_Q + OWN_K :] = up.astype(BF)


def units_up(r, t):
    gate_up = dot(r.mid_rows[t], r.gu_all[...].reshape(WIDTH, HIDDEN_TWO))
    gate, up = gate_up[:, :FF_OWN], gate_up[:, FF_OWN:]
    sigmoid = 1.0 / (1.0 + jnp.exp(-gate))
    swish = gate * sigmoid
    r.active[t] = (swish * up).astype(BF)
    blocks = pl.ds(8 * t, 8)
    by_gate = up * (sigmoid * (1.0 + gate * (1.0 - sigmoid)))
    r.d_gu[blocks, :, :FF_OWN] = by_gate.astype(BF).reshape(8, 32, FF_OWN)
    r.d_gu[blocks, :, FF_OWN:] = swish.astype(BF).reshape(8, 32, FF_OWN)


def units_down(r, t):
    d_active = dot_nt(r.cot_rows[t], r.down_all[...].reshape(FF_OWN, WIDTH)).reshape(8, 32, FF_OWN)
    blocks = pl.ds(8 * t, 8)
    r.d_gu[blocks, :, :FF_OWN] = (d_active * r.d_gu[blocks, :, :FF_OWN].astype(F32)).astype(BF)
    r.d_gu[blocks, :, FF_OWN:] = (d_active * r.d_gu[blocks, :, FF_OWN:].astype(F32)).astype(BF)
    d_gu = r.d_gu[blocks].reshape(TOK, HIDDEN_TWO)
    return dot_nt(d_gu, r.gu_all[...].reshape(WIDTH, HIDDEN_TWO))


def whole_block(r):
    l = r.links = Links(r.send_sems, r.recv_sems, r.local_sems)
    l.greet(pltpu.get_barrier_semaphore(), l.everyone())
    read = [l.keep(src, dst) for src, dst in ((r.inputs, r.x_own), (r.w_query, r.wq), (r.w_key, r.wk), (r.w_value, r.wv))]
    read_units = [l.keep(r.w_gate, r.wg), l.keep(r.w_up, r.wu)]
    read_own = [
        l.keep(r.w_out, r.out_all.at[l.dp, l.s]),
        l.keep(r.w_down, r.down_all.at[l.dp]),
        l.keep(r.cotangent, r.cot_rows.at[l.s]),
    ]
    for copy in read:
        copy.wait()
    own_parts(r)
    r.qkv_all[l.dp, l.s] = r.w_qkv[l.s]
    x = r.x_own[...].astype(F32)
    r.u_rows[l.s] = unit_norm(x).astype(BF)
    for copy in read_units:
        copy.wait()
    own_units(r)
    r.gu_all[l.dp, l.s] = r.d_gu[32 + l.s]
    for copy in read_own:
        copy.wait()
    pl.semaphore_wait(pltpu.get_barrier_semaphore(), len(l.everyone()))
    out = PairGather(l, lambda b: r.out_all.at[b, l.s])
    qkv = Gather(l, lambda b: r.qkv_all.at[b])
    gate_up = [Gather(l, lambda b, g=g: r.gu_all.at[b, g]) for g in (l.s,) + l.others]
    down_a = Gather(l, lambda b: r.down_all.at[b, pl.ds(0, DOWN_A)])
    down_b = PairGather(l, lambda b: r.down_all.at[b, pl.ds(DOWN_A, DOWN_B)])
    qkv_cols = [l.push(r.w_qkv.at[o], r.qkv_all.at[l.dp, l.s], s=o) for o in l.others]
    out.start_y()
    u_far = l.push(r.u_rows.at[l.s], r.u_rows.at[l.s], s=l.s2)
    u_near = l.push(r.u_rows.at[l.s], r.u_rows.at[l.s], s=l.s1)
    gate_up[0].start_y()
    gate_up[0].start_z()
    down_b.start_y()
    for copy in qkv_cols:
        copy.wait_recv()
    qkv.start_z()
    out.start_z()
    rotation_tables(r, 0)
    out.join()
    qkv.step(0)
    qkv.start_y()
    gu_cols = [l.push(r.d_gu.at[32 + o], r.gu_all.at[l.dp, l.s], s=o) for o in l.others]
    down_b.start_z()
    qkv.step(1)
    gate_up[0].step(0)
    out.step(0)
    u_far.wait_recv()
    u_more = l.push(r.u_rows.at[l.s2], r.u_rows.at[l.s2], s=l.s1)
    qkv.step(2)
    gu_cols[1].wait_recv()
    gu_cols[2].wait_recv()
    u_near.wait_recv()
    u_more.wait_recv()
    gu_cols[0].wait_recv()
    gate_up[1].start_y()
    out.step(1)
    gate_up[1].start_z()
    gate_up[0].step(1)
    rotation_tables(r, 1)
    gate_up[2].start_y()
    qkv.finish()
    head_forward(r)
    gate_up[3].start_y()
    gate_up[1].step(0)
    out.step(2)
    attention_block(r, 0, 3)
    out_far = l.push(r.out_all.at[:, l.s], r.out_all.at[:, l.s], s=l.s2)
    out_near = l.push(r.out_all.at[:, l.s], r.out_all.at[:, l.s], s=l.s1)
    gate_up[3].start_z()
    gate_up[2].start_z()
    attention_block(r, 1, 3)
    gate_up[0].step(2)
    attention_block(r, 0, 2)
    attention_block(r, 1, 2)
    gate_up[3].step(0)
    attention_block(r, 0, 1)
    gate_up[1].step(1)
    attention_block(r, 1, 1)
    attention_block(r, 0, 0)
    attention_block(r, 1, 0)
    att = [l.push(r.att_own.at[o], r.att_local.at[l.s], s=o) for o in l.others]
    r.att_local[l.s] = r.att_own[l.s]
    gate_up[0].finish()
    out_far.wait_recv()
    out_more = l.push(r.out_all.at[:, l.s2], r.out_all.at[:, l.s2], s=l.s1)
    gate_up[3].step(1)
    gate_up[2].step(0)
    down_a.start_z()
    gate_up[1].step(2)
    out_near.wait_recv()
    out_more.wait_recv()
    for copy in att:
        copy.wait_recv()
    middle = x
    for part in range(SEQ):
        rows = r.out_all[part * 2 : (part + 1) * 2].reshape(OWN_Q, WIDTH)
        middle = middle + dot(r.att_local[part], rows)
    r.middle[...] = middle
    r.mid_rows[l.s] = unit_norm(middle).astype(BF)
    mid_far = l.push(r.mid_rows.at[l.s], r.mid_rows.at[l.s], s=l.s2)
    mid_near = l.push(r.mid_rows.at[l.s], r.mid_rows.at[l.s], s=l.s1)
    gate_up[2].step(1)
    down_b.join()
    gate_up[3].step(2)
    gate_up[2].step(2)
    down_a.start_y()
    down_a.step(0)
    cot_far = l.push(r.cot_rows.at[l.s], r.cot_rows.at[l.s], s=l.s2)
    cot_near = l.push(r.cot_rows.at[l.s], r.cot_rows.at[l.s], s=l.s1)
    down_a.step(1)
    mid_far.wait_recv()
    mid_more = l.push(r.mid_rows.at[l.s2], r.mid_rows.at[l.s2], s=l.s1)
    mid_near.wait_recv()
    mid_more.wait_recv()
    gate_up[2].finish()
    gate_up[3].finish()
    gate_up[1].finish()
    units_up(r, l.s3)
    down_b.step(0)
    units_up(r, l.s2)
    units_up(r, l.s1)
    down_a.step(2)
    units_up(r, l.s)
    down_b.step(1)
    cot_far.wait_recv()
    cot_more = l.push(r.cot_rows.at[l.s2], r.cot_rows.at[l.s2], s=l.s1)
    cot_near.wait_recv()
    cot_more.wait_recv()
    for t in range(SEQ):
        r.flipped[:, t * TOK : (t + 1) * TOK] = r.active[t].T
    cot = r.cot_rows[...].reshape(ROW, WIDTH)

    @pl.loop(0, 4)
    def _(k):
        rows = pl.ds(pl.multiple_of(k * 288, 32), 288)
        grad = dot(r.flipped[rows, :], cot).astype(BF)
        r.down_part[pl.ds(2 * k, 2)] = grad.reshape(2, FF_SHARD, WIDTH)

    down_a_sum = Scatter(
        l, lambda b: r.down_part.at[b, pl.ds(0, SUM_A)], lambda k: r.down_a_slots.at[k], lambda k: r.down_a_slots.at[4 + k]
    )
    down_b_sum = PairScatter(
        l,
        lambda b: r.down_part.at[b, pl.ds(SUM_A, SUM_B)],
        r.down_b_slots.at[10],
        lambda k: r.down_b_slots.at[k],
        lambda k: r.down_b_slots.at[5 + k],
    )
    d_mid = RowSum(l, r.slots_a)
    home = []
    kept = []
    down_a_sum.start()
    down_b_sum.start()
    down_b_sum.step(0)
    down_a.finish()
    down_b.step(2)
    l.drain()
    r.parts[0] = units_down(r, l.s3).astype(BF).reshape(8, 32, WIDTH)
    d_mid.hand_over(r.parts.at[0])
    r.parts[1] = units_down(r, l.s2).astype(BF).reshape(8, 32, WIDTH)
    d_mid.cross(r.parts.at[1])
    r.parts[2] = units_down(r, l.s1).astype(BF).reshape(8, 32, WIDTH)
    d_mid.near(r.parts.at[2])
    r.d_input[...] = units_down(r, l.s)
    for t in range(SEQ):
        r.flipped[:WIDTH, t * TOK : (t + 1) * TOK] = r.mid_rows[t].T
    d_gu = r.d_gu[0:32].reshape(ROW, HIDDEN_TWO)

    @pl.loop(0, 4)
    def _(k):
        rows = pl.ds(pl.multiple_of(k * 256, 256), 256)
        grad = dot(r.flipped[rows, :], d_gu).astype(BF)
        r.gu_all[pl.ds(2 * k, 2)] = grad.reshape(2, 4, 32, HIDDEN_TWO)

    l.greet(r.free, l.column())
    pl.semaphore_wait(r.free, len(l.column()))
    l.start_over()
    gu_sums = [
        Scatter(
            l,
            lambda b, g=g: r.gu_all.at[b, g],
            lambda k, n=n: r.d_gu.at[9 * n + k],
            lambda k, n=n: r.d_gu.at[9 * n + 4 + k],
        )
        for n, g in enumerate(l.others)
    ]
    own_gu_sum = PairScatter(
        l,
        lambda b: r.gu_all.at[b, l.s],
        r.d_gu.at[37],
        lambda k: r.d_gu.at[27 + k],
        lambda k: r.d_gu.at[32 + k],
    )
    down_a_sum.join()
    down_a_sum.step(0)
    down_b_sum.step(1)
    gu_sums[2].start()
    d_values, ffn_gain_part = norm_back_unit(d_mid.total(r.d_input[...]), r.middle[...])
    d_middle = r.cot_rows[l.s].astype(F32) + d_values
    r.d_input[...] = d_middle
    d_branch = d_middle.astype(BF)
    r.gains[0, 1:2, :] = ffn_gain_part
    for part in range(SEQ):
        rows = r.out_all[part * 2 : (part + 1) * 2].reshape(OWN_Q, WIDTH)
        r.att_own[part] = dot_nt(d_branch, rows).astype(BF)
    d_att = [l.push(r.att_own.at[o], r.d_att_rows.at[l.s], s=o) for o in l.others]
    r.d_att_rows[l.s] = r.att_own[l.s]
    own_gu_sum.start()
    own_gu_sum.step(0)
    for part in range(SEQ):
        grad = dot_tn(r.att_local[part], d_branch).astype(BF)
        r.out_all[2 * part : 2 * part + 2] = grad.reshape(2, 4, 32, WIDTH)
    out_row = RowSum(l, r.slots_b)
    out_row.hand_over(r.out_all.at[:, l.s3])
    out_row.cross(r.out_all.at[:, l.s2])
    out_row.near(r.out_all.at[:, l.s1])
    for copy in d_att:
        copy.wait_recv()
    l.settle((d_mid.first, d_mid.second, d_mid.third))
    gu_sums[1].start()
    gu_sums[0].start()
    down_b_sum.step(2)
    attention_block_back(r, 0, 3)
    attention_block_back(r, 1, 3)
    attention_block_back(r, 0, 2)
    attention_block_back(r, 1, 2)
    down_a_sum.step(1)
    attention_block_back(r, 0, 1)
    gu_sums[2].join()
    gu_sums[2].step(0)
    attention_block_back(r, 1, 1)
    down_b_sum.cross()
    attention_block_back(r, 0, 0)
    out_total = out_row.total(r.out_all[:, l.s].astype(F32))
    r.out_all[:, l.s] = out_total.astype(BF)
    out_sum = Scatter(
        l, lambda b: r.out_all.at[b, l.s], lambda k: r.out_slots.at[k], lambda k: r.out_slots.at[4 + k]
    )
    attention_block_back(r, 1, 0)
    own_gu_sum.step(1)
    head_backward(r)
    down_a_sum.step(2)
    d_u = RowSum(l, r.slots_a)
    weights = r.qkv_all[...].reshape(WIDTH, QKV)

    def d_u_part(t):
        return dot_nt(r.d_qkv[pl.ds(pl.multiple_of(t * TOK, TOK), TOK), :], weights)

    r.parts[0] = d_u_part(l.s3).astype(BF).reshape(8, 32, WIDTH)
    d_u.hand_over(r.parts.at[0])
    r.parts[1] = d_u_part(l.s2).astype(BF).reshape(8, 32, WIDTH)
    d_u.cross(r.parts.at[1])
    r.parts[2] = d_u_part(l.s1).astype(BF).reshape(8, 32, WIDTH)
    d_u.near(r.parts.at[2])
    own = d_u_part(l.s)
    for t in range(SEQ):
        r.flipped[:WIDTH, t * TOK : (t + 1) * TOK] = r.u_rows[t].T
    grad = dot(r.flipped[:WIDTH, :], r.d_qkv[...]).astype(BF)
    r.qkv_all[...] = grad.reshape(8, 4, 32, QKV)
    qkv_sum = Scatter(l, lambda b: r.qkv_all.at[b], lambda k: r.qkv_slots.at[k], lambda k: r.qkv_slots.at[4 + k])
    own_gu_sum.step(2)
    gu_sums[1].join()
    gu_sums[1].step(0)
    qkv_sum.start()
    gu_sums[2].step(1)
    gu_sums[1].step(1)
    gu_sums[0].join()
    gu_sums[0].step(0)
    x = r.x_own[...].astype(F32)
    d_values, attn_gain_part = norm_back_unit(d_u.total(own), x)
    r.d_input[...] += d_values
    kept.append(l.keep(r.d_input, r.input_grad))
    r.gains[0, 0:1, :] = attn_gain_part
    r.gains[0, 2:3, 0:128] = r.head_gain_part[0:1]
    r.gains[0, 2:3, 128:256] = r.head_gain_part[1:2]
    r.gains[0, 2:3, 256:] = jnp.zeros((1, WIDTH - 256), F32)
    r.gains[0, 3:8, :] = jnp.zeros((5, WIDTH), F32)
    gains = [l.push(r.gains.at[0], r.gain_slots.at[k], s=o) for k, o in enumerate(l.others)]
    l.settle((d_u.first, d_u.second, d_u.third))
    down_all = r.down_all[...].reshape(FF_OWN, WIDTH)
    last = RowSum(l, r.slots_b)
    r.parts[0] = dot(r.active[l.s3], down_all).astype(BF).reshape(8, 32, WIDTH)
    last.hand_over(r.parts.at[0])
    r.parts[1] = dot(r.active[l.s2], down_all).astype(BF).reshape(8, 32, WIDTH)
    last.cross(r.parts.at[1])
    own_gu_sum.cross()
    gu_sums[1].step(2)
    qkv_sum.join()
    qkv_sum.step(0)
    gu_sums[0].step(1)
    out_sum.start()
    gu_sums[2].step(2)
    r.parts[2] = dot(r.active[l.s1], down_all).astype(BF).reshape(8, 32, WIDTH)
    last.near(r.parts.at[2])
    own = r.middle[...] + dot(r.active[l.s], down_all)
    for copy in gains:
        copy.wait_recv()
    r.gains[1] = r.gains[0] + r.gain_slots[0] + r.gain_slots[1] + r.gain_slots[2]
    gains_y = l.push(r.gains.at[1], r.gain_slots.at[3], dp=l.y_peer)
    gu_sums[0].step(2)
    r.gu_all[l.dp, l.s2] = gu_sums[1].total().astype(BF)
    home.append(l.push(r.gu_all.at[l.dp, l.s2], r.gu_grad.at[l.s], s=l.s2))
    qkv_sum.step(1)
    out_sum.join()
    out_sum.step(0)
    r.gu_all[l.dp, l.s3] = gu_sums[2].total().astype(BF)
    home.append(l.push(r.gu_all.at[l.dp, l.s3], r.gu_grad.at[l.s], s=l.s3))
    r.down_own[0:SUM_A] = down_a_sum.total()
    kept.append(l.keep(r.down_own.at[pl.ds(0, SUM_A)], r.down_grad.at[pl.ds(0, SUM_A)]))
    qkv_sum.step(2)
    r.gu_all[l.dp, l.s] = own_gu_sum.total().astype(BF)
    kept.append(l.keep(r.gu_all.at[l.dp, l.s], r.gu_grad.at[l.s]))
    r.gu_all[l.dp, l.s1] = gu_sums[0].total().astype(BF)
    home.append(l.push(r.gu_all.at[l.dp, l.s1], r.gu_grad.at[l.s], s=l.s1))
    out_sum.step(1)
    r.output_own[...] = last.total(own).astype(BF)
    kept.append(l.keep(r.output_own, r.output))
    gains_y.wait_recv()
    r.gains[2] = r.gains[1] + r.gain_slots[3]
    gains_z = [l.push(r.gains.at[2], r.gain_slots.at[4 + k], dp=p) for k, p in enumerate(l.z_peers)]
    r.qkv_all[l.dp] = qkv_sum.total().astype(BF)
    home += [l.push(r.qkv_all.at[l.dp, o], r.qkv_grad.at[l.s], s=o) for o in l.others]
    kept.append(l.keep(r.qkv_all.at[l.dp, l.s], r.qkv_grad.at[l.s]))
    out_sum.step(2)
    r.down_own[SUM_A:] = down_b_sum.total()
    kept.append(l.keep(r.down_own.at[pl.ds(SUM_A, SUM_B)], r.down_grad.at[pl.ds(SUM_A, SUM_B)]))
    r.out_own[...] = out_sum.total()
    kept.append(l.keep(r.out_own, r.out_grad))
    for copy in gains_z + home:
        copy.wait_recv()
    for copy in kept:
        copy.wait()
    r.gain_grads[...] = r.gains[2] + r.gain_slots[4] + r.gain_slots[5] + r.gain_slots[6]
    l.drain()
    l.drain_late()


def own_lanes(row, size):
    place = (lax.axis_index("dp") * SEQ + lax.axis_index("seq")) * size
    return pltpu.roll(row, lax.rem(WIDTH - place, WIDTH), 1)[:, :size]


def lay_out(
    output, input_grad, down_grad, out_grad, gu_grad, qkv_grad, gains, attn_gain, ffn_gain,
    output_o, input_o, attn_o, query_o, key_o, value_o, q_gain_o, k_gain_o, out_o, ffn_o, gate_o, up_o, down_o,
):
    for src, dst in ((output, output_o), (input_grad, input_o), (down_grad, down_o), (out_grad, out_o)):
        dst[...] = src[...]
    attn_scale = scale = column(as_row(attn_gain))
    for o in range(SEQ):
        for ref, first, size in ((query_o, 0, OWN_Q), (key_o, OWN_Q, OWN_K), (value_o, OWN_Q + OWN_K, OWN_K)):
            ref[:, o * size : (o + 1) * size] = qkv_grad[o, :, first : first + size].astype(F32) * scale
    scale = column(as_row(ffn_gain))
    for ref, first in ((gate_o, 0), (up_o, FF_OWN)):
        parts = []
        for j in range(8):
            for o in range(SEQ):
                part = gu_grad[o, :, first + j * FF_SHARD : first + (j + 1) * FF_SHARD]
                parts.append(part.astype(F32) * scale)
        ref[...] = jnp.concatenate(parts, axis=1)
    size = attn_o.shape[0]
    attn_o[...] = (column(own_lanes(gains[0:1, :], size)) / attn_scale).reshape(size)
    ffn_o[...] = (column(own_lanes(gains[1:2, :], size)) / scale).reshape(size)
    q_gain_o[...] = (gains[2:3, 0:64] + gains[2:3, 64:128]).reshape(HEAD_SIZE)
    k_gain_o[...] = (gains[2:3, 128:192] + gains[2:3, 192:256]).reshape(HEAD_SIZE)


class Names:
    pass


def frequencies():
    steps = np.arange(HEAD_SIZE // 2, dtype=np.float64) * (2.0 / HEAD_SIZE)
    return jnp.asarray(np.tile(THETA ** (-steps), 4)[None], F32)


COLUMN_COPIES = 126
ROW_COPIES = 45
LOCAL_COPIES = 16
VMEM_BYTES = 63 * 2**20


def on_device_in_kernels(
    inputs,
    doc_starts,
    cotangent,
    attn_gain,
    w_query,
    key_projection_weight,
    value_projection_weight,
    q_gain,
    k_gain,
    w_out,
    ffn_gain,
    w_gate,
    w_up,
    w_down,
):
    given = dict(
        inputs=inputs,
        cotangent=cotangent,
        attn_gain=attn_gain,
        ffn_gain=ffn_gain,
        q_gain=q_gain,
        k_gain=k_gain,
        w_query=w_query,
        w_key=key_projection_weight,
        w_value=value_projection_weight,
        w_out=w_out,
        w_gate=w_gate,
        w_up=w_up,
        w_down=w_down,
        frequency=frequencies(),
        doc_starts=doc_starts,
    )
    results = dict(
        output=((TOK, WIDTH), BF),
        input_grad=((TOK, WIDTH), F32),
        down_grad=((FF_SHARD, WIDTH), F32),
        out_grad=((32, WIDTH), F32),
        gu_grad=((SEQ, 32, HIDDEN_TWO), BF),
        qkv_grad=((SEQ, 32, QKV), BF),
        gain_grads=((8, WIDTH), F32),
    )
    kept = dict(
        x_own=((TOK, WIDTH), BF),
        wq=((32, SEQ * OWN_Q), BF),
        wk=((32, SEQ * OWN_K), BF),
        wv=((32, SEQ * OWN_K), BF),
        wg=((32, FF), BF),
        wu=((32, FF), BF),
        output_own=((TOK, WIDTH), BF),
        d_input=((TOK, WIDTH), F32),
        down_own=((FF_SHARD, WIDTH), F32),
        out_own=((32, WIDTH), F32),
        w_qkv=((SEQ, 32, QKV), BF),
        cosine=((ROW, 128), F32),
        sine=((ROW, 128), F32),
        u_rows=((SEQ, TOK, WIDTH), BF),
        cot_rows=((SEQ, TOK, WIDTH), BF),
        mid_rows=((SEQ, TOK, WIDTH), BF),
        qkv_all=((8, 4, 32, QKV), BF),
        gu_all=((8, 4, 32, HIDDEN_TWO), BF),
        down_all=((8, FF_SHARD, WIDTH), BF),
        out_all=((8, 4, 32, WIDTH), BF),
        q_linear=((ROW, OWN_Q), F32),
        k_linear=((ROW, OWN_K), F32),
        q_heads=((2, 2, ROW, HEAD_SIZE), BF),
        k_heads=((2, ROW, HEAD_SIZE), BF),
        v_heads=((2, ROW, HEAD_SIZE), BF),
        log_total=((ROW, 128), F32),
        att_own=((SEQ, TOK, OWN_Q), BF),
        att_local=((SEQ, TOK, OWN_Q), BF),
        middle=((TOK, WIDTH), F32),
        active=((SEQ, TOK, FF_OWN), BF),
        d_gu=((38, 32, HIDDEN_TWO), BF),
        parts=((3, 8, 32, WIDTH), BF),
        slots_a=((3, 8, 32, WIDTH), BF),
        slots_b=((3, 8, 32, WIDTH), BF),
        d_att_rows=((SEQ, TOK, OWN_Q), BF),
        flipped=((FF_OWN, ROW), BF),
        down_part=((8, FF_SHARD, WIDTH), BF),
        down_a_slots=((9, SUM_A, WIDTH), BF),
        down_b_slots=((11, SUM_B, WIDTH), BF),
        out_slots=((9, 32, WIDTH), BF),
        qkv_slots=((9, 4, 32, QKV), BF),
        d_query=((ROW, OWN_Q), BF),
        d_kv=((2, ROW, 128), F32),
        d_qkv=((ROW, QKV), BF),
        head_gain_part=((2, 128), F32),
        gains=((3, 8, WIDTH), F32),
        gain_slots=((7, 8, WIDTH), F32),
    )

    def body(*refs):
        r = Names()
        names = [*given, *results, *kept]
        for name, ref in zip(names, refs):
            setattr(r, name, ref)
        r.send_sems, r.recv_sems, r.local_sems, r.free = refs[len(names) :]
        whole_block(r)

    done = pl.pallas_call(
        body,
        out_shape=[jax.ShapeDtypeStruct(*result) for result in results.values()],
        in_specs=[
            pl.BlockSpec(memory_space=pltpu.SMEM if a is doc_starts else pltpu.VMEM if a.size < 1024 else pl.ANY)
            for a in given.values()
        ],
        out_specs=[pl.BlockSpec(memory_space=pl.ANY)] * (len(results) - 1) + [pl.BlockSpec(memory_space=pltpu.VMEM)],
        scratch_shapes=[pltpu.VMEM(*shape) for shape in kept.values()]
        + [
            pltpu.SemaphoreType.DMA((COLUMN_COPIES + ROW_COPIES,)),
            pltpu.SemaphoreType.DMA((COLUMN_COPIES + ROW_COPIES,)),
            pltpu.SemaphoreType.DMA((LOCAL_COPIES,)),
            pltpu.SemaphoreType.REGULAR,
        ],
        compiler_params=pltpu.CompilerParams(
            collective_id=0, has_side_effects=True, vmem_limit_bytes=VMEM_BYTES
        ),
        cost_estimate=pl.CostEstimate(flops=30_000_000_000, bytes_accessed=10_000_000, transcendentals=0),
    )(*given.values())
    rows = w_query.shape[0]
    shapes = [
        ((TOK, WIDTH), BF),
        ((TOK, WIDTH), F32),
        ((rows,), F32),
        ((rows, SEQ * OWN_Q), F32),
        ((rows, SEQ * OWN_K), F32),
        ((rows, SEQ * OWN_K), F32),
        ((HEAD_SIZE,), F32),
        ((HEAD_SIZE,), F32),
        ((rows, WIDTH), F32),
        ((rows,), F32),
        ((rows, FF), F32),
        ((rows, FF), F32),
        ((FF_SHARD, WIDTH), F32),
    ]
    return tuple(
        pl.pallas_call(
            lay_out,
            out_shape=[jax.ShapeDtypeStruct(*shape) for shape in shapes],
            in_specs=[pl.BlockSpec(memory_space=pltpu.VMEM)] * 9,
            out_specs=[pl.BlockSpec(memory_space=pltpu.VMEM)] * 13,
            compiler_params=pltpu.CompilerParams(vmem_limit_bytes=VMEM_BYTES),
            cost_estimate=pl.CostEstimate(flops=1_000_000, bytes_accessed=10_000_000, transcendentals=0),
        )(*done, given["attn_gain"], given["ffn_gain"])
    )


def solution(mesh):
    in_kernels = (mesh.shape["dp"], mesh.shape["seq"]) == (8, 4)
    placed = (
        P(("dp", "seq"), None),
        P("dp", None),
        P(("dp", "seq"), None),
        P(("dp", "seq")),
        P(("dp", "seq"), None),
        P(("dp", "seq"), None),
        P(("dp", "seq"), None),
        P(),
        P(),
        P(("dp", "seq"), None),
        P(("dp", "seq")),
        P(("dp", "seq"), None),
        P(("dp", "seq"), None),
        P(("dp", "seq"), None),
    )
    return jax.shard_map(
        on_device_in_kernels if in_kernels else on_device,
        mesh=mesh,
        in_specs=placed,
        out_specs=(
            P(("dp", "seq"), None),
            P(("dp", "seq"), None),
            P(("dp", "seq")),
            P(("dp", "seq"), None),
            P(("dp", "seq"), None),
            P(("dp", "seq"), None),
            P(),
            P(),
            P(("dp", "seq"), None),
            P(("dp", "seq")),
            P(("dp", "seq"), None),
            P(("dp", "seq"), None),
            P(("dp", "seq"), None),
        ),
        check_vma=False,
    )
```

```python
import jax
import jax.numpy as jnp
import numpy as np
from jax import lax
from jax.experimental import pallas as pl
from jax.experimental.pallas import tpu as pltpu
from jax.sharding import PartitionSpec as P

QUERY_HEADS = 16
KEY_VALUE_HEADS = 8
HEAD_SIZE = 64
FF = 4608


EPS = 1e-05
THETA = 1000000.0
MASKED = -1e30
CONTRACT_ROWS = (((0,), (0,)), ((), ()))
CONTRACT_COLS = (((1,), (1,)), ((), ()))


def rms_norm(values, gain_vec):
    return values * lax.rsqrt(jnp.mean(values * values, axis=-1, keepdims=True) + EPS) * gain_vec


def rotate_half(values):
    half_len = values.shape[-1] // 2
    return jnp.concatenate([-values[..., half_len:], values[..., :half_len]], axis=-1)


def unrotate_half(values):
    half_len = values.shape[-1] // 2
    return jnp.concatenate([values[..., half_len:], -values[..., :half_len]], axis=-1)


def row_layout(row_starts, places):
    inside = places[:, None] >= row_starts[None, :]
    doc_ids = jnp.sum(inside.astype(jnp.int32), axis=1) - 1
    begins = jnp.max(jnp.where(inside, row_starts[None, :], 0), axis=1)
    offsets = (places - begins).astype(jnp.float32)
    freq_steps = jnp.arange(HEAD_SIZE // 2, dtype=jnp.float32) * (2.0 / HEAD_SIZE)
    frequency = THETA ** (-freq_steps)
    angles = offsets[:, None] * frequency[None, :]
    angles = jnp.concatenate([angles, angles], axis=-1)
    return (doc_ids, jnp.cos(angles), jnp.sin(angles))


def norm_back(upstream, values, gain_vec):
    inverse = lax.rsqrt(jnp.mean(values * values, axis=-1, keepdims=True) + EPS)
    unit_vec = values * inverse
    gain_part = jnp.sum(upstream * unit_vec, axis=tuple(range(values.ndim - 1)))
    scaled = upstream * gain_vec
    return (
        inverse * (scaled - unit_vec * jnp.mean(scaled * unit_vec, axis=-1, keepdims=True)),
        gain_part,
    )


def head_forward_pass(linear, gain_vec, cosine_table, sine_table, heads):
    local_rows = linear.shape[0]
    shaped = rms_norm(linear.reshape(local_rows, heads, HEAD_SIZE), gain_vec)
    turned = shaped * cosine_table + rotate_half(shaped) * sine_table
    return turned.astype(jnp.bfloat16).reshape(local_rows, heads * HEAD_SIZE)


def head_backward_pass(grad_in, linear, gain_vec, cosine_table, sine_table, heads):
    local_rows = linear.shape[0]
    shaped = linear.reshape(local_rows, heads, HEAD_SIZE)
    upstream = grad_in.astype(jnp.float32).reshape(local_rows, heads, HEAD_SIZE)
    d_normed = upstream * cosine_table + unrotate_half(upstream * sine_table)
    d_linear, gain_part = norm_back(d_normed, shaped, gain_vec)
    return (d_linear.reshape(local_rows, heads * HEAD_SIZE).astype(jnp.bfloat16), gain_part)


def block_scores(q_block, keys_all, block_places, block_docs, places, doc_ids):
    score_scale = HEAD_SIZE ** (-0.5)
    scores = (
        jnp.einsum("qkgd,skd->kgqs", q_block, keys_all, preferred_element_type=jnp.float32)
        * score_scale
    )
    allowed = (places[None, :] <= block_places[:, None]) & (doc_ids[None, :] == block_docs[:, None])
    return jnp.where(allowed[None, None], scores, MASKED)


def attend_forward(query_rows, keys_in, values_in, places, doc_ids):
    total_length = query_rows.shape[0]
    kv_heads = keys_in.shape[1] // HEAD_SIZE
    query_group = QUERY_HEADS // KEY_VALUE_HEADS
    block_length = min(512, total_length)
    number_of_blocks = total_length // block_length
    keys_all = keys_in.reshape(total_length, kv_heads, HEAD_SIZE)
    values_all = values_in.reshape(total_length, kv_heads, HEAD_SIZE)
    grouped_queries = query_rows.reshape(
        number_of_blocks, block_length, kv_heads, query_group, HEAD_SIZE
    )

    def one_block(pieces):
        q_block, block_places, block_docs = pieces
        scores = block_scores(q_block, keys_all, block_places, block_docs, places, doc_ids)
        row_max = jnp.max(scores, axis=-1, keepdims=True)
        weights = jnp.exp(scores - row_max)
        sum_total = jnp.sum(weights, axis=-1, keepdims=True)
        soft_max = (weights / sum_total).astype(jnp.bfloat16)
        mixture = jnp.einsum(
            "kgqs,skd->qkgd", soft_max, values_all, preferred_element_type=jnp.float32
        )
        return (mixture.astype(jnp.bfloat16), row_max[..., 0] + jnp.log(sum_total[..., 0]))

    mixture, log_total = lax.map(
        one_block,
        (
            grouped_queries,
            places.reshape(number_of_blocks, block_length),
            doc_ids.reshape(number_of_blocks, block_length),
        ),
    )
    return (mixture.reshape(total_length, kv_heads * query_group * HEAD_SIZE), log_total)


def attend_back(query_rows, keys_in, values_in, grad_out, log_total, places, doc_ids):
    total_length = query_rows.shape[0]
    kv_heads = keys_in.shape[1] // HEAD_SIZE
    query_group = QUERY_HEADS // KEY_VALUE_HEADS
    block_length = min(512, total_length)
    number_of_blocks = total_length // block_length
    score_scale = HEAD_SIZE ** (-0.5)
    keys_all = keys_in.reshape(total_length, kv_heads, HEAD_SIZE)
    values_all = values_in.reshape(total_length, kv_heads, HEAD_SIZE)
    grouped_queries = query_rows.reshape(
        number_of_blocks, block_length, kv_heads, query_group, HEAD_SIZE
    )
    grads_all = grad_out.reshape(number_of_blocks, block_length, kv_heads, query_group, HEAD_SIZE)

    def one_block(carried, pieces):
        key_total, value_total = carried
        q_block, g_block, block_log, block_places, block_docs = pieces
        scores = block_scores(q_block, keys_all, block_places, block_docs, places, doc_ids)
        chances = jnp.exp(scores - block_log[..., None])
        d_chances = jnp.einsum(
            "qkgd,skd->kgqs", g_block, values_all, preferred_element_type=jnp.float32
        )
        row_dots = jnp.sum(d_chances * chances, axis=-1, keepdims=True)
        d_scores = (chances * (d_chances - row_dots)).astype(jnp.bfloat16)
        d_query = (
            jnp.einsum("kgqs,skd->qkgd", d_scores, keys_all, preferred_element_type=jnp.float32)
            * score_scale
        )
        key_total = (
            key_total
            + jnp.einsum("kgqs,qkgd->skd", d_scores, q_block, preferred_element_type=jnp.float32)
            * score_scale
        )
        value_total = value_total + jnp.einsum(
            "kgqs,qkgd->skd",
            chances.astype(jnp.bfloat16),
            g_block,
            preferred_element_type=jnp.float32,
        )
        return ((key_total, value_total), d_query)

    zero_kv = jnp.zeros((total_length, kv_heads, HEAD_SIZE), jnp.float32)
    inputs_scan = (
        grouped_queries,
        grads_all,
        log_total,
        places.reshape(number_of_blocks, block_length),
        doc_ids.reshape(number_of_blocks, block_length),
    )
    (key_total, value_total), d_query = lax.scan(one_block, (zero_kv, zero_kv), inputs_scan)
    return (
        d_query.reshape(total_length, kv_heads * query_group * HEAD_SIZE).astype(jnp.bfloat16),
        key_total.reshape(total_length, kv_heads * HEAD_SIZE).astype(jnp.bfloat16),
        value_total.reshape(total_length, kv_heads * HEAD_SIZE).astype(jnp.bfloat16),
    )


def on_device(
    inputs,
    doc_starts,
    cotangent,
    attn_gain,
    w_query,
    key_projection_weight,
    value_projection_weight,
    q_gain,
    k_gain,
    w_out,
    ffn_gain,
    w_gate,
    w_up,
    w_down,
):
    local_rows = inputs.shape[0]
    seq_parts = lax.axis_size("seq")
    total_length = local_rows * seq_parts
    row_starts = doc_starts[0]
    local_places = lax.axis_index("seq") * local_rows + jnp.arange(local_rows, dtype=jnp.int32)
    unused_docs, cosine_table, sine_table = row_layout(row_starts, local_places)
    cosine_table = cosine_table[:, None, :]
    sine_table = sine_table[:, None, :]
    all_places = jnp.arange(total_length, dtype=jnp.int32)
    all_docs = jnp.sum((all_places[:, None] >= row_starts[None, :]).astype(jnp.int32), axis=1) - 1
    q_scale = q_gain.astype(jnp.float32)
    key_norm_scale = k_gain.astype(jnp.float32)
    attn_scale, query_full, key_full, value_full, out_full = (
        lax.all_gather(attn_gain, ("dp", "seq"), axis=0, tiled=True),
        lax.all_gather(w_query, ("dp", "seq"), axis=0, tiled=True),
        lax.all_gather(key_projection_weight, ("dp", "seq"), axis=0, tiled=True),
        lax.all_gather(value_projection_weight, ("dp", "seq"), axis=0, tiled=True),
        lax.all_gather(w_out, ("dp", "seq"), axis=0, tiled=True),
    )
    source = inputs.astype(jnp.float32)
    normalized_input = rms_norm(source, attn_scale.astype(jnp.float32)).astype(jnp.bfloat16)
    q_linear = jnp.dot(normalized_input, query_full, preferred_element_type=jnp.float32)
    key_linear_output = jnp.dot(normalized_input, key_full, preferred_element_type=jnp.float32)
    q_sent = head_forward_pass(q_linear, q_scale, cosine_table, sine_table, QUERY_HEADS)
    key_sent_rows = head_forward_pass(
        key_linear_output, key_norm_scale, cosine_table, sine_table, KEY_VALUE_HEADS
    )
    v_sent = jnp.dot(normalized_input, value_full, preferred_element_type=jnp.float32).astype(
        jnp.bfloat16
    )
    q_heads, k_heads, v_heads = (
        lax.all_to_all(q_sent, "seq", split_axis=1, concat_axis=0, tiled=True),
        lax.all_to_all(key_sent_rows, "seq", split_axis=1, concat_axis=0, tiled=True),
        lax.all_to_all(v_sent, "seq", split_axis=1, concat_axis=0, tiled=True),
    )
    mixture, log_total = attend_forward(q_heads, k_heads, v_heads, all_places, all_docs)
    attended = lax.all_to_all(mixture, "seq", split_axis=0, concat_axis=1, tiled=True)
    middle = source + jnp.dot(attended, out_full, preferred_element_type=jnp.float32)
    ffn_scale, gate_full, up_full, down_full = (
        lax.all_gather(ffn_gain, ("dp", "seq"), axis=0, tiled=True),
        lax.all_gather(w_gate, ("dp", "seq"), axis=0, tiled=True),
        lax.all_gather(w_up, ("dp", "seq"), axis=0, tiled=True),
        lax.all_gather(w_down, ("dp", "seq"), axis=0, tiled=True),
    )
    normed_mid = rms_norm(middle, ffn_scale.astype(jnp.float32)).astype(jnp.bfloat16)
    gate_lin = jnp.dot(normed_mid, gate_full, preferred_element_type=jnp.float32)
    upward = jnp.dot(normed_mid, up_full, preferred_element_type=jnp.float32)
    sigmoid_gate = jax.nn.sigmoid(gate_lin)
    swish = gate_lin * sigmoid_gate
    active = (swish * upward).astype(jnp.bfloat16)
    output = (middle + jnp.dot(active, down_full, preferred_element_type=jnp.float32)).astype(
        jnp.bfloat16
    )
    ffn_scale, gate_full, up_full, down_full = (
        lax.all_gather(ffn_gain, ("dp", "seq"), axis=0, tiled=True),
        lax.all_gather(w_gate, ("dp", "seq"), axis=0, tiled=True),
        lax.all_gather(w_up, ("dp", "seq"), axis=0, tiled=True),
        lax.all_gather(w_down, ("dp", "seq"), axis=0, tiled=True),
    )
    d_active = lax.dot_general(
        cotangent, down_full, CONTRACT_COLS, preferred_element_type=jnp.float32
    )
    d_gate = (d_active * upward * (sigmoid_gate * (1.0 + gate_lin * (1.0 - sigmoid_gate)))).astype(
        jnp.bfloat16
    )
    d_up = (d_active * swish).astype(jnp.bfloat16)
    d_normed_mid = lax.dot_general(
        d_gate, gate_full, CONTRACT_COLS, preferred_element_type=jnp.float32
    )
    d_normed_mid = d_normed_mid + lax.dot_general(
        d_up, up_full, CONTRACT_COLS, preferred_element_type=jnp.float32
    )
    d_middle_norm, ffn_gain_part = norm_back(d_normed_mid, middle, ffn_scale.astype(jnp.float32))
    d_middle = cotangent.astype(jnp.float32) + d_middle_norm
    d_branch = d_middle.astype(jnp.bfloat16)
    attn_scale, query_full, key_full, value_full, out_full = (
        lax.all_gather(attn_gain, ("dp", "seq"), axis=0, tiled=True),
        lax.all_gather(w_query, ("dp", "seq"), axis=0, tiled=True),
        lax.all_gather(key_projection_weight, ("dp", "seq"), axis=0, tiled=True),
        lax.all_gather(value_projection_weight, ("dp", "seq"), axis=0, tiled=True),
        lax.all_gather(w_out, ("dp", "seq"), axis=0, tiled=True),
    )
    d_attended = lax.dot_general(
        d_branch, out_full, CONTRACT_COLS, preferred_element_type=jnp.float32
    ).astype(jnp.bfloat16)
    d_mixture = lax.all_to_all(d_attended, "seq", split_axis=1, concat_axis=0, tiled=True)
    d_q_heads, d_k_heads, d_v_heads = attend_back(
        q_heads, k_heads, v_heads, d_mixture, log_total, all_places, all_docs
    )
    d_q_sent, key_sent_gradient, d_v_sent = (
        lax.all_to_all(d_q_heads, "seq", split_axis=0, concat_axis=1, tiled=True),
        lax.all_to_all(d_k_heads, "seq", split_axis=0, concat_axis=1, tiled=True),
        lax.all_to_all(d_v_heads, "seq", split_axis=0, concat_axis=1, tiled=True),
    )
    d_q_linear, q_gain_part = head_backward_pass(
        d_q_sent, q_linear, q_scale, cosine_table, sine_table, QUERY_HEADS
    )
    key_linear_gradient, key_gain_piece = head_backward_pass(
        key_sent_gradient,
        key_linear_output,
        key_norm_scale,
        cosine_table,
        sine_table,
        KEY_VALUE_HEADS,
    )
    d_normed = lax.dot_general(
        d_q_linear, query_full, CONTRACT_COLS, preferred_element_type=jnp.float32
    )
    d_normed = d_normed + lax.dot_general(
        key_linear_gradient, key_full, CONTRACT_COLS, preferred_element_type=jnp.float32
    )
    d_normed = d_normed + lax.dot_general(
        d_v_sent, value_full, CONTRACT_COLS, preferred_element_type=jnp.float32
    )
    d_source_norm, attn_gain_part = norm_back(d_normed, source, attn_scale.astype(jnp.float32))
    input_grad = d_middle + d_source_norm
    attn_columns = jnp.concatenate([d_q_linear, key_linear_gradient, d_v_sent], axis=1)
    ffn_columns = jnp.concatenate([d_gate, d_up], axis=1)
    left = normalized_input
    first_part = lax.dot_general(
        left, attn_columns, CONTRACT_ROWS, preferred_element_type=jnp.float32
    )
    second_part = lax.dot_general(
        normed_mid, ffn_columns, CONTRACT_ROWS, preferred_element_type=jnp.float32
    )
    width_sums = lax.psum_scatter(
        jnp.concatenate([first_part, second_part], axis=1),
        ("dp", "seq"),
        scatter_dimension=0,
        tiled=True,
    )
    left = attended
    out_grad = lax.psum_scatter(
        lax.dot_general(left, d_branch, CONTRACT_ROWS, preferred_element_type=jnp.float32),
        ("dp", "seq"),
        scatter_dimension=0,
        tiled=True,
    )
    left = active
    down_grad = lax.psum_scatter(
        lax.dot_general(left, cotangent, CONTRACT_ROWS, preferred_element_type=jnp.float32),
        ("dp", "seq"),
        scatter_dimension=0,
        tiled=True,
    )
    attn_gain_grad, ffn_gain_grad = (
        lax.psum_scatter(attn_gain_part, ("dp", "seq"), scatter_dimension=0, tiled=True),
        lax.psum_scatter(ffn_gain_part, ("dp", "seq"), scatter_dimension=0, tiled=True),
    )
    q_gain_grad, k_gain_grad = lax.psum((q_gain_part, key_gain_piece), ("dp", "seq"))
    q_cols = QUERY_HEADS * HEAD_SIZE
    kv_cols = KEY_VALUE_HEADS * HEAD_SIZE
    query_grad = width_sums[:, :q_cols]
    key_grad = width_sums[:, q_cols : q_cols + kv_cols]
    value_grad = width_sums[:, q_cols + kv_cols : q_cols + 2 * kv_cols]
    gate_grad = width_sums[:, q_cols + 2 * kv_cols : q_cols + 2 * kv_cols + FF]
    up_grad = width_sums[:, q_cols + 2 * kv_cols + FF :]
    return (
        output,
        input_grad,
        attn_gain_grad,
        query_grad,
        key_grad,
        value_grad,
        q_gain_grad,
        k_gain_grad,
        out_grad,
        ffn_gain_grad,
        gate_grad,
        up_grad,
        down_grad,
    )


BF = jnp.bfloat16
F32 = jnp.float32
MESH = pl.DeviceIdType.MESH
SEQ = 4
PLANES = 4
TOK = 256
WIDTH = 1024
ROW = 1024
OWN_Q = 256
OWN_K = 128
QKV = 512
FF_OWN = 1152
FF_SHARD = 144
HIDDEN_TWO = 2304
DOWN_A = 80
DOWN_B = 64
SUM_A = 80
SUM_B = 64


def flip(value, bit):
    return value + bit - 2 * bit * lax.rem(lax.div(value, bit), 2)


def dot(left, right):
    return lax.dot_general(left, right, (((1,), (0,)), ((), ())), preferred_element_type=F32)


def dot_nt(left, right):
    return lax.dot_general(left, right, (((1,), (1,)), ((), ())), preferred_element_type=F32)


def dot_tn(left, right):
    return lax.dot_general(left, right, (((0,), (0,)), ((), ())), preferred_element_type=F32)


class Links:
    def __init__(self, send_sems, recv_sems, local_sems):
        self.send_sems, self.recv_sems, self.local_sems = send_sems, recv_sems, local_sems
        self.column_copies = 0
        self.row_copies = COLUMN_COPIES
        self.local_copies = []
        self.open = []
        self.late = []
        self.dp = lax.axis_index("dp")
        self.s = lax.axis_index("seq")
        self.s1 = flip(self.s, 1)
        self.s2 = flip(self.s, 2)
        self.s3 = flip(self.s1, 2)
        self.others = (self.s1, self.s2, self.s3)
        self.y = lax.rem(self.dp, 2)
        self.z = lax.div(self.dp, 2)
        self.y_peer = flip(self.dp, 1)
        z1 = flip(self.z, 1)
        self.planes = (z1, flip(self.z, 2), flip(z1, 2))
        self.z_peers = tuple(2 * z + self.y for z in self.planes)

    def greet(self, semaphore, partners):
        for place in partners:
            pl.semaphore_signal(semaphore, inc=1, device_id=place, device_id_type=MESH)

    def column(self):
        return [(p, self.s) for p in (self.y_peer,) + self.z_peers]

    def everyone(self):
        return [(self.dp, s) for s in self.others] + self.column()

    def plan(self, src, dst, dp=None, s=None):
        if dp is None:
            n = self.row_copies
            self.row_copies += 1
        else:
            n = self.column_copies
            self.column_copies += 1
        copy = pltpu.make_async_remote_copy(
            src_ref=src,
            dst_ref=dst,
            send_sem=self.send_sems.at[n],
            recv_sem=self.recv_sems.at[n],
            device_id=(self.dp if dp is None else dp, self.s if s is None else s),
            device_id_type=MESH,
        )
        return copy

    def push(self, src, dst, dp=None, s=None, when=None, late=False):
        copy = self.plan(src, dst, dp, s)
        if when is None:
            copy.start()
        else:
            pl.when(when)(copy.start)
        (self.late if late else self.open).append((copy, when))
        return copy

    def start_over(self):
        self.column_copies = 0

    def keep(self, src, dst):
        copy = pltpu.make_async_copy(src, dst, self.local_sems.at[len(self.local_copies)])
        copy.start()
        self.local_copies.append(copy)
        return copy

    def settle(self, copies):
        for copy in copies:
            copy.wait_send()
        self.open = [item for item in self.open if all(item[0] is not copy for copy in copies)]

    def drain_late(self):
        self.open, self.late = self.late, []
        self.drain()

    def drain(self):
        for copy, when in self.open:
            if when is None:
                copy.wait_send()
            else:
                pl.when(when)(copy.wait_send)
        self.open = []


class Line:
    def __init__(self, links, view):
        self.links, self.view = links, view
        self.hops = []

    def pass_on(self, step):
        l = self.links
        below, above = l.z - step, l.z + step
        low = self.view(jnp.maximum(below, 0))
        high = self.view(jnp.minimum(above, PLANES - 1))
        up = l.push(
            low, low, dp=jnp.minimum(l.dp + 2, 2 * PLANES - 1), when=(below >= 0) & (l.z < PLANES - 1)
        )
        down = l.push(high, high, dp=jnp.maximum(l.dp - 2, 0), when=(above <= PLANES - 1) & (l.z > 0))
        self.hops.append((up, down))

    def start(self):
        self.pass_on(0)

    def step(self, k):
        l = self.links
        below, above = l.z - 1 - k, l.z + 1 + k
        from_below, from_above = below >= 0, above <= PLANES - 1
        pl.when(from_below)(self.hops[k][0].wait_recv)
        pl.when(from_above)(self.hops[k][1].wait_recv)
        if k < PLANES - 2:
            self.pass_on(k + 1)
        return [
            (from_below, self.view(jnp.maximum(below, 0))),
            (from_above, self.view(jnp.minimum(above, PLANES - 1))),
        ]


class Gather:
    def __init__(self, links, view):
        self.links = links
        self.line = Line(links, lambda z: view(2 * z + links.y))
        self.own = view(links.dp)
        self.over_y = []

    def start_y(self):
        self.over_y.append((None, self.links.push(self.own, self.own, dp=self.links.y_peer)))

    def start_z(self):
        self.line.start()

    def step(self, k):
        for when, block in self.line.step(k):
            copy = self.links.push(block, block, dp=self.links.y_peer, when=when)
            self.over_y.append((when, copy))

    def finish(self):
        for when, copy in self.over_y:
            if when is None:
                copy.wait_recv()
            else:
                pl.when(when)(copy.wait_recv)


class PairGather:
    def __init__(self, links, view):
        self.links = links
        self.near = Line(links, lambda z: view(2 * z + links.y))
        self.far = Line(links, lambda z: view(2 * z + 1 - links.y))
        self.own = view(links.dp)

    def start_y(self):
        self.over_y = self.links.push(self.own, self.own, dp=self.links.y_peer)

    def start_z(self):
        self.near.start()

    def join(self):
        self.over_y.wait_recv()
        self.far.start()

    def step(self, k):
        self.near.step(k)
        self.far.step(k)


class Chain:
    def __init__(self, links, view, slots):
        self.links, self.view, self.slots = links, view, slots
        self.up, self.down = {}, {}

    def start(self):
        l = self.links
        last = PLANES - 1
        for d in range(PLANES):
            if d > 0:
                self.up[d] = l.plan(self.view(d), self.slots(d), dp=jnp.minimum(l.dp + 2, 2 * last + 1))
            if d < last:
                place = jnp.where(l.z == d + 1, PLANES, d)
                self.down[d] = l.plan(self.view(d), self.slots(place), dp=jnp.maximum(l.dp - 2, 0))

    def add(self, d, copy):
        copy.wait_recv()
        block = self.view(d)
        block[...] = (block[...].astype(F32) + self.slots(d)[...].astype(F32)).astype(BF)

    def step(self, j):
        last = PLANES - 1

        @pl.when(self.links.z == j)
        def _():
            for d in range(last, j, -1):
                if j > 0:
                    self.add(d, self.up[d])
                self.up[d].start()

        @pl.when(self.links.z == last - j)
        def _():
            for d in range(last - j):
                if j > 0:
                    self.add(d, self.down[d])
                self.down[d].start()

        for d in range(PLANES):
            if d > j:
                self.links.late.append((self.up[d], self.links.z == j))
            if d < last - j:
                self.links.late.append((self.down[d], self.links.z == last - j))

    def total(self):
        l = self.links
        for d in range(PLANES):
            if d > 0:
                pl.when(l.z == d)(self.up[d].wait_recv)
            if d < PLANES - 1:
                pl.when(l.z == d)(self.down[d].wait_recv)
        own = self.view(l.z)[...].astype(F32)
        below = jnp.where(l.z > 0, self.slots(l.z)[...].astype(F32), 0.0)
        above = jnp.where(l.z < PLANES - 1, self.slots(PLANES)[...].astype(F32), 0.0)
        return own + (below + above)


class Scatter:
    def __init__(self, links, view, y_slots, z_slots):
        self.links, self.view, self.y_slots = links, view, y_slots
        self.chain = Chain(links, lambda z: view(2 * z + links.y), z_slots)

    def start(self):
        l = self.links
        self.order = [jnp.where(l.z < PLANES // 2, PLANES - 1 - k, k) for k in range(PLANES)]
        self.over_y = [
            l.push(self.view(2 * d + 1 - l.y), self.y_slots(k), dp=l.y_peer, late=True) for k, d in enumerate(self.order)
        ]
        self.chain.start()

    def join(self):
        for k, copy in enumerate(self.over_y):
            copy.wait_recv()
            block = self.view(2 * self.order[k] + self.links.y)
            block[...] = (block[...].astype(F32) + self.y_slots(k)[...].astype(F32)).astype(BF)

    def step(self, j):
        self.chain.step(j)

    def total(self):
        return self.chain.total()


class PairScatter:
    def __init__(self, links, view, y_slot, near_slots, far_slots):
        self.links, self.view, self.y_slot = links, view, y_slot
        self.near = Chain(links, lambda z: view(2 * z + links.y), near_slots)
        self.far = Chain(links, lambda z: view(2 * z + 1 - links.y), far_slots)

    def start(self):
        self.far.start()
        self.near.start()

    def step(self, j):
        self.far.step(j)
        self.near.step(j)

    def cross(self):
        l = self.links
        block = self.view(2 * l.z + 1 - l.y)
        block[...] = self.far.total().astype(BF)
        self.over_y = l.push(block, self.y_slot, dp=l.y_peer, late=True)

    def total(self):
        own = self.near.total()
        self.over_y.wait_recv()
        return own + self.y_slot[...].astype(F32)


class RowSum:
    def __init__(self, links, slots):
        self.links, self.slots = links, slots

    def hand_over(self, src):
        self.first = self.links.push(src, self.slots.at[0], s=self.links.s1)

    def cross(self, src):
        self.first.wait_recv()
        src[...] = (src[...].astype(F32) + self.slots[0].astype(F32).reshape(src.shape)).astype(BF)
        self.second = self.links.push(src, self.slots.at[1], s=self.links.s2)

    def near(self, src):
        self.third = self.links.push(src, self.slots.at[2], s=self.links.s1)

    def total(self, own):
        self.third.wait_recv()
        self.second.wait_recv()
        return own + self.slots[1].astype(F32).reshape(own.shape) + self.slots[2].astype(F32).reshape(own.shape)


def lane_masks(rows):
    lane = lax.broadcasted_iota(jnp.int32, (rows, 128), 1)
    return lane < 64, lax.rem(lane, 64) < 32


def turned(values, low):
    return jnp.where(low, -pltpu.roll(values, 96, 1), pltpu.roll(values, 32, 1))


def unturned(values, low):
    return jnp.where(low, pltpu.roll(values, 96, 1), -pltpu.roll(values, 32, 1))


def per_head_mean(values, first):
    left = jnp.sum(jnp.where(first, values, 0.0), axis=-1, keepdims=True)
    right = jnp.sum(jnp.where(first, 0.0, values), axis=-1, keepdims=True)
    return jnp.where(first, left, right) * (1.0 / HEAD_SIZE)


def norm_rope(values, gain, cosine, sine, first, low):
    normed = values * lax.rsqrt(per_head_mean(values * values, first) + EPS) * gain
    return normed * cosine + turned(normed, low) * sine


def norm_rope_back(upstream, values, gain, cosine, sine, first, low):
    d_normed = upstream * cosine + unturned(upstream * sine, low)
    inverse = lax.rsqrt(per_head_mean(values * values, first) + EPS)
    unit = values * inverse
    scaled = d_normed * gain
    d_values = inverse * (scaled - unit * per_head_mean(scaled * unit, first))
    return d_values, jnp.sum(d_normed * unit, axis=0, keepdims=True)


def allowed_block(r, block, keys):
    query = lax.broadcasted_iota(jnp.int32, (TOK, keys), 0) + block * TOK
    key = lax.broadcasted_iota(jnp.int32, (TOK, keys), 1)
    place = lax.broadcasted_iota(jnp.int32, (TOK, 1), 0) + block * TOK
    begin = jnp.zeros((TOK, 1), jnp.int32)
    for k in range(4):
        start = r.doc_starts[0, k]
        begin = jnp.maximum(begin, jnp.where(place >= start, start, 0))
    return (key <= query) & (key >= begin)


SCORE_SCALE = HEAD_SIZE ** (-0.5)


def attention_block(r, pair, block):
    keys = (block + 1) * TOK
    rows = pl.ds(block * TOK, TOK)
    queries = r.q_heads[pair, :, rows, :].reshape(2 * TOK, HEAD_SIZE)
    scores = dot_nt(queries, r.k_heads[pair, :keys, :]).reshape(2, TOK, keys) * SCORE_SCALE
    scores = jnp.where(allowed_block(r, block, keys)[None], scores, MASKED)
    top = jnp.max(scores, axis=-1, keepdims=True)
    weights = jnp.exp(scores - top)
    total = jnp.sum(weights, axis=-1, keepdims=True)
    mixed = dot(weights.astype(BF).reshape(2 * TOK, keys), r.v_heads[pair, :keys, :])
    mixed = mixed.reshape(2, TOK, HEAD_SIZE) / total
    log_total = top + jnp.log(total)
    r.log_total[rows, 2 * pair : 2 * pair + 1] = log_total[0]
    r.log_total[rows, 2 * pair + 1 : 2 * pair + 2] = log_total[1]
    r.att_own[block, :, pair * 128 : (pair + 1) * 128] = jnp.concatenate(
        [mixed[0], mixed[1]], axis=-1
    ).astype(BF)


def attention_block_back(r, pair, block):
    keys = (block + 1) * TOK
    rows = pl.ds(block * TOK, TOK)
    queries = r.q_heads[pair, :, rows, :].reshape(2 * TOK, HEAD_SIZE)
    grads = r.d_att_rows[block, :, pair * 128 : (pair + 1) * 128]
    grads = jnp.concatenate([grads[:, :HEAD_SIZE], grads[:, HEAD_SIZE:]], axis=0)
    keys_in, values_in = r.k_heads[pair, :keys, :], r.v_heads[pair, :keys, :]
    scores = dot_nt(queries, keys_in).reshape(2, TOK, keys) * SCORE_SCALE
    log_total = jnp.stack([r.log_total[rows, 2 * pair + g : 2 * pair + g + 1] for g in range(2)])
    chances = jnp.exp(scores - log_total)
    chances = jnp.where(allowed_block(r, block, keys)[None], chances, 0.0)
    d_chances = dot_nt(grads, values_in).reshape(2, TOK, keys)
    row_dots = jnp.sum(d_chances * chances, axis=-1, keepdims=True)
    d_scores = (chances * (d_chances - row_dots)).astype(BF).reshape(2 * TOK, keys)
    d_query = (dot(d_scores, keys_in) * SCORE_SCALE).astype(BF)
    r.d_query[rows, pair * 128 : (pair + 1) * 128] = jnp.concatenate(
        [d_query[:TOK], d_query[TOK:]], axis=-1
    )
    d_key = dot_tn(d_scores, queries) * SCORE_SCALE
    d_value = dot_tn(chances.astype(BF).reshape(2 * TOK, keys), grads)
    if block == ROW // TOK - 1:
        r.d_kv[pair, :, :HEAD_SIZE] = d_key
        r.d_kv[pair, :, HEAD_SIZE:] = d_value
    else:
        r.d_kv[pair, :keys, :HEAD_SIZE] += d_key
        r.d_kv[pair, :keys, HEAD_SIZE:] += d_value


def norm_back_row(upstream, values, gain):
    inverse = lax.rsqrt(jnp.mean(values * values, axis=-1, keepdims=True) + EPS)
    unit = values * inverse
    scaled = upstream * gain
    d_values = inverse * (
        scaled - unit * jnp.mean(scaled * unit, axis=-1, keepdims=True)
    )
    return d_values, jnp.sum(upstream * unit, axis=0, keepdims=True)


def unit_norm(values):
    return values * lax.rsqrt(jnp.mean(values * values, axis=-1, keepdims=True) + EPS)


def as_row(vector):
    return vector[...].astype(F32).reshape(1, vector.shape[0])


def twice(vector):
    row = as_row(vector)
    return jnp.concatenate([row, row], axis=1)


def own_parts(r):
    for o in range(SEQ):
        for ref, first, size in ((r.wq, 0, OWN_Q), (r.wk, OWN_Q, OWN_K), (r.wv, OWN_Q + OWN_K, OWN_K)):
            r.w_qkv[o, :, first : first + size] = ref[:, o * size : (o + 1) * size]


def own_gains(r):
    size = r.attn_gain.shape[0]
    rest = jnp.zeros((1, 128 - size), F32)
    place = r.links.s * size
    rows = [pltpu.roll(jnp.concatenate([as_row(gain), rest], axis=1), place, 1) for gain in (r.attn_gain, r.ffn_gain)]
    row = lax.broadcasted_iota(jnp.int32, (16, 128), 0)
    return jnp.where(row == 0, rows[0], jnp.where(row == 1, rows[1], 0.0)).astype(BF)


def all_gains(r):
    for b in range(2 * PLANES):
        total = r.gain_all[b, 0].astype(F32)
        for o in range(1, SEQ):
            total = total + r.gain_all[b, o].astype(F32)
        r.gain_rows[:, b * 128 : (b + 1) * 128] = total[0:8]


def own_units(r):
    for ref, first in ((r.wg, 0), (r.wu, FF_OWN)):
        scaled = ref[...].astype(F32)
        for o in range(SEQ):
            parts = [scaled[:, (4 * j + o) * FF_SHARD : (4 * j + o + 1) * FF_SHARD] for j in range(8)]
            r.d_gu[32 + o, :, first : first + FF_OWN] = jnp.concatenate(parts, axis=1).astype(BF)


def rotation_tables(r, half):
    size = ROW // 2
    rows = pl.ds(half * size, size)
    place = lax.broadcasted_iota(jnp.int32, (size, 1), 0) + half * size
    begin = jnp.zeros((size, 1), jnp.int32)
    for k in range(4):
        start = r.doc_starts[0, k]
        begin = jnp.maximum(begin, jnp.where(place >= start, start, 0))
    angles = (place - begin).astype(F32) * r.frequency[...]
    r.cosine[rows, :] = jnp.cos(angles)
    r.sine[rows, :] = jnp.sin(angles)


def head_forward(r):
    first, low = lane_masks(TOK)

    @pl.loop(0, SEQ)
    def _(t):
        rows = pl.ds(pl.multiple_of(t * TOK, TOK), TOK)
        linear = dot(r.u_rows[t], r.qkv_all[...].reshape(WIDTH, QKV))
        r.q_linear[rows, :] = linear[:, :OWN_Q]
        r.k_linear[rows, :] = linear[:, OWN_Q : OWN_Q + OWN_K]
        cosine, sine = r.cosine[rows, :], r.sine[rows, :]
        for pair in range(2):
            part = linear[:, pair * 128 : (pair + 1) * 128]
            part = norm_rope(part, twice(r.q_gain), cosine, sine, first, low).astype(BF)
            r.q_heads[pair, 0, rows, :] = part[:, :HEAD_SIZE]
            r.q_heads[pair, 1, rows, :] = part[:, HEAD_SIZE:]
        part = linear[:, OWN_Q : OWN_Q + OWN_K]
        part = norm_rope(part, twice(r.k_gain), cosine, sine, first, low).astype(BF)
        r.k_heads[0, rows, :] = part[:, :HEAD_SIZE]
        r.k_heads[1, rows, :] = part[:, HEAD_SIZE:]
        part = linear[:, OWN_Q + OWN_K :].astype(BF)
        r.v_heads[0, rows, :] = part[:, :HEAD_SIZE]
        r.v_heads[1, rows, :] = part[:, HEAD_SIZE:]


def head_backward(r):
    first, low = lane_masks(TOK)
    r.head_gain_part[...] = jnp.zeros((2, 128), F32)

    @pl.loop(0, SEQ)
    def _(t):
        rows = pl.ds(pl.multiple_of(t * TOK, TOK), TOK)
        cosine, sine = r.cosine[rows, :], r.sine[rows, :]
        for pair in range(2):
            cols = slice(pair * 128, (pair + 1) * 128)
            up = r.d_query[rows, cols].astype(F32)
            back, gain_part = norm_rope_back(up, r.q_linear[rows, cols], twice(r.q_gain), cosine, sine, first, low)
            r.d_qkv[rows, cols] = back.astype(BF)
            r.head_gain_part[0:1] += gain_part
        up = jnp.concatenate([r.d_kv[0, rows, :HEAD_SIZE], r.d_kv[1, rows, :HEAD_SIZE]], axis=-1)
        up = up.astype(BF).astype(F32)
        back, gain_part = norm_rope_back(up, r.k_linear[rows, :], twice(r.k_gain), cosine, sine, first, low)
        r.d_qkv[rows, OWN_Q : OWN_Q + OWN_K] = back.astype(BF)
        r.head_gain_part[1:2] += gain_part
        up = jnp.concatenate([r.d_kv[0, rows, HEAD_SIZE:], r.d_kv[1, rows, HEAD_SIZE:]], axis=-1)
        r.d_qkv[rows, OWN_Q + OWN_K :] = up.astype(BF)


def units_up(r, t):
    gate_up = dot(r.mid_rows[t], r.gu_all[...].reshape(WIDTH, HIDDEN_TWO))
    gate, up = gate_up[:, :FF_OWN], gate_up[:, FF_OWN:]
    sigmoid = 1.0 / (1.0 + jnp.exp(-gate))
    swish = gate * sigmoid
    r.active[t] = (swish * up).astype(BF)
    blocks = pl.ds(8 * t, 8)
    by_gate = up * (sigmoid * (1.0 + gate * (1.0 - sigmoid)))
    r.d_gu[blocks, :, :FF_OWN] = by_gate.astype(BF).reshape(8, 32, FF_OWN)
    r.d_gu[blocks, :, FF_OWN:] = swish.astype(BF).reshape(8, 32, FF_OWN)


def units_down(r, t):
    d_active = dot_nt(r.cot_rows[t], r.down_all[...].reshape(FF_OWN, WIDTH)).reshape(8, 32, FF_OWN)
    blocks = pl.ds(8 * t, 8)
    r.d_gu[blocks, :, :FF_OWN] = (d_active * r.d_gu[blocks, :, :FF_OWN].astype(F32)).astype(BF)
    r.d_gu[blocks, :, FF_OWN:] = (d_active * r.d_gu[blocks, :, FF_OWN:].astype(F32)).astype(BF)
    d_gu = r.d_gu[blocks].reshape(TOK, HIDDEN_TWO)
    return dot_nt(d_gu, r.gu_all[...].reshape(WIDTH, HIDDEN_TWO))


def whole_block(r):
    l = r.links = Links(r.send_sems, r.recv_sems, r.local_sems)
    l.greet(pltpu.get_barrier_semaphore(), l.everyone())
    read = [l.keep(src, dst) for src, dst in ((r.inputs, r.x_own), (r.w_query, r.wq), (r.w_key, r.wk), (r.w_value, r.wv))]
    read_units = [l.keep(r.w_gate, r.wg), l.keep(r.w_up, r.wu)]
    read_own = [
        l.keep(r.w_out, r.out_all.at[l.dp, l.s]),
        l.keep(r.w_down, r.down_all.at[l.dp]),
        l.keep(r.cotangent, r.cot_rows.at[l.s]),
    ]
    for copy in read:
        copy.wait()
    own_parts(r)
    r.qkv_all[l.dp, l.s] = r.w_qkv[l.s]
    r.gain_all[l.dp, l.s] = own_gains(r)
    for copy in read_units:
        copy.wait()
    own_units(r)
    r.gu_all[l.dp, l.s] = r.d_gu[32 + l.s]
    for copy in read_own:
        copy.wait()
    pl.semaphore_wait(pltpu.get_barrier_semaphore(), len(l.everyone()))
    out = PairGather(l, lambda b: r.out_all.at[b, l.s])
    qkv = Gather(l, lambda b: r.qkv_all.at[b])
    gate_up = [Gather(l, lambda b, g=g: r.gu_all.at[b, g]) for g in (l.s,) + l.others]
    down_a = Gather(l, lambda b: r.down_all.at[b, pl.ds(0, DOWN_A)])
    down_b = PairGather(l, lambda b: r.down_all.at[b, pl.ds(DOWN_A, DOWN_B)])
    gain_z = [
        l.push(r.gain_all.at[l.dp, l.s], r.gain_all.at[l.dp, l.s], dp=p) for p in l.z_peers
    ]
    gain_y = [l.push(r.gain_all.at[l.dp, l.s], r.gain_all.at[l.dp, l.s], dp=l.y_peer)]
    qkv_cols = [l.push(r.w_qkv.at[o], r.qkv_all.at[l.dp, l.s], s=o) for o in l.others]
    out.start_y()
    gate_up[0].start_y()
    gate_up[0].start_z()
    for copy, p in zip(gain_z, l.z_peers):
        copy.wait_recv()
        gain_y.append(l.push(r.gain_all.at[p, l.s], r.gain_all.at[p, l.s], dp=l.y_peer))
    for copy in qkv_cols:
        copy.wait_recv()
    qkv.start_z()
    out.start_z()
    down_a.start_y()
    gu_cols = [l.push(r.d_gu.at[32 + o], r.gu_all.at[l.dp, l.s], s=o) for o in l.others]
    qkv.start_y()
    for copy in gain_y:
        copy.wait_recv()
    gain_row = [l.push(r.gain_all.at[:, l.s], r.gain_all.at[:, l.s], s=o) for o in l.others]
    out.join()
    rotation_tables(r, 0)
    qkv.step(0)
    for copy in gain_row:
        copy.wait_recv()
    all_gains(r)
    x = r.x_own[...].astype(F32)
    r.u_rows[l.s] = (unit_norm(x) * r.gain_rows[0:1, :]).astype(BF)
    u_far = l.push(r.u_rows.at[l.s], r.u_rows.at[l.s], s=l.s2)
    u_near = l.push(r.u_rows.at[l.s], r.u_rows.at[l.s], s=l.s1)
    out.step(0)
    gu_cols[1].wait_recv()
    gu_cols[2].wait_recv()
    qkv.step(1)
    gu_cols[0].wait_recv()
    out.step(1)
    gate_up[0].step(0)
    down_a.start_z()
    gate_up[1].start_z()
    rotation_tables(r, 1)
    down_b.start_z()
    qkv.step(2)
    gate_up[3].start_y()
    gate_up[2].start_y()
    u_far.wait_recv()
    u_more = l.push(r.u_rows.at[l.s2], r.u_rows.at[l.s2], s=l.s1)
    out.step(2)
    down_b.start_y()
    u_near.wait_recv()
    u_more.wait_recv()
    qkv.finish()
    head_forward(r)
    attention_block(r, 0, 3)
    gate_up[1].start_y()
    attention_block(r, 1, 3)
    out_far = l.push(r.out_all.at[:, l.s], r.out_all.at[:, l.s], s=l.s2)
    out_near = l.push(r.out_all.at[:, l.s], r.out_all.at[:, l.s], s=l.s1)
    gate_up[3].start_z()
    gate_up[1].step(0)
    attention_block(r, 0, 2)
    attention_block(r, 1, 2)
    attention_block(r, 0, 1)
    gate_up[0].step(1)
    gate_up[3].step(0)
    attention_block(r, 1, 1)
    attention_block(r, 0, 0)
    attention_block(r, 1, 0)
    att = [l.push(r.att_own.at[o], r.att_local.at[l.s], s=o) for o in l.others]
    r.att_local[l.s] = r.att_own[l.s]
    gate_up[1].step(1)
    out_far.wait_recv()
    out_more = l.push(r.out_all.at[:, l.s2], r.out_all.at[:, l.s2], s=l.s1)
    gate_up[0].step(2)
    gate_up[3].step(1)
    gate_up[2].start_z()
    out_near.wait_recv()
    out_more.wait_recv()
    for copy in att:
        copy.wait_recv()
    middle = x
    for part in range(SEQ):
        rows = r.out_all[part * 2 : (part + 1) * 2].reshape(OWN_Q, WIDTH)
        middle = middle + dot(r.att_local[part], rows)
    r.middle[...] = middle
    r.mid_rows[l.s] = (unit_norm(middle) * r.gain_rows[1:2, :]).astype(BF)
    mid_far = l.push(r.mid_rows.at[l.s], r.mid_rows.at[l.s], s=l.s2)
    mid_near = l.push(r.mid_rows.at[l.s], r.mid_rows.at[l.s], s=l.s1)
    cot_far = l.push(r.cot_rows.at[l.s], r.cot_rows.at[l.s], s=l.s2)
    cot_near = l.push(r.cot_rows.at[l.s], r.cot_rows.at[l.s], s=l.s1)
    gate_up[3].step(2)
    gate_up[2].step(0)
    down_b.join()
    gate_up[2].step(1)
    gate_up[1].step(2)
    gate_up[2].step(2)
    down_a.step(0)
    down_b.step(0)
    mid_far.wait_recv()
    mid_more = l.push(r.mid_rows.at[l.s2], r.mid_rows.at[l.s2], s=l.s1)
    mid_near.wait_recv()
    mid_more.wait_recv()
    gate_up[3].finish()
    gate_up[1].finish()
    down_a.step(1)
    gate_up[0].finish()
    gate_up[2].finish()
    units_up(r, l.s3)
    units_up(r, l.s2)
    down_b.step(1)
    units_up(r, l.s1)
    units_up(r, l.s)
    cot_far.wait_recv()
    cot_more = l.push(r.cot_rows.at[l.s2], r.cot_rows.at[l.s2], s=l.s1)
    down_a.step(2)
    cot_near.wait_recv()
    cot_more.wait_recv()
    for t in range(SEQ):
        r.flipped[:, t * TOK : (t + 1) * TOK] = r.active[t].T
    cot = r.cot_rows[...].reshape(ROW, WIDTH)

    @pl.loop(0, 4)
    def _(k):
        rows = pl.ds(pl.multiple_of(k * 288, 32), 288)
        grad = dot(r.flipped[rows, :], cot).astype(BF)
        r.down_part[pl.ds(2 * k, 2)] = grad.reshape(2, FF_SHARD, WIDTH)

    down_a_sum = Scatter(
        l, lambda b: r.down_part.at[b, pl.ds(0, SUM_A)], lambda k: r.down_a_slots.at[k], lambda k: r.down_a_slots.at[4 + k]
    )
    down_b_sum = PairScatter(
        l,
        lambda b: r.down_part.at[b, pl.ds(SUM_A, SUM_B)],
        r.down_b_slots.at[10],
        lambda k: r.down_b_slots.at[k],
        lambda k: r.down_b_slots.at[5 + k],
    )
    d_mid = RowSum(l, r.slots_a)
    home = []
    kept = []
    down_b_sum.start()
    down_b_sum.step(0)
    down_b.step(2)
    down_a.finish()
    l.drain()
    down_a_sum.start()
    r.parts[0] = units_down(r, l.s3).astype(BF).reshape(8, 32, WIDTH)
    d_mid.hand_over(r.parts.at[0])
    r.parts[1] = units_down(r, l.s2).astype(BF).reshape(8, 32, WIDTH)
    d_mid.cross(r.parts.at[1])
    r.parts[2] = units_down(r, l.s1).astype(BF).reshape(8, 32, WIDTH)
    d_mid.near(r.parts.at[2])
    r.d_input[...] = units_down(r, l.s)
    for t in range(SEQ):
        r.flipped[:WIDTH, t * TOK : (t + 1) * TOK] = r.mid_rows[t].T
    d_gu = r.d_gu[0:32].reshape(ROW, HIDDEN_TWO)

    @pl.loop(0, 4)
    def _(k):
        rows = pl.ds(pl.multiple_of(k * 256, 256), 256)
        grad = dot(r.flipped[rows, :], d_gu).astype(BF)
        r.gu_all[pl.ds(2 * k, 2)] = grad.reshape(2, 4, 32, HIDDEN_TWO)

    l.greet(r.free, l.column())
    pl.semaphore_wait(r.free, len(l.column()))
    l.start_over()
    gu_sums = [
        Scatter(
            l,
            lambda b, g=g: r.gu_all.at[b, g],
            lambda k, n=n: r.d_gu.at[9 * n + k],
            lambda k, n=n: r.d_gu.at[9 * n + 4 + k],
        )
        for n, g in enumerate(l.others)
    ]
    own_gu_sum = PairScatter(
        l,
        lambda b: r.gu_all.at[b, l.s],
        r.d_gu.at[37],
        lambda k: r.d_gu.at[27 + k],
        lambda k: r.d_gu.at[32 + k],
    )
    gu_sums[1].start()
    own_gu_sum.start()
    own_gu_sum.step(0)
    d_values, ffn_gain_part = norm_back_row(d_mid.total(r.d_input[...]), r.middle[...], r.gain_rows[1:2, :])
    d_middle = r.cot_rows[l.s].astype(F32) + d_values
    r.d_input[...] = d_middle
    d_branch = d_middle.astype(BF)
    r.gains[0, 1:2, :] = ffn_gain_part
    for part in range(SEQ):
        rows = r.out_all[part * 2 : (part + 1) * 2].reshape(OWN_Q, WIDTH)
        r.att_own[part] = dot_nt(d_branch, rows).astype(BF)
    d_att = [l.push(r.att_own.at[o], r.d_att_rows.at[l.s], s=o) for o in l.others]
    r.d_att_rows[l.s] = r.att_own[l.s]
    for part in range(SEQ):
        grad = dot_tn(r.att_local[part], d_branch).astype(BF)
        r.out_all[2 * part : 2 * part + 2] = grad.reshape(2, 4, 32, WIDTH)
    out_row = RowSum(l, r.slots_b)
    out_row.hand_over(r.out_all.at[:, l.s3])
    gu_sums[0].start()
    out_row.cross(r.out_all.at[:, l.s2])
    out_row.near(r.out_all.at[:, l.s1])
    down_b_sum.step(1)
    for copy in d_att:
        copy.wait_recv()
    l.settle((d_mid.first, d_mid.second, d_mid.third))
    gu_sums[2].start()
    attention_block_back(r, 0, 3)
    gu_sums[1].join()
    gu_sums[1].step(0)
    attention_block_back(r, 1, 3)
    attention_block_back(r, 0, 2)
    down_a_sum.join()
    down_a_sum.step(0)
    own_gu_sum.step(1)
    attention_block_back(r, 1, 2)
    down_b_sum.step(2)
    attention_block_back(r, 0, 1)
    attention_block_back(r, 1, 1)
    attention_block_back(r, 0, 0)
    out_total = out_row.total(r.out_all[:, l.s].astype(F32))
    r.out_all[:, l.s] = out_total.astype(BF)
    out_sum = Scatter(
        l, lambda b: r.out_all.at[b, l.s], lambda k: r.out_slots.at[k], lambda k: r.out_slots.at[4 + k]
    )
    attention_block_back(r, 1, 0)
    head_backward(r)
    gu_sums[1].step(1)
    d_u = RowSum(l, r.slots_a)
    weights = r.qkv_all[...].reshape(WIDTH, QKV)

    def d_u_part(t):
        return dot_nt(r.d_qkv[pl.ds(pl.multiple_of(t * TOK, TOK), TOK), :], weights)

    r.parts[0] = d_u_part(l.s3).astype(BF).reshape(8, 32, WIDTH)
    d_u.hand_over(r.parts.at[0])
    r.parts[1] = d_u_part(l.s2).astype(BF).reshape(8, 32, WIDTH)
    d_u.cross(r.parts.at[1])
    r.parts[2] = d_u_part(l.s1).astype(BF).reshape(8, 32, WIDTH)
    d_u.near(r.parts.at[2])
    own = d_u_part(l.s)
    out_sum.start()
    gu_sums[0].join()
    gu_sums[0].step(0)
    gu_sums[2].join()
    gu_sums[2].step(0)
    for t in range(SEQ):
        r.flipped[:WIDTH, t * TOK : (t + 1) * TOK] = r.u_rows[t].T
    grad = dot(r.flipped[:WIDTH, :], r.d_qkv[...]).astype(BF)
    r.qkv_all[...] = grad.reshape(8, 4, 32, QKV)
    qkv_sum = Scatter(l, lambda b: r.qkv_all.at[b], lambda k: r.qkv_slots.at[k], lambda k: r.qkv_slots.at[4 + k])
    qkv_sum.start()
    down_a_sum.step(1)
    own_gu_sum.step(2)
    gu_sums[0].step(1)
    x = r.x_own[...].astype(F32)
    d_values, attn_gain_part = norm_back_row(d_u.total(own), x, r.gain_rows[0:1, :])
    r.d_input[...] += d_values
    kept.append(l.keep(r.d_input, r.input_grad))
    r.gains[0, 0:1, :] = attn_gain_part
    r.gains[0, 2:3, 0:128] = r.head_gain_part[0:1]
    r.gains[0, 2:3, 128:256] = r.head_gain_part[1:2]
    r.gains[0, 2:3, 256:] = jnp.zeros((1, WIDTH - 256), F32)
    r.gains[0, 3:8, :] = jnp.zeros((5, WIDTH), F32)
    gains = [l.push(r.gains.at[0], r.gain_slots.at[k], s=o) for k, o in enumerate(l.others)]
    l.settle((d_u.first, d_u.second, d_u.third))
    down_all = r.down_all[...].reshape(FF_OWN, WIDTH)
    last = RowSum(l, r.slots_b)
    r.parts[0] = dot(r.active[l.s3], down_all).astype(BF).reshape(8, 32, WIDTH)
    last.hand_over(r.parts.at[0])
    r.parts[1] = dot(r.active[l.s2], down_all).astype(BF).reshape(8, 32, WIDTH)
    last.cross(r.parts.at[1])
    own_gu_sum.cross()
    down_b_sum.cross()
    gu_sums[1].step(2)
    qkv_sum.join()
    qkv_sum.step(0)
    gu_sums[0].step(2)
    gu_sums[2].step(1)
    down_a_sum.step(2)
    r.parts[2] = dot(r.active[l.s1], down_all).astype(BF).reshape(8, 32, WIDTH)
    last.near(r.parts.at[2])
    own = r.middle[...] + dot(r.active[l.s], down_all)
    for copy in gains:
        copy.wait_recv()
    r.gains[1] = r.gains[0] + r.gain_slots[0] + r.gain_slots[1] + r.gain_slots[2]
    gains_y = l.push(r.gains.at[1], r.gain_slots.at[3], dp=l.y_peer)
    out_sum.join()
    out_sum.step(0)
    r.gu_all[l.dp, l.s1] = gu_sums[0].total().astype(BF)
    home.append(l.push(r.gu_all.at[l.dp, l.s1], r.gu_grad.at[l.s], s=l.s1))
    r.gu_all[l.dp, l.s2] = gu_sums[1].total().astype(BF)
    home.append(l.push(r.gu_all.at[l.dp, l.s2], r.gu_grad.at[l.s], s=l.s2))
    gu_sums[2].step(2)
    qkv_sum.step(1)
    r.down_own[0:SUM_A] = down_a_sum.total()
    kept.append(l.keep(r.down_own.at[pl.ds(0, SUM_A)], r.down_grad.at[pl.ds(0, SUM_A)]))
    qkv_sum.step(2)
    r.gu_all[l.dp, l.s3] = gu_sums[2].total().astype(BF)
    home.append(l.push(r.gu_all.at[l.dp, l.s3], r.gu_grad.at[l.s], s=l.s3))
    r.output_own[...] = last.total(own).astype(BF)
    kept.append(l.keep(r.output_own, r.output))
    gains_y.wait_recv()
    r.gains[2] = r.gains[1] + r.gain_slots[3]
    gains_z = [l.push(r.gains.at[2], r.gain_slots.at[4 + k], dp=p) for k, p in enumerate(l.z_peers)]
    out_sum.step(1)
    r.gu_all[l.dp, l.s] = own_gu_sum.total().astype(BF)
    kept.append(l.keep(r.gu_all.at[l.dp, l.s], r.gu_grad.at[l.s]))
    r.qkv_all[l.dp] = qkv_sum.total().astype(BF)
    home += [l.push(r.qkv_all.at[l.dp, o], r.qkv_grad.at[l.s], s=o) for o in l.others]
    kept.append(l.keep(r.qkv_all.at[l.dp, l.s], r.qkv_grad.at[l.s]))
    out_sum.step(2)
    r.down_own[SUM_A:] = down_b_sum.total()
    kept.append(l.keep(r.down_own.at[pl.ds(SUM_A, SUM_B)], r.down_grad.at[pl.ds(SUM_A, SUM_B)]))
    r.out_own[...] = out_sum.total()
    kept.append(l.keep(r.out_own, r.out_grad))
    for copy in gains_z + home:
        copy.wait_recv()
    for copy in kept:
        copy.wait()
    r.gain_grads[...] = r.gains[2] + r.gain_slots[4] + r.gain_slots[5] + r.gain_slots[6]
    l.drain()
    l.drain_late()


def own_lanes(row, size):
    place = (lax.axis_index("dp") * SEQ + lax.axis_index("seq")) * size
    return pltpu.roll(row, lax.rem(WIDTH - place, WIDTH), 1)[:, :size]


def lay_out(
    output, input_grad, down_grad, out_grad, gu_grad, qkv_grad, gains,
    output_o, input_o, attn_o, query_o, key_o, value_o, q_gain_o, k_gain_o, out_o, ffn_o, gate_o, up_o, down_o,
):
    for src, dst in ((output, output_o), (input_grad, input_o), (down_grad, down_o), (out_grad, out_o)):
        dst[...] = src[...]
    for o in range(SEQ):
        for ref, first, size in ((query_o, 0, OWN_Q), (key_o, OWN_Q, OWN_K), (value_o, OWN_Q + OWN_K, OWN_K)):
            ref[:, o * size : (o + 1) * size] = qkv_grad[o, :, first : first + size].astype(F32)
    for ref, first in ((gate_o, 0), (up_o, FF_OWN)):
        parts = []
        for j in range(8):
            for o in range(SEQ):
                part = gu_grad[o, :, first + j * FF_SHARD : first + (j + 1) * FF_SHARD]
                parts.append(part.astype(F32))
        ref[...] = jnp.concatenate(parts, axis=1)
    size = attn_o.shape[0]
    attn_o[...] = own_lanes(gains[0:1, :], size).reshape(size)
    ffn_o[...] = own_lanes(gains[1:2, :], size).reshape(size)
    q_gain_o[...] = (gains[2:3, 0:64] + gains[2:3, 64:128]).reshape(HEAD_SIZE)
    k_gain_o[...] = (gains[2:3, 128:192] + gains[2:3, 192:256]).reshape(HEAD_SIZE)


class Names:
    pass


def frequencies():
    steps = np.arange(HEAD_SIZE // 2, dtype=np.float64) * (2.0 / HEAD_SIZE)
    return jnp.asarray(np.tile(THETA ** (-steps), 4)[None], F32)


COLUMN_COPIES = 133
ROW_COPIES = 48
LOCAL_COPIES = 16
VMEM_BYTES = 63 * 2**20


def on_device_in_kernels(
    inputs,
    doc_starts,
    cotangent,
    attn_gain,
    w_query,
    key_projection_weight,
    value_projection_weight,
    q_gain,
    k_gain,
    w_out,
    ffn_gain,
    w_gate,
    w_up,
    w_down,
):
    given = dict(
        inputs=inputs,
        cotangent=cotangent,
        attn_gain=attn_gain,
        ffn_gain=ffn_gain,
        q_gain=q_gain,
        k_gain=k_gain,
        w_query=w_query,
        w_key=key_projection_weight,
        w_value=value_projection_weight,
        w_out=w_out,
        w_gate=w_gate,
        w_up=w_up,
        w_down=w_down,
        frequency=frequencies(),
        doc_starts=doc_starts,
    )
    results = dict(
        output=((TOK, WIDTH), BF),
        input_grad=((TOK, WIDTH), F32),
        down_grad=((FF_SHARD, WIDTH), F32),
        out_grad=((32, WIDTH), F32),
        gu_grad=((SEQ, 32, HIDDEN_TWO), BF),
        qkv_grad=((SEQ, 32, QKV), BF),
        gain_grads=((8, WIDTH), F32),
    )
    kept = dict(
        x_own=((TOK, WIDTH), BF),
        wq=((32, SEQ * OWN_Q), BF),
        wk=((32, SEQ * OWN_K), BF),
        wv=((32, SEQ * OWN_K), BF),
        wg=((32, FF), BF),
        wu=((32, FF), BF),
        output_own=((TOK, WIDTH), BF),
        d_input=((TOK, WIDTH), F32),
        down_own=((FF_SHARD, WIDTH), F32),
        out_own=((32, WIDTH), F32),
        gain_all=((2 * PLANES, SEQ, 16, 128), BF),
        gain_rows=((8, WIDTH), F32),
        w_qkv=((SEQ, 32, QKV), BF),
        cosine=((ROW, 128), F32),
        sine=((ROW, 128), F32),
        u_rows=((SEQ, TOK, WIDTH), BF),
        cot_rows=((SEQ, TOK, WIDTH), BF),
        mid_rows=((SEQ, TOK, WIDTH), BF),
        qkv_all=((8, 4, 32, QKV), BF),
        gu_all=((8, 4, 32, HIDDEN_TWO), BF),
        down_all=((8, FF_SHARD, WIDTH), BF),
        out_all=((8, 4, 32, WIDTH), BF),
        q_linear=((ROW, OWN_Q), F32),
        k_linear=((ROW, OWN_K), F32),
        q_heads=((2, 2, ROW, HEAD_SIZE), BF),
        k_heads=((2, ROW, HEAD_SIZE), BF),
        v_heads=((2, ROW, HEAD_SIZE), BF),
        log_total=((ROW, 128), F32),
        att_own=((SEQ, TOK, OWN_Q), BF),
        att_local=((SEQ, TOK, OWN_Q), BF),
        middle=((TOK, WIDTH), F32),
        active=((SEQ, TOK, FF_OWN), BF),
        d_gu=((38, 32, HIDDEN_TWO), BF),
        parts=((3, 8, 32, WIDTH), BF),
        slots_a=((3, 8, 32, WIDTH), BF),
        slots_b=((3, 8, 32, WIDTH), BF),
        d_att_rows=((SEQ, TOK, OWN_Q), BF),
        flipped=((FF_OWN, ROW), BF),
        down_part=((8, FF_SHARD, WIDTH), BF),
        down_a_slots=((9, SUM_A, WIDTH), BF),
        down_b_slots=((11, SUM_B, WIDTH), BF),
        out_slots=((9, 32, WIDTH), BF),
        qkv_slots=((9, 4, 32, QKV), BF),
        d_query=((ROW, OWN_Q), BF),
        d_kv=((2, ROW, 128), F32),
        d_qkv=((ROW, QKV), BF),
        head_gain_part=((2, 128), F32),
        gains=((3, 8, WIDTH), F32),
        gain_slots=((7, 8, WIDTH), F32),
    )

    def body(*refs):
        r = Names()
        names = [*given, *results, *kept]
        for name, ref in zip(names, refs):
            setattr(r, name, ref)
        r.send_sems, r.recv_sems, r.local_sems, r.free = refs[len(names) :]
        whole_block(r)

    done = pl.pallas_call(
        body,
        out_shape=[jax.ShapeDtypeStruct(*result) for result in results.values()],
        in_specs=[
            pl.BlockSpec(memory_space=pltpu.SMEM if a is doc_starts else pltpu.VMEM if a.size < 1024 else pl.ANY)
            for a in given.values()
        ],
        out_specs=[pl.BlockSpec(memory_space=pl.ANY)] * (len(results) - 1) + [pl.BlockSpec(memory_space=pltpu.VMEM)],
        scratch_shapes=[pltpu.VMEM(*shape) for shape in kept.values()]
        + [
            pltpu.SemaphoreType.DMA((COLUMN_COPIES + ROW_COPIES,)),
            pltpu.SemaphoreType.DMA((COLUMN_COPIES + ROW_COPIES,)),
            pltpu.SemaphoreType.DMA((LOCAL_COPIES,)),
            pltpu.SemaphoreType.REGULAR,
        ],
        compiler_params=pltpu.CompilerParams(
            collective_id=0, has_side_effects=True, vmem_limit_bytes=VMEM_BYTES
        ),
        cost_estimate=pl.CostEstimate(flops=30_000_000_000, bytes_accessed=10_000_000, transcendentals=0),
    )(*given.values())
    rows = w_query.shape[0]
    shapes = [
        ((TOK, WIDTH), BF),
        ((TOK, WIDTH), F32),
        ((rows,), F32),
        ((rows, SEQ * OWN_Q), F32),
        ((rows, SEQ * OWN_K), F32),
        ((rows, SEQ * OWN_K), F32),
        ((HEAD_SIZE,), F32),
        ((HEAD_SIZE,), F32),
        ((rows, WIDTH), F32),
        ((rows,), F32),
        ((rows, FF), F32),
        ((rows, FF), F32),
        ((FF_SHARD, WIDTH), F32),
    ]
    return tuple(
        pl.pallas_call(
            lay_out,
            out_shape=[jax.ShapeDtypeStruct(*shape) for shape in shapes],
            in_specs=[pl.BlockSpec(memory_space=pltpu.VMEM)] * 7,
            out_specs=[pl.BlockSpec(memory_space=pltpu.VMEM)] * 13,
            compiler_params=pltpu.CompilerParams(vmem_limit_bytes=VMEM_BYTES),
            cost_estimate=pl.CostEstimate(flops=1_000_000, bytes_accessed=10_000_000, transcendentals=0),
        )(*done)
    )


def solution(mesh):
    in_kernels = (mesh.shape["dp"], mesh.shape["seq"]) == (8, 4)
    placed = (
        P(("dp", "seq"), None),
        P("dp", None),
        P(("dp", "seq"), None),
        P(("dp", "seq")),
        P(("dp", "seq"), None),
        P(("dp", "seq"), None),
        P(("dp", "seq"), None),
        P(),
        P(),
        P(("dp", "seq"), None),
        P(("dp", "seq")),
        P(("dp", "seq"), None),
        P(("dp", "seq"), None),
        P(("dp", "seq"), None),
    )
    return jax.shard_map(
        on_device_in_kernels if in_kernels else on_device,
        mesh=mesh,
        in_specs=placed,
        out_specs=(
            P(("dp", "seq"), None),
            P(("dp", "seq"), None),
            P(("dp", "seq")),
            P(("dp", "seq"), None),
            P(("dp", "seq"), None),
            P(("dp", "seq"), None),
            P(),
            P(),
            P(("dp", "seq"), None),
            P(("dp", "seq")),
            P(("dp", "seq"), None),
            P(("dp", "seq"), None),
            P(("dp", "seq"), None),
        ),
        check_vma=False,
    )
```
